128 devices in a mesh: group: 4 (over z), table: 32 (over y, x, core).
Axes of the slice: x: 4, y: 4, z: 4, core: 2. Of those that a mesh axis runs over, the one named last changes fastest.
Arguments:
- table: float32 [128, 2048, 128], P('table'), may hold values from -0.36 to 0.36
- accum: float32 [128, 2048], P('table'), may hold values from 0.05 to 2
- w_hidden: bfloat16 [128, 128, 128], replicated, may hold values from -0.5 to 0.5
- w_out: float32 [128], replicated, may hold values from -1.8 to 1.8
- ids: int32 [128, 8, 16384], P('table', None, 'group'), may hold values from 0 to 2047, as said below
- labels: float32 [16384], P(('group', 'table')), may hold values from 0 to 1, as said below
- touched: int32 [128, 512], P('table'), may hold values from 0 to 2047, as said below
- row_noise: float32 [128, 512, 128], P('table'), may hold values from -1.8 to 1.8
- dense_noise: float32 [128, 128, 128], P('table', 'group'), may hold values from -3.6 to 3.6
Outputs:
- new_table: float32 [128, 2048, 128], P('table')
- new_accum: float32 [128, 2048], P('table')
- dense_grad: float32 [128, 128, 128], P('table', 'group')
The draws below stay inside these ranges and needn't reach their ends.
Inputs may be any that keep to these rules, and one draw needn't show every extreme that they name: `touched`: for each feature, 512 different rows of that feature's table. `ids`: every id of feature f is one of the rows listed for f in touched. `labels`: each target is 0 or 1.
All inputs are finite; a program needn't handle non-finite values.
Results may differ from the reference program's by a relative error of at most 0.003.
Values may be sent and summed in bfloat16 or wider, within the bound.
A program may use at most 128 MiB of HBM per device.

```python
import math
import jax
import jax.numpy as jnp
from jax import lax

E = 128
F = 128
H1 = 128
HOTS = 8
ROWS_F = 2048
TOUCH_F = 512
EXAMPLES = 16384


def listed_rows(key):
    keys = jax.random.split(key, F)

    def one_feature(feature_key):
        return jax.random.permutation(feature_key, ROWS_F)[:TOUCH_F]
    return jax.vmap(one_feature)(keys).astype(jnp.int32)


def pick_slots(source, slots):
    return source[slots]


def rising_weights(key, lowest):
    values = jnp.clip(jax.random.normal(key, (F, E, H1), jnp.float32), -6.0, 6.0) * 0.045
    ramp = jnp.arange(F, dtype=jnp.float32) / max(F - 1, 1)
    amplitude = lowest + ramp
    return values * amplitude[:, None, None]


def draw_touched(key, part):
    listed = listed_rows(key)
    return listed


def draw_ids(key, part):
    listed = listed_rows(key)
    key = jax.random.fold_in(key, 5)
    first_key, second_key = jax.random.split(key)
    first = jax.random.randint(first_key, (F, HOTS, EXAMPLES), 0, TOUCH_F)
    second = jax.random.randint(second_key, (F, HOTS, EXAMPLES), 0, TOUCH_F)
    slots = jnp.minimum(first, second)
    return jax.vmap(pick_slots)(listed, slots).astype(jnp.int32)


def draw_w_hidden(key, part):
    key = jax.random.fold_in(key, 11)
    weights = rising_weights(key, 0.5)
    return weights.astype(jnp.bfloat16)


def draw_labels(key, part):
    key = jax.random.fold_in(key, 13)
    return jax.random.bernoulli(key, 0.5, (EXAMPLES,)).astype(jnp.float32)


def shard_levels(own_key, extent, pieces, smallest, largest):
    factor_of, own = 1.0, jax.random.fold_in(own_key, 6)
    for dim, shards_of in pieces:
        heights = jnp.exp(jax.random.uniform(jax.random.fold_in(own, dim), (shards_of,), jnp.float32, smallest / len(pieces), largest / len(pieces)))
        factor_of = factor_of * jnp.repeat(heights, extent[dim] // shards_of).reshape([-1 if axis == dim else 1 for axis in range(len(extent))])
    return factor_of


def gaussian(key, extent, deviation, limit, pieces=(), held_as=jnp.bfloat16):
    array = jax.random.normal(key, extent, jnp.float32) * deviation
    if len(pieces) > 0:
        array = shard_levels(key, extent, pieces, -0.22, 0.18) * array
    return jnp.clip(array, min=-limit, max=limit).astype(held_as)


def setup_inputs(seed: int = 0) -> dict:
    seeds = jax.random.split(jax.random.key(seed), 10)
    table = gaussian(seeds[0], (F, ROWS_F, E), 0.06, 0.36, ((0, 32),), jnp.float32)
    accum = jnp.clip(jnp.exp(math.log(2.0) - 3.6888794 * jax.random.uniform(seeds[1], (F, ROWS_F), jnp.float32) ** shard_levels(seeds[1], (F, ROWS_F), ((0, 32),), -0.2, 0.2)), 0.05, 2.0)
    w_hidden = draw_w_hidden(jax.random.fold_in(seeds[9], 71), 0)
    w_out = gaussian(seeds[3], (H1,), 0.3, 1.8, (), jnp.float32)
    ids = draw_ids(jax.random.fold_in(seeds[9], 71), 0)
    labels = draw_labels(jax.random.fold_in(seeds[9], 71), 0)
    touched = draw_touched(jax.random.fold_in(seeds[9], 71), 0)
    row_noise = gaussian(seeds[7], (F, TOUCH_F, E), 0.3, 1.8, ((0, 32),), jnp.float32)
    dense_noise = gaussian(seeds[8], (F, E, H1), 0.6, 3.6, ((0, 32), (1, 4)), jnp.float32)
    return {"table": table, "accum": accum, "w_hidden": w_hidden, "w_out": w_out, "ids": ids, "labels": labels, "touched": touched, "row_noise": row_noise, "dense_noise": dense_noise}


CLIP = 1.0
LEARN = 0.05

def silu_slope(pre):
    gate = jax.nn.sigmoid(pre)
    return gate * (1.0 + pre * (1.0 - gate))

def pick_rows(source, where):
    return source[where]

def put_rows(target, where, values):
    return target.at[where].set(values)

def add_rows(target, where, values):
    return target.at[where.reshape(-1)].add(values.reshape(-1, values.shape[-1]))

def reference(table, accum, w_hidden, w_out, ids, labels, touched, row_noise, dense_noise):
    block = math.gcd(EXAMPLES, 256)
    block_count = EXAMPLES // block
    table_low = table.astype(jnp.bfloat16).astype(jnp.float32)
    w_flat = w_hidden.reshape(F * E, H1).astype(jnp.float32)

    def one_block(carry, number):
        grads, dense = carry
        start = number * block
        bags = lax.dynamic_slice_in_dim(ids, start, block, 2)
        targets = lax.dynamic_slice_in_dim(labels, start, block, 0)
        looked = jax.vmap(pick_rows)(table_low, bags)
        pooled = jnp.transpose(lax.optimization_barrier(jnp.sum(looked, axis=1)), (1, 0, 2)).astype(jnp.bfloat16)
        flat = pooled.reshape(block, F * E).astype(jnp.float32)
        pre = jnp.dot(flat, w_flat)
        logit = lax.optimization_barrier(jnp.sum(jax.nn.silu(pre) * w_out, axis=1))
        prob = jax.nn.sigmoid(logit)
        delta = silu_slope(pre) * w_out * (prob - targets)[:, None]
        delta_low = delta.astype(jnp.bfloat16).astype(jnp.float32)
        grad_pool = jnp.dot(delta_low, w_flat.T).astype(jnp.bfloat16).reshape(block, F, E)
        repeats = lax.optimization_barrier(jnp.sum((bags[:, :, None, :] == bags[:, None, :, :]).astype(jnp.float32), axis=(1, 2)))
        grad_sq = lax.optimization_barrier(jnp.sum(jnp.square(grad_pool.astype(jnp.float32)), axis=2))
        embed_sq = lax.optimization_barrier(jnp.sum(repeats.T * grad_sq, axis=1))
        dense_sq = lax.optimization_barrier(jnp.sum(flat * flat, axis=1)) * lax.optimization_barrier(jnp.sum(delta * delta, axis=1))
        factor = CLIP / jnp.maximum(jnp.sqrt(embed_sq + dense_sq), CLIP)
        scaled = (factor[:, None, None] * grad_pool.astype(jnp.float32)).astype(jnp.bfloat16)
        clip_rows = (factor[:, None] * delta).astype(jnp.bfloat16)
        spread = jnp.broadcast_to(jnp.transpose(scaled.astype(jnp.float32), (1, 0, 2))[:, None], (F, HOTS, block, E))
        grads = jax.vmap(add_rows)(grads, bags, spread)
        dense = dense + jnp.einsum('bfe,bh->feh', pooled.astype(jnp.float32), clip_rows.astype(jnp.float32))
        return ((grads, dense), None)
    start_carry = (jnp.zeros((F, ROWS_F, E), jnp.float32), jnp.zeros((F, E, H1), jnp.float32))
    (grads, dense), unused = lax.scan(one_block, start_carry, jnp.arange(block_count, dtype=jnp.int32))
    listed = jax.vmap(pick_rows)(grads, touched) + row_noise
    new_acc = jax.vmap(pick_rows)(accum, touched) + lax.optimization_barrier(jnp.mean(listed * listed, axis=2))
    new_rows = jax.vmap(pick_rows)(table, touched) - LEARN * listed / jnp.sqrt(new_acc)[:, :, None]
    new_table = jax.vmap(put_rows)(table, touched, new_rows)
    new_accum = jax.vmap(put_rows)(accum, touched, new_acc)
    return (new_table, new_accum, dense + dense_noise)
```

```python
import functools

import jax
import jax.numpy as jnp
from jax import lax
from jax.experimental import pallas as pl
from jax.experimental.pallas import tpu as pltpu
from jax.sharding import PartitionSpec as P

CLIP = 1.0
LEARN = 0.05
MESH = pl.DeviceIdType.MESH
BF = jnp.bfloat16
F32 = jnp.float32
LAG = 2


def code_of(ids):
    return lax.shift_left((ids & 127) + 128, lax.shift_right_logical(ids, 7)).astype(F32)


def split_dot(a, b, dims):
    return lax.dot_general(a, b, (dims, ((), ())), preferred_element_type=F32)


def core(
    touched_s, accum_s, ids, touched_v, w_out, labels, noise, table_h, w_h,
    rows_out, nacc_out, dense_out,
    table_v, w_v, trows, ttr, tcode, wtr, counts, pool, keep, stage, sibin, outb, slots,
    pacc, clip, accb, s_acc, zsend, zrecv, rg, dsend,
    load_sem, s1, r1, s2, r2, s3, r3, s4, r4, s5, r5, s6, r6, s7, r7,
):
    g = lax.axis_index("group")
    t = lax.axis_index("table")
    c = lax.rem(t, 2)
    p = t // 2
    y = p // 4
    x = lax.rem(p, 4)
    sib = t + 1 - 2 * c

    def ahead(off):
        return lax.rem(y + off // 4, 4) * 4 + lax.rem(x + lax.rem(off, 4), 4)

    def behind(off):
        return lax.rem(y + 4 - off // 4, 4) * 4 + lax.rem(x + 4 - lax.rem(off, 4), 4)

    load_table = pltpu.make_async_copy(table_h, table_v, load_sem.at[0])
    load_w = pltpu.make_async_copy(w_h, w_v, load_sem.at[1])
    load_table.start()
    load_w.start()

    barrier = pltpu.get_barrier_semaphore()

    def greet(off, carry):
        pl.semaphore_signal(
            barrier, inc=1, device_id=(g, ahead(off) * 2 + c), device_id_type=MESH
        )
        return carry

    lax.fori_loop(1, 16, greet, 0)
    pl.semaphore_signal(barrier, inc=1, device_id=(g, sib), device_id_type=MESH)
    for i in range(1, 4):
        pl.semaphore_signal(
            barrier, inc=1, device_id=(lax.rem(g + i, 4), t), device_id_type=MESH
        )

    for f in range(4):
        row = code_of(touched_v[f : f + 1, :])
        for q in range(4):
            wide = jnp.broadcast_to(row[:, q * 128 : (q + 1) * 128], (128, 128))
            tcode[f, q * 128 : (q + 1) * 128, :] = wide.T.astype(BF)

    load_table.wait()

    def pick(n, carry):
        f = n // 64
        k = lax.rem(n, 64) * 8
        for i in range(8):
            r = touched_s[f, k + i]
            trows[f, pl.ds(k + i, 1), :] = table_v[f, pl.ds(r, 1), :]
        return carry

    lax.fori_loop(0, 256, pick, 0)
    for f in range(4):
        ttr[f] = trows[f].T.astype(BF)

    load_w.wait()
    for f in range(4):
        wtr[:, f * 128 : (f + 1) * 128] = w_v[t * 4 + f].astype(F32).T.astype(BF)

    pl.semaphore_wait(barrier, 19)

    rows16 = lax.broadcasted_iota(jnp.int32, (16, 256), 0)

    def relay(s):
        pltpu.make_async_remote_copy(
            src_ref=stage.at[s], dst_ref=sibin.at[s], send_sem=s1.at[s], recv_sem=r1.at[s],
            device_id=(g, sib), device_id_type=MESH,
        ).wait_recv()
        outb[s] = (keep[s] + sibin[s].astype(F32)).astype(BF)

    def out_copy(s):
        return pltpu.make_async_remote_copy(
            src_ref=outb.at[s], dst_ref=slots.at[p], send_sem=s2.at[s], recv_sem=r2.at[p],
            device_id=(g, ahead(15 - s) * 2 + c), device_id_type=MESH,
        )

    def sib_copy(s):
        return pltpu.make_async_remote_copy(
            src_ref=stage.at[s], dst_ref=sibin.at[s], send_sem=s1.at[s], recv_sem=r1.at[s],
            device_id=(g, sib), device_id_type=MESH,
        )

    def step(s, carry):
        b0 = pl.multiple_of(ahead(15 - s) * 256, 256)

        def feature(f, carry):
            extra, sumsq = carry
            bag = ids[f, :, pl.ds(b0, 256)]
            code = code_of(bag)
            mult = jnp.ones((8, 256), F32)
            for d in range(1, 8):
                mult = mult + jnp.where(bag == pltpu.roll(bag, d, 0), 1.0, 0.0)
            repeats = jnp.sum(mult, axis=0, keepdims=True)
            extra = jnp.where(rows16 == c * 4 + f, repeats, extra)
            codes = []
            mults = []
            for half in range(2):
                lanes = slice(half * 128, half * 128 + 128)
                codes.append(
                    [jnp.broadcast_to(code[h : h + 1, lanes], (16, 128)).astype(BF) for h in range(8)]
                )
                mults.append(
                    [jnp.broadcast_to(mult[h : h + 1, lanes], (16, 128)).astype(BF) for h in range(8)]
                )
            total = jnp.zeros((128, 256), F32)
            zero = jnp.zeros((16, 128), BF)
            for part in range(2):
                tiles = []
                for kt in range(16):
                    k0 = part * 256 + kt * 16
                    want = tcode[f, k0 : k0 + 16, :]
                    both = []
                    for half in range(2):
                        count = zero
                        for h in range(8):
                            count = jnp.where(want == codes[half][h], mults[half][h], count)
                        both.append(count)
                    tiles.append(jnp.concatenate(both, axis=1))
                block = jnp.concatenate(tiles, axis=0)
                counts[f, part * 256 : part * 256 + 256, pl.ds(b0, 256)] = block
                total = total + split_dot(
                    ttr[f, :, part * 256 : part * 256 + 256], block, ((1,), (0,))
                )
            low = total.astype(BF)
            pool[pl.ds(pl.multiple_of(f * 128, 128), 128), :] = low
            wide = low.astype(F32)
            sumsq = sumsq + jnp.sum(wide * wide, axis=0, keepdims=True)
            return extra, sumsq

        extra, sumsq = lax.fori_loop(
            0, 4, feature, (jnp.zeros((16, 256), F32), jnp.zeros((1, 256), F32))
        )
        high = sumsq.astype(BF).astype(F32)
        extra = jnp.where(rows16 == 8 + 2 * c, high, extra)
        extra = jnp.where(rows16 == 9 + 2 * c, sumsq - high, extra)
        part = split_dot(wtr[...], pool[...], ((1,), (0,)))
        first = c == 0
        keep[s, 0:128, :] = jnp.where(first, part[:, :128], part[:, 128:])
        keep[s, 128:144, :] = jnp.where(first, extra[:, :128], extra[:, 128:])
        stage[s, 0:128, :] = jnp.where(first, part[:, 128:], part[:, :128]).astype(BF)
        stage[s, 128:144, :] = jnp.where(first, extra[:, 128:], extra[:, :128]).astype(BF)
        sib_copy(s).start()

        @pl.when(s >= LAG)
        def _():
            relay(s - LAG)
            out_copy(s - LAG).start()

        return carry

    lax.fori_loop(0, 16, step, 0)
    relay(14)
    out_copy(14).start()
    relay(15)
    slots[p] = outb[15]

    pacc[...] = slots[p, 0:128, :].astype(F32)

    def arrive(s, carry):
        src = behind(15 - s)
        pltpu.make_async_remote_copy(
            src_ref=outb.at[s], dst_ref=slots.at[src], send_sem=s2.at[s], recv_sem=r2.at[src],
            device_id=(g, ahead(15 - s) * 2 + c), device_id_type=MESH,
        ).wait_recv()
        pacc[...] += slots[src, 0:128, :].astype(F32)
        return carry

    lax.fori_loop(0, 15, arrive, 0)
    pre = pacc[...]
    weight = jnp.broadcast_to(w_out[...], (128, 128)).T
    gate = jax.nn.sigmoid(pre)
    logit = jnp.sum(pre * gate * weight, axis=0, keepdims=True)
    prob = jax.nn.sigmoid(logit)
    delta = gate * (1.0 + pre * (1.0 - gate)) * weight * (prob - labels[...])
    delta_low = delta.astype(BF)

    def norms(q, carry):
        acc, ssq = carry
        grad = split_dot(
            w_v[pl.ds(q * 8, 8)].reshape(1024, 128), delta_low, ((1,), (0,))
        )
        square = jnp.sum((grad * grad).reshape(8, 128, 128), axis=1)
        tail = slots[q, 128:144, :].astype(F32)
        return acc + square * tail[0:8], ssq + tail[8:16]

    acc, ssq = lax.fori_loop(
        0, 16, norms, (jnp.zeros((8, 128), F32), jnp.zeros((8, 128), F32))
    )
    norm_sq = jnp.sum(acc, axis=0, keepdims=True) + jnp.sum(
        ssq, axis=0, keepdims=True
    ) * jnp.sum(delta * delta, axis=0, keepdims=True)
    factor = CLIP / jnp.maximum(jnp.sqrt(norm_sq), CLIP)
    clip[t] = (factor * delta).T.astype(BF)

    def clip_copy(off):
        return pltpu.make_async_remote_copy(
            src_ref=clip.at[t], dst_ref=clip.at[t], send_sem=s3.at[off], recv_sem=r3.at[p],
            device_id=(g, ahead(off) * 2 + c), device_id_type=MESH,
        )

    def clip_arrival(off):
        src = behind(off)
        return pltpu.make_async_remote_copy(
            src_ref=clip.at[t], dst_ref=clip.at[src * 2 + c], send_sem=s3.at[off],
            recv_sem=r3.at[src], device_id=(g, ahead(off) * 2 + c), device_id_type=MESH,
        )

    def pass_on(off):
        src = behind(off)
        return pltpu.make_async_remote_copy(
            src_ref=clip.at[src * 2 + c], dst_ref=clip.at[src * 2 + c], send_sem=s4.at[off],
            recv_sem=r4.at[src], device_id=(g, sib), device_id_type=MESH,
        )

    def passed(off):
        src = behind(off)
        return pltpu.make_async_remote_copy(
            src_ref=clip.at[src * 2 + c], dst_ref=clip.at[src * 2 + 1 - c], send_sem=s4.at[off],
            recv_sem=r4.at[src], device_id=(g, sib), device_id_type=MESH,
        )

    def spread(off, carry):
        clip_copy(off).start()
        return carry

    pass_on(0).start()
    lax.fori_loop(1, 16, spread, 0)

    def pick_acc(n, carry):
        f = n // 64
        k = lax.rem(n, 64) * 8
        for i in range(8):
            value = accum_s[f, touched_s[f, k + i]]
            accb[f, pl.ds(k + i, 1), :] = jnp.full((1, 128), value, F32)
        return carry

    lax.fori_loop(0, 256, pick_acc, 0)

    for dy in range(4):
        for dx in range(4):
            off = dy * 4 + dx
            if off > 0:
                clip_arrival(off).wait_recv()
                pass_on(off).start()
        for dx in range(4):
            passed(dy * 4 + dx).wait_recv()
        row = lax.rem(y + 4 - dy, 4)
        b0 = pl.multiple_of(row * 1024, 1024)
        block = clip[pl.ds(row * 8, 8)].reshape(1024, 128)

        def add(i, carry):
            f = lax.rem(g + 1 + i, 4)
            part = split_dot(counts[f, :, pl.ds(b0, 1024)], block, ((1,), (0,)))
            if dy == 0:
                s_acc[f] = part
            elif dy < 3:
                s_acc[f] += part
            else:
                part = part + s_acc[f]
                s_acc[f] = part

                @pl.when(i < 3)
                def _():
                    zsend[i] = part.astype(BF)
                    pltpu.make_async_remote_copy(
                        src_ref=zsend.at[i], dst_ref=zrecv.at[g], send_sem=s5.at[i],
                        recv_sem=r5.at[g], device_id=(f, t), device_id_type=MESH,
                    ).start()

            return carry

        lax.fori_loop(0, 4, add, 0)

    summed = s_acc[g]
    for i in range(3):
        src = lax.rem(g + 3 - i, 4)
        pltpu.make_async_remote_copy(
            src_ref=zsend.at[i], dst_ref=zrecv.at[src], send_sem=s5.at[i], recv_sem=r5.at[src],
            device_id=(lax.rem(g + 1 + i, 4), t), device_id_type=MESH,
        ).wait_recv()
        summed = summed + zrecv[src].astype(F32)
    low = summed.astype(BF)
    rg[g] = split_dot(low, w_v[t * 4 + g], ((1,), (1,))).astype(BF)

    def row_copy(i):
        return pltpu.make_async_remote_copy(
            src_ref=rg.at[g], dst_ref=rg.at[g], send_sem=s6.at[i], recv_sem=r6.at[g],
            device_id=(lax.rem(g + 1 + i, 4), t), device_id_type=MESH,
        )

    def dense_copy(i):
        to = lax.rem(g + 1 + i, 4)
        return pltpu.make_async_remote_copy(
            src_ref=dsend.at[to], dst_ref=dense_out.at[g], send_sem=s7.at[i], recv_sem=r7.at[g],
            device_id=(to, t), device_id_type=MESH,
        )

    for i in range(3):
        row_copy(i).start()
    dsend[...] = split_dot(ttr[g], low, ((1,), (0,))).reshape(4, 32, 128)
    for i in range(3):
        dense_copy(i).start()
    dense_out[g] = dsend[g]

    diagonal = lax.broadcasted_iota(jnp.int32, (128, 128), 0) == lax.broadcasted_iota(
        jnp.int32, (128, 128), 1
    )

    def update(f):
        listed = rg[f].astype(F32) + noise[f]
        new_acc = accb[f] + jnp.sum(listed * listed, axis=1, keepdims=True) * (1.0 / 128.0)
        rows_out[f] = trows[f] - LEARN * listed / jnp.sqrt(new_acc)
        for q in range(4):
            tile = jnp.where(diagonal, new_acc[q * 128 : (q + 1) * 128, :], 0.0)
            nacc_out[f, q : q + 1, :] = jnp.sum(tile, axis=0, keepdims=True)

    update(g)
    for i in range(3):
        src = lax.rem(g + 3 - i, 4)
        pltpu.make_async_remote_copy(
            src_ref=rg.at[g], dst_ref=rg.at[src], send_sem=s6.at[i], recv_sem=r6.at[src],
            device_id=(lax.rem(g + 1 + i, 4), t), device_id_type=MESH,
        ).wait_recv()
        update(src)
    for i in range(3):
        src = lax.rem(g + 3 - i, 4)
        pltpu.make_async_remote_copy(
            src_ref=dsend.at[0], dst_ref=dense_out.at[src], send_sem=s7.at[i],
            recv_sem=r7.at[src], device_id=(lax.rem(g + 1 + i, 4), t), device_id_type=MESH,
        ).wait_recv()

    def drain(s, carry):
        sib_copy(s).wait_send()
        pass_on(s).wait_send()
        return carry

    def drain_far(s, carry):
        out_copy(s).wait_send()
        clip_copy(s + 1).wait_send()
        return carry

    lax.fori_loop(0, 16, drain, 0)
    lax.fori_loop(0, 15, drain_far, 0)
    for i in range(3):
        pltpu.make_async_remote_copy(
            src_ref=zsend.at[i], dst_ref=zrecv.at[g], send_sem=s5.at[i], recv_sem=r5.at[g],
            device_id=(lax.rem(g + 1 + i, 4), t), device_id_type=MESH,
        ).wait_send()
        row_copy(i).wait_send()
        dense_copy(i).wait_send()


def write_rows(touched_s, nacc_s, accum_h, table, rows, out, accum_out, acc_s, sem):
    f = pl.program_id(0)

    @pl.when(f == 0)
    def _():
        copy = pltpu.make_async_copy(accum_h, acc_s, sem)
        copy.start()
        copy.wait()

    out[...] = table[...]

    def put(n, carry):
        for i in range(8):
            k = n * 8 + i
            r = touched_s[f, k]
            out[0, pl.ds(r, 1), :] = rows[0, pl.ds(k, 1), :]
            acc_s[f, r] = nacc_s[f, k]
        return carry

    lax.fori_loop(0, 64, put, 0)

    @pl.when(f == 3)
    def _():
        copy = pltpu.make_async_copy(acc_s, accum_out, sem)
        copy.start()
        copy.wait()


def body(table, accum, w_hidden, w_out, ids, labels, touched, row_noise, dense_noise):
    vmem = pl.BlockSpec(memory_space=pltpu.VMEM)
    smem = pl.BlockSpec(memory_space=pltpu.SMEM)
    hbm = pl.BlockSpec(memory_space=pl.ANY)
    dma = pltpu.SemaphoreType.DMA
    rows, nacc, dense = pl.pallas_call(
        core,
        out_shape=(
            jax.ShapeDtypeStruct((4, 512, 128), F32),
            jax.ShapeDtypeStruct((4, 4, 128), F32),
            jax.ShapeDtypeStruct((4, 32, 128), F32),
        ),
        in_specs=[smem, smem, vmem, vmem, vmem, vmem, vmem, hbm, hbm],
        out_specs=(vmem, vmem, vmem),
        scratch_shapes=[
            pltpu.VMEM((4, 2048, 128), F32),
            pltpu.VMEM((128, 128, 128), BF),
            pltpu.VMEM((4, 512, 128), F32),
            pltpu.VMEM((4, 128, 512), BF),
            pltpu.VMEM((4, 512, 128), BF),
            pltpu.VMEM((128, 512), BF),
            pltpu.VMEM((4, 512, 4096), BF),
            pltpu.VMEM((512, 256), BF),
            pltpu.VMEM((16, 144, 128), F32),
            pltpu.VMEM((16, 144, 128), BF),
            pltpu.VMEM((16, 144, 128), BF),
            pltpu.VMEM((16, 144, 128), BF),
            pltpu.VMEM((16, 144, 128), BF),
            pltpu.VMEM((128, 128), F32),
            pltpu.VMEM((32, 128, 128), BF),
            pltpu.VMEM((4, 512, 128), F32),
            pltpu.VMEM((4, 512, 128), F32),
            pltpu.VMEM((3, 512, 128), BF),
            pltpu.VMEM((4, 512, 128), BF),
            pltpu.VMEM((4, 512, 128), BF),
            pltpu.VMEM((4, 32, 128), F32),
            dma((2,)),
            dma((16,)), dma((16,)), dma((16,)), dma((16,)),
            dma((16,)), dma((16,)), dma((16,)), dma((16,)),
            dma((3,)), dma((4,)), dma((3,)), dma((4,)), dma((3,)), dma((4,)),
        ],
        compiler_params=pltpu.CompilerParams(
            collective_id=0, has_side_effects=True, vmem_limit_bytes=56 * 1024 * 1024
        ),
        cost_estimate=pl.CostEstimate(
            flops=6 * 10**9, bytes_accessed=12 * 2**20, transcendentals=10**5
        ),
        name="step",
    )(
        touched, accum, ids, touched, w_out.reshape(1, 128), labels.reshape(1, 128),
        row_noise, table, w_hidden,
    )
    new_table, new_accum = pl.pallas_call(
        write_rows,
        grid=(4,),
        out_shape=(
            jax.ShapeDtypeStruct((4, 2048, 128), F32),
            jax.ShapeDtypeStruct((4, 2048), F32),
        ),
        in_specs=[
            smem, smem, hbm,
            pl.BlockSpec((1, 2048, 128), lambda f: (f, 0, 0)),
            pl.BlockSpec((1, 512, 128), lambda f: (f, 0, 0)),
        ],
        out_specs=(pl.BlockSpec((1, 2048, 128), lambda f: (f, 0, 0)), hbm),
        scratch_shapes=[pltpu.SMEM((4, 2048), F32), dma(())],
        compiler_params=pltpu.CompilerParams(vmem_limit_bytes=16 * 1024 * 1024),
        name="write_rows",
    )(touched, nacc.reshape(4, 512), accum, table, rows)
    return (new_table, new_accum, dense + dense_noise)


def solution(mesh):
    in_specs = (
        P("table", None, None),
        P("table", None),
        P(),
        P(),
        P("table", None, "group"),
        P(("group", "table")),
        P("table", None),
        P("table", None, None),
        P("table", "group", None),
    )
    out_specs = (P("table", None, None), P("table", None), P("table", "group", None))
    return jax.shard_map(body, mesh=mesh, in_specs=in_specs, out_specs=out_specs, check_vma=False)
```

```python
import functools

import jax
import jax.numpy as jnp
from jax import lax
from jax.experimental import pallas as pl
from jax.experimental.pallas import tpu as pltpu
from jax.sharding import PartitionSpec as P

CLIP = 1.0
LEARN = 0.05
MESH = pl.DeviceIdType.MESH
BF = jnp.bfloat16
F32 = jnp.float32
LAG = 2


def split_dot(a, b, dims):
    return lax.dot_general(a, b, (dims, ((), ())), preferred_element_type=F32)


def core(
    touched_s, accum, ids, touched_v, w_out, labels, noise, table_h, w_h,
    rows_out, macc_out, dense_out,
    table_v, w_v, trows, ttr, smap, low_col, wtr, counts, pool, keep, stage, sibin, outb, slots,
    pacc, clip, accb, s_acc, zsend, zrecv, rg, dsend,
    load_sem, s1, r1, s2, r2, s3, r3, s4, r4, s5, r5, s6, r6, s7, r7,
):
    g = lax.axis_index("group")
    t = lax.axis_index("table")
    c = lax.rem(t, 2)
    p = t // 2
    y = p // 4
    x = lax.rem(p, 4)
    sib = t + 1 - 2 * c

    def ahead(off):
        return lax.rem(y + off // 4, 4) * 4 + lax.rem(x + lax.rem(off, 4), 4)

    def behind(off):
        return lax.rem(y + 4 - off // 4, 4) * 4 + lax.rem(x + 4 - lax.rem(off, 4), 4)

    load_table = pltpu.make_async_copy(table_h, table_v, load_sem.at[0])
    load_w = pltpu.make_async_copy(w_h, w_v, load_sem.at[1])
    load_table.start()
    load_w.start()

    barrier = pltpu.get_barrier_semaphore()

    def greet(off, carry):
        pl.semaphore_signal(
            barrier, inc=1, device_id=(g, ahead(off) * 2 + c), device_id_type=MESH
        )
        return carry

    lax.fori_loop(1, 16, greet, 0)
    pl.semaphore_signal(barrier, inc=1, device_id=(g, sib), device_id_type=MESH)
    for i in range(1, 4):
        pl.semaphore_signal(
            barrier, inc=1, device_id=(lax.rem(g + i, 4), t), device_id_type=MESH
        )

    high_of = lax.broadcasted_iota(jnp.int32, (16, 512), 0)
    low_of = lax.broadcasted_iota(jnp.int32, (128, 512), 0)
    lane = lax.broadcasted_iota(jnp.int32, (1, 512), 1)
    for f in range(4):
        row = touched_v[f : f + 1, :]
        row_low = row & 127
        is_high = high_of == lax.shift_right_logical(row, 7)
        is_low = jnp.where(low_of == row_low, 1.0, 0.0).astype(BF)
        number = jnp.concatenate(
            [
                jnp.where(is_high, lax.shift_right_logical(lane, 4), 0),
                jnp.where(is_high, lane & 15, 0),
            ],
            axis=0,
        )
        pair = split_dot(number.astype(F32).astype(BF), is_low, ((1,), (1,)))
        smap[f] = (pair[:16] * 16.0 + pair[16:]).astype(jnp.int32)
        for q in range(4):
            wide = jnp.broadcast_to(row_low[:, q * 128 : (q + 1) * 128], (128, 128))
            low_col[f, q * 128 : (q + 1) * 128, :] = wide.T

    load_table.wait()

    def pick(n, carry):
        f = n // 16
        k = lax.rem(n, 16) * 32
        for i in range(32):
            r = touched_s[f, k + i]
            trows[f, pl.ds(k + i, 1), :] = table_v[f, pl.ds(r, 1), :]
        return carry

    lax.fori_loop(0, 64, pick, 0)
    for f in range(4):
        ttr[f] = trows[f].T.astype(BF)

    load_w.wait()
    for f in range(4):
        wtr[:, f * 128 : (f + 1) * 128] = w_v[t * 4 + f].astype(F32).T.astype(BF)

    pl.semaphore_wait(barrier, 19)

    words = lax.broadcasted_iota(jnp.int32, (64, 128), 0)
    rows16 = lax.broadcasted_iota(jnp.int32, (16, 256), 0)

    def relay(s):
        pltpu.make_async_remote_copy(
            src_ref=stage.at[s], dst_ref=sibin.at[s], send_sem=s1.at[s], recv_sem=r1.at[s],
            device_id=(g, sib), device_id_type=MESH,
        ).wait_recv()
        outb[s] = (keep[s] + sibin[s].astype(F32)).astype(BF)

    def out_copy(s):
        return pltpu.make_async_remote_copy(
            src_ref=outb.at[s], dst_ref=slots.at[p], send_sem=s2.at[s], recv_sem=r2.at[p],
            device_id=(g, ahead(15 - s) * 2 + c), device_id_type=MESH,
        )

    def sib_copy(s):
        return pltpu.make_async_remote_copy(
            src_ref=stage.at[s], dst_ref=sibin.at[s], send_sem=s1.at[s], recv_sem=r1.at[s],
            device_id=(g, sib), device_id_type=MESH,
        )

    def step(s, carry):
        b0 = pl.multiple_of(ahead(15 - s) * 256, 256)

        extra = jnp.zeros((16, 256), F32)
        sumsq = jnp.zeros((1, 256), F32)
        for f in range(4):
            bag = ids[f, :, pl.ds(b0, 256)]
            mult = jnp.ones((8, 256), F32)
            for d in range(1, 8):
                mult = mult + jnp.where(bag == pltpu.roll(bag, d, 0), 1.0, 0.0)
            repeats = jnp.sum(mult, axis=0, keepdims=True)
            extra = jnp.where(rows16 == c * 4 + f, repeats, extra)
            halves = []
            for half in range(2):
                part = bag[:, half * 128 : half * 128 + 128]
                high = lax.shift_right_logical(part, 7)
                low = part & 127
                slot = jnp.zeros((8, 128), jnp.int32)
                for q in range(16):
                    row = jnp.broadcast_to(smap[f, q : q + 1, :], (8, 128))
                    slot = jnp.where(high == q, jnp.take_along_axis(row, low, axis=1), slot)
                word = slot & 63
                digit = lax.shift_left(
                    jnp.ones((8, 128), jnp.int32), lax.shift_right_logical(slot, 6) * 4
                )
                packed = jnp.zeros((64, 128), jnp.int32)
                for h in range(8):
                    packed = packed + jnp.where(words == word[h : h + 1], digit[h : h + 1], 0)
                tiles = []
                for i in range(8):
                    one = lax.shift_right_logical(packed, 4 * i) if i else packed
                    tiles.append((one & 15).astype(F32).astype(BF))
                halves.append(jnp.concatenate(tiles, axis=0))
            block = jnp.concatenate(halves, axis=1)
            counts[f, :, pl.ds(b0, 256)] = block
            pooled = split_dot(ttr[f], block, ((1,), (0,))).astype(BF)
            pool[f * 128 : f * 128 + 128, :] = pooled
            wide = pooled.astype(F32)
            sumsq = sumsq + jnp.sum(wide * wide, axis=0, keepdims=True)

        high = sumsq.astype(BF).astype(F32)
        extra = jnp.where(rows16 == 8 + 2 * c, high, extra)
        extra = jnp.where(rows16 == 9 + 2 * c, sumsq - high, extra)
        part = split_dot(wtr[...], pool[...], ((1,), (0,)))
        first = c == 0
        keep[s, 0:128, :] = jnp.where(first, part[:, :128], part[:, 128:])
        keep[s, 128:144, :] = jnp.where(first, extra[:, :128], extra[:, 128:])
        stage[s, 0:128, :] = jnp.where(first, part[:, 128:], part[:, :128]).astype(BF)
        stage[s, 128:144, :] = jnp.where(first, extra[:, 128:], extra[:, :128]).astype(BF)
        sib_copy(s).start()

        @pl.when(s >= LAG)
        def _():
            relay(s - LAG)
            out_copy(s - LAG).start()

        return carry

    lax.fori_loop(0, 16, step, 0)
    relay(14)
    out_copy(14).start()
    relay(15)
    slots[p] = outb[15]

    pacc[...] = slots[p, 0:128, :].astype(F32)

    def arrive(s, carry):
        src = behind(15 - s)
        pltpu.make_async_remote_copy(
            src_ref=outb.at[s], dst_ref=slots.at[src], send_sem=s2.at[s], recv_sem=r2.at[src],
            device_id=(g, ahead(15 - s) * 2 + c), device_id_type=MESH,
        ).wait_recv()
        pacc[...] += slots[src, 0:128, :].astype(F32)
        return carry

    lax.fori_loop(0, 15, arrive, 0)
    pre = pacc[...]
    weight = jnp.broadcast_to(w_out[...], (128, 128)).T
    gate = jax.nn.sigmoid(pre)
    logit = jnp.sum(pre * gate * weight, axis=0, keepdims=True)
    prob = jax.nn.sigmoid(logit)
    delta = gate * (1.0 + pre * (1.0 - gate)) * weight * (prob - labels[...])
    delta_low = delta.astype(BF)

    nothing = jnp.zeros((128, 128), BF)
    twice = jnp.concatenate(
        [
            jnp.concatenate([delta_low, nothing], axis=1),
            jnp.concatenate([nothing, delta_low], axis=1),
        ],
        axis=0,
    )

    def norms(q, carry):
        acc, ssq = carry
        weights = w_v[pl.ds(q * 32, 32)]
        side = jnp.concatenate(
            [weights[:16].reshape(2048, 128), weights[16:].reshape(2048, 128)], axis=1
        )
        grad = split_dot(side, twice, ((1,), (0,)))
        square = jnp.sum((grad * grad).reshape(16, 128, 256), axis=1)
        for i in range(4):
            tail = slots[q * 4 + i, 128:144, :].astype(F32)
            half = square[:, :128] if i < 2 else square[:, 128:]
            acc = acc + half[(i % 2) * 8 : (i % 2) * 8 + 8] * tail[0:8]
            ssq = ssq + tail[8:16]
        return acc, ssq

    acc, ssq = lax.fori_loop(
        0, 4, norms, (jnp.zeros((8, 128), F32), jnp.zeros((8, 128), F32))
    )
    norm_sq = jnp.sum(acc, axis=0, keepdims=True) + jnp.sum(
        ssq, axis=0, keepdims=True
    ) * jnp.sum(delta * delta, axis=0, keepdims=True)
    factor = CLIP / jnp.maximum(jnp.sqrt(norm_sq), CLIP)
    clip[t] = (factor * delta).T.astype(BF)

    def high_one(f):
        row = lax.shift_right_logical(touched_v[pl.ds(f, 1), :], 7)
        return jnp.where(high_of == row, 1.0, 0.0).astype(BF)

    def three(values):
        first = values.astype(BF)
        rest = values - first.astype(F32)
        second = rest.astype(BF)
        return first, second, (rest - second.astype(F32)).astype(BF)

    def clip_copy(off):
        return pltpu.make_async_remote_copy(
            src_ref=clip.at[t], dst_ref=clip.at[t], send_sem=s3.at[off], recv_sem=r3.at[p],
            device_id=(g, ahead(off) * 2 + c), device_id_type=MESH,
        )

    def clip_arrival(off):
        src = behind(off)
        return pltpu.make_async_remote_copy(
            src_ref=clip.at[t], dst_ref=clip.at[src * 2 + c], send_sem=s3.at[off],
            recv_sem=r3.at[src], device_id=(g, ahead(off) * 2 + c), device_id_type=MESH,
        )

    def pass_on(off):
        src = behind(off)
        return pltpu.make_async_remote_copy(
            src_ref=clip.at[src * 2 + c], dst_ref=clip.at[src * 2 + c], send_sem=s4.at[off],
            recv_sem=r4.at[src], device_id=(g, sib), device_id_type=MESH,
        )

    def passed(off):
        src = behind(off)
        return pltpu.make_async_remote_copy(
            src_ref=clip.at[src * 2 + c], dst_ref=clip.at[src * 2 + 1 - c], send_sem=s4.at[off],
            recv_sem=r4.at[src], device_id=(g, sib), device_id_type=MESH,
        )

    def spread(off, carry):
        clip_copy(off).start()
        return carry

    pass_on(0).start()
    lax.fori_loop(1, 16, spread, 0)

    lanes = lax.broadcasted_iota(jnp.int32, (512, 128), 1)
    for f in range(4):
        is_high = high_one(f)
        values = jnp.concatenate(
            [accum[f : f + 1, q * 128 : (q + 1) * 128] for q in range(16)], axis=0
        )
        first, second, third = three(values)
        spread_out = split_dot(
            jnp.concatenate([is_high, is_high, is_high], axis=0),
            jnp.concatenate([first, second, third], axis=0),
            ((0,), (0,)),
        )
        found = jnp.where(lanes == low_col[f], spread_out, 0.0)
        accb[f] = jnp.broadcast_to(jnp.sum(found, axis=1, keepdims=True), (512, 128))

    for dy in range(4):
        for dx in range(4):
            off = dy * 4 + dx
            if off > 0:
                clip_arrival(off).wait_recv()
                pass_on(off).start()
        for dx in range(4):
            passed(dy * 4 + dx).wait_recv()
        row = lax.rem(y + 4 - dy, 4)
        b0 = pl.multiple_of(row * 1024, 1024)
        block = clip[pl.ds(row * 8, 8)].reshape(1024, 128)

        def add(i, carry):
            f = lax.rem(g + 1 + i, 4)
            part = split_dot(counts[f, :, pl.ds(b0, 1024)], block, ((1,), (0,)))
            if dy == 0:
                s_acc[f] = part
            elif dy < 3:
                s_acc[f] += part
            else:
                part = part + s_acc[f]
                s_acc[f] = part

                @pl.when(i < 3)
                def _():
                    zsend[i] = part.astype(BF)
                    pltpu.make_async_remote_copy(
                        src_ref=zsend.at[i], dst_ref=zrecv.at[g], send_sem=s5.at[i],
                        recv_sem=r5.at[g], device_id=(f, t), device_id_type=MESH,
                    ).start()

            return carry

        lax.fori_loop(0, 4, add, 0)

    summed = s_acc[g]
    for i in range(3):
        src = lax.rem(g + 3 - i, 4)
        pltpu.make_async_remote_copy(
            src_ref=zsend.at[i], dst_ref=zrecv.at[src], send_sem=s5.at[i], recv_sem=r5.at[src],
            device_id=(lax.rem(g + 1 + i, 4), t), device_id_type=MESH,
        ).wait_recv()
        summed = summed + zrecv[src].astype(F32)
    low = summed.astype(BF)
    rg[g] = split_dot(low, w_v[t * 4 + g], ((1,), (1,))).astype(BF)

    def row_copy(i):
        return pltpu.make_async_remote_copy(
            src_ref=rg.at[g], dst_ref=rg.at[g], send_sem=s6.at[i], recv_sem=r6.at[g],
            device_id=(lax.rem(g + 1 + i, 4), t), device_id_type=MESH,
        )

    def dense_copy(i):
        to = lax.rem(g + 1 + i, 4)
        return pltpu.make_async_remote_copy(
            src_ref=dsend.at[to], dst_ref=dense_out.at[g], send_sem=s7.at[i], recv_sem=r7.at[g],
            device_id=(to, t), device_id_type=MESH,
        )

    for i in range(3):
        row_copy(i).start()
    dsend[...] = split_dot(ttr[g], low, ((1,), (0,))).reshape(4, 32, 128)
    for i in range(3):
        dense_copy(i).start()
    dense_out[g] = dsend[g]

    def update(f):
        listed = rg[f].astype(F32) + noise[f]
        mean = jnp.sum(listed * listed, axis=1, keepdims=True) * (1.0 / 128.0)
        new_acc = accb[f] + mean
        rows_out[f] = trows[f] - LEARN * listed / jnp.sqrt(new_acc)
        is_high = high_one(f)
        first, second, third = three(jnp.where(lanes == low_col[f], mean, 0.0))
        macc_out[f] = (
            split_dot(is_high, first, ((1,), (0,)))
            + split_dot(is_high, second, ((1,), (0,)))
            + split_dot(is_high, third, ((1,), (0,)))
        )

    update(g)
    for i in range(3):
        src = lax.rem(g + 3 - i, 4)
        pltpu.make_async_remote_copy(
            src_ref=rg.at[g], dst_ref=rg.at[src], send_sem=s6.at[i], recv_sem=r6.at[src],
            device_id=(lax.rem(g + 1 + i, 4), t), device_id_type=MESH,
        ).wait_recv()
        update(src)
    for i in range(3):
        src = lax.rem(g + 3 - i, 4)
        pltpu.make_async_remote_copy(
            src_ref=dsend.at[0], dst_ref=dense_out.at[src], send_sem=s7.at[i],
            recv_sem=r7.at[src], device_id=(lax.rem(g + 1 + i, 4), t), device_id_type=MESH,
        ).wait_recv()

    def drain(s, carry):
        sib_copy(s).wait_send()
        pass_on(s).wait_send()
        return carry

    def drain_far(s, carry):
        out_copy(s).wait_send()
        clip_copy(s + 1).wait_send()
        return carry

    lax.fori_loop(0, 16, drain, 0)
    lax.fori_loop(0, 15, drain_far, 0)
    for i in range(3):
        pltpu.make_async_remote_copy(
            src_ref=zsend.at[i], dst_ref=zrecv.at[g], send_sem=s5.at[i], recv_sem=r5.at[g],
            device_id=(lax.rem(g + 1 + i, 4), t), device_id_type=MESH,
        ).wait_send()
        row_copy(i).wait_send()
        dense_copy(i).wait_send()


def write_rows(
    touched_s, accum, macc, dense, dense_noise, table_h, rows,
    table_out, accum_out, dense_out, block, in_sem, out_sem,
):
    def load(f):
        return pltpu.make_async_copy(table_h.at[f], block.at[f], in_sem.at[f])

    def save(f):
        return pltpu.make_async_copy(block.at[f], table_out.at[f], out_sem.at[f])

    for f in range(4):
        load(f).start()
    dense_out[...] = dense[...] + dense_noise[...]
    for f in range(4):
        for q in range(16):
            lanes = slice(q * 128, (q + 1) * 128)
            accum_out[f : f + 1, lanes] = accum[f : f + 1, lanes] + macc[f, q : q + 1, :]
    for f in range(4):
        load(f).wait()

        def put(n, carry):
            k = pl.multiple_of(n * 32, 32)
            for i in range(32):
                block[f, pl.ds(touched_s[f, k + i], 1), :] = rows[f, pl.ds(k + i, 1), :]
            return carry

        lax.fori_loop(0, 16, put, 0)
        save(f).start()
    for f in range(4):
        save(f).wait()


def body(table, accum, w_hidden, w_out, ids, labels, touched, row_noise, dense_noise):
    vmem = pl.BlockSpec(memory_space=pltpu.VMEM)
    smem = pl.BlockSpec(memory_space=pltpu.SMEM)
    hbm = pl.BlockSpec(memory_space=pl.ANY)
    dma = pltpu.SemaphoreType.DMA
    rows, macc, dense = pl.pallas_call(
        core,
        out_shape=(
            jax.ShapeDtypeStruct((4, 512, 128), F32),
            jax.ShapeDtypeStruct((4, 16, 128), F32),
            jax.ShapeDtypeStruct((4, 32, 128), F32),
        ),
        in_specs=[smem, vmem, vmem, vmem, vmem, vmem, vmem, hbm, hbm],
        out_specs=(vmem, vmem, vmem),
        scratch_shapes=[
            pltpu.VMEM((4, 2048, 128), F32),
            pltpu.VMEM((128, 128, 128), BF),
            pltpu.VMEM((4, 512, 128), F32),
            pltpu.VMEM((4, 128, 512), BF),
            pltpu.VMEM((4, 16, 128), jnp.int32),
            pltpu.VMEM((4, 512, 128), jnp.int32),
            pltpu.VMEM((128, 512), BF),
            pltpu.VMEM((4, 512, 4096), BF),
            pltpu.VMEM((512, 256), BF),
            pltpu.VMEM((16, 144, 128), F32),
            pltpu.VMEM((16, 144, 128), BF),
            pltpu.VMEM((16, 144, 128), BF),
            pltpu.VMEM((16, 144, 128), BF),
            pltpu.VMEM((16, 144, 128), BF),
            pltpu.VMEM((128, 128), F32),
            pltpu.VMEM((32, 128, 128), BF),
            pltpu.VMEM((4, 512, 128), F32),
            pltpu.VMEM((4, 512, 128), F32),
            pltpu.VMEM((3, 512, 128), BF),
            pltpu.VMEM((4, 512, 128), BF),
            pltpu.VMEM((4, 512, 128), BF),
            pltpu.VMEM((4, 32, 128), F32),
            dma((2,)),
            dma((16,)), dma((16,)), dma((16,)), dma((16,)),
            dma((16,)), dma((16,)), dma((16,)), dma((16,)),
            dma((3,)), dma((4,)), dma((3,)), dma((4,)), dma((3,)), dma((4,)),
        ],
        compiler_params=pltpu.CompilerParams(
            collective_id=0, has_side_effects=True, vmem_limit_bytes=56 * 1024 * 1024
        ),
        cost_estimate=pl.CostEstimate(
            flops=6 * 10**9, bytes_accessed=12 * 2**20, transcendentals=10**5
        ),
        name="step",
    )(
        touched, accum, ids, touched, w_out.reshape(1, 128), labels.reshape(1, 128),
        row_noise, table, w_hidden,
    )
    return pl.pallas_call(
        write_rows,
        out_shape=(
            jax.ShapeDtypeStruct((4, 2048, 128), F32),
            jax.ShapeDtypeStruct((4, 2048), F32),
            jax.ShapeDtypeStruct((4, 32, 128), F32),
        ),
        in_specs=[smem, vmem, vmem, vmem, vmem, hbm, vmem],
        out_specs=(hbm, vmem, vmem),
        scratch_shapes=[pltpu.VMEM((4, 2048, 128), F32), dma((4,)), dma((4,))],
        compiler_params=pltpu.CompilerParams(vmem_limit_bytes=16 * 1024 * 1024),
        name="write_rows",
    )(touched, accum, macc, dense, dense_noise, table, rows)


def solution(mesh):
    in_specs = (
        P("table", None, None),
        P("table", None),
        P(),
        P(),
        P("table", None, "group"),
        P(("group", "table")),
        P("table", None),
        P("table", None, None),
        P("table", "group", None),
    )
    out_specs = (P("table", None, None), P("table", None), P("table", "group", None))
    return jax.shard_map(body, mesh=mesh, in_specs=in_specs, out_specs=out_specs, check_vma=False)
```

```python
import functools

import jax
import jax.numpy as jnp
from jax import lax
from jax.experimental import pallas as pl
from jax.experimental.pallas import tpu as pltpu
from jax.sharding import PartitionSpec as P

CLIP = 1.0
LEARN = 0.05
MESH = pl.DeviceIdType.MESH
BF = jnp.bfloat16
F32 = jnp.float32


def scale_of(i):
    return 16.0**i if i < 7 else 1.0


def split_dot(a, b, dims):
    return lax.dot_general(a, b, (dims, ((), ())), preferred_element_type=F32)


def core(
    touched_s, accum, ids, touched_v, w_out, labels, noise, table_h, w_h,
    rows_out, macc_out, dense_out,
    rows_v, macc_v, dense_v,
    table_v, w_v, trows, ttr, smap, low_col, wtr, counts, ring, pool, bags, keep, stage, sibin,
    outb, slots, pacc, clip, accb, s_acc, zsend, zrecv, rg, dsend,
    load_sem, s1, r1, s2, r2, s3, r3, s4, r4, s5, r5, s6, r6, s7, r7, s8, r8, r9, out_sem,
):
    g = lax.axis_index("group")
    t = lax.axis_index("table")
    c = lax.rem(t, 2)
    p = t // 2
    y = p // 4
    x = lax.rem(p, 4)
    sib = t + 1 - 2 * c

    def ahead(off):
        return lax.rem(y + off // 4, 4) * 4 + lax.rem(x + lax.rem(off, 4), 4)

    def behind(off):
        return lax.rem(y + 4 - off // 4, 4) * 4 + lax.rem(x + 4 - lax.rem(off, 4), 4)

    def load_table(f):
        return pltpu.make_async_copy(table_h.at[f], table_v.at[f], load_sem.at[f])

    for f in range(4):
        load_table(f).start()
    load_w = pltpu.make_async_copy(w_h, w_v, load_sem.at[4])
    load_w.start()

    barrier = pltpu.get_barrier_semaphore()

    def greet(off, carry):
        pl.semaphore_signal(
            barrier, inc=1, device_id=(g, ahead(off) * 2 + c), device_id_type=MESH
        )
        return carry

    lax.fori_loop(1, 16, greet, 0)
    pl.semaphore_signal(barrier, inc=1, device_id=(g, sib), device_id_type=MESH)
    for i in range(1, 4):
        pl.semaphore_signal(
            barrier, inc=1, device_id=(lax.rem(g + i, 4), t), device_id_type=MESH
        )

    high_of = lax.broadcasted_iota(jnp.int32, (16, 512), 0)
    low_of = lax.broadcasted_iota(jnp.int32, (128, 512), 0)
    lane = lax.broadcasted_iota(jnp.int32, (1, 512), 1)
    for f in range(4):
        row = touched_v[f : f + 1, :]
        row_low = row & 127
        is_high = high_of == lax.shift_right_logical(row, 7)
        is_low = jnp.where(low_of == row_low, 1.0, 0.0).astype(BF)
        number = jnp.concatenate(
            [
                jnp.where(is_high, lax.shift_right_logical(lane, 4), 0),
                jnp.where(is_high, lane & 15, 0),
            ],
            axis=0,
        )
        pair = split_dot(number.astype(F32).astype(BF), is_low, ((1,), (1,)))
        smap[f] = (pair[:16] * 16.0 + pair[16:]).astype(jnp.int32)
        for q in range(4):
            wide = jnp.broadcast_to(row_low[:, q * 128 : (q + 1) * 128], (128, 128))
            low_col[f, q * 128 : (q + 1) * 128, :] = wide.T

    bags[...] = jnp.zeros((16, 8, 256), F32)
    sublane = lax.broadcasted_iota(jnp.int32, (8, 128), 0)
    scale = jnp.concatenate([jnp.full((64, 128), 1.0 / scale_of(i), F32) for i in range(8)], axis=0)

    def count(s, f, target):
        b0 = pl.multiple_of(ahead(15 - s) * 256, 256)
        bag = ids[f, :, pl.ds(b0, 256)]
        others = jnp.zeros((8, 256), F32)
        for d in range(1, 5):
            others = others + jnp.where(bag == pltpu.roll(bag, d, 0), 1.0 if d == 4 else 2.0, 0.0)
        bags[s, pl.ds(f, 1), :] = 8.0 + jnp.sum(others, axis=0, keepdims=True)
        halves = []
        for half in range(2):
            part = bag[:, half * 128 : half * 128 + 128]
            high = lax.shift_right_logical(part, 7)
            low = part & 127
            slot = jnp.zeros((8, 128), jnp.int32)
            for q in range(16):
                row = jnp.broadcast_to(smap[f, q : q + 1, :], (8, 128))
                slot = jnp.where(high == q, jnp.take_along_axis(row, low, axis=1), slot)
            word = slot & 63
            digit = lax.shift_left(
                jnp.ones((8, 128), jnp.int32), lax.shift_right_logical(slot, 6) * 4
            )
            packed = [jnp.zeros((8, 128), jnp.int32) for _ in range(8)]
            for h in range(8):
                place = jnp.broadcast_to(word[h : h + 1], (8, 128)) - sublane
                value = jnp.broadcast_to(digit[h : h + 1], (8, 128))
                for v in range(8):
                    packed[v] = packed[v] + jnp.where(place == 8 * v, value, 0)
            packed = jnp.concatenate(packed, axis=0)
            tiles = []
            for i in range(7):
                tiles.append((packed & (15 << (4 * i))).astype(F32).astype(BF))
            tiles.append(lax.shift_right_logical(packed, 28).astype(F32).astype(BF))
            halves.append(jnp.concatenate(tiles, axis=0))
        block = jnp.concatenate(halves, axis=1)
        target[f] = block
        counts[f, :, pl.ds(b0, 256)] = block

    def early(n, carry):
        s = n // 4
        f = lax.rem(n, 4)
        count(s, f, ring.at[s])
        k = f * 128
        for i in range(128):
            r = touched_s[s, k + i]
            trows[s, pl.ds(k + i, 1), :] = table_v[s, pl.ds(r, 1), :]
        return carry

    for f in range(4):
        load_table(f).wait()
    lax.fori_loop(0, 16, early, 0)
    for f in range(4):
        ttr[f] = (trows[f] * scale).T.astype(BF)

    load_w.wait()
    for f in range(4):
        wtr[:, f * 128 : (f + 1) * 128] = w_v[t * 4 + f].astype(F32).T.astype(BF)

    pl.semaphore_wait(barrier, 19)

    rows8 = lax.broadcasted_iota(jnp.int32, (8, 256), 0)

    def relay(s):
        pltpu.make_async_remote_copy(
            src_ref=stage.at[s], dst_ref=sibin.at[s], send_sem=s1.at[s], recv_sem=r1.at[s],
            device_id=(g, sib), device_id_type=MESH,
        ).wait_recv()
        outb[s] = (keep[s] + sibin[s].astype(F32)).astype(BF)

    def out_copy(s):
        return pltpu.make_async_remote_copy(
            src_ref=outb.at[s], dst_ref=slots.at[p], send_sem=s2.at[s], recv_sem=r2.at[p],
            device_id=(g, ahead(15 - s) * 2 + c), device_id_type=MESH,
        )

    def sib_copy(s):
        return pltpu.make_async_remote_copy(
            src_ref=stage.at[s], dst_ref=sibin.at[s], send_sem=s1.at[s], recv_sem=r1.at[s],
            device_id=(g, sib), device_id_type=MESH,
        )

    def finish(s, source):
        sumsq = jnp.zeros((1, 256), F32)
        for f in range(4):
            pooled = split_dot(ttr[f], source[f], ((1,), (0,))).astype(BF)
            pool[f * 128 : f * 128 + 128, :] = pooled
            wide = pooled.astype(F32)
            sumsq = sumsq + jnp.sum(wide * wide, axis=0, keepdims=True)
        high = sumsq.astype(BF).astype(F32)
        first = c == 0
        repeats = bags[s]
        repeats = jnp.where(first, repeats, pltpu.roll(repeats, 4, 0))
        squares = jnp.where(rows8 == 2 * c, high, 0.0)
        squares = jnp.where(rows8 == 2 * c + 1, sumsq - high, squares)
        extra = jnp.concatenate([repeats, squares], axis=0)
        part = split_dot(wtr[...], pool[...], ((1,), (0,)))
        keep[s, 0:128, :] = jnp.where(first, part[:, :128], part[:, 128:])
        keep[s, 128:144, :] = jnp.where(first, extra[:, :128], extra[:, 128:])
        stage[s, 0:128, :] = jnp.where(first, part[:, 128:], part[:, :128]).astype(BF)
        stage[s, 128:144, :] = jnp.where(first, extra[:, 128:], extra[:, :128]).astype(BF)

    def send(s):
        relay(s)
        out_copy(s).start()

    def catch_up(s, carry):
        finish(s, ring.at[s])
        sib_copy(s).start()
        return carry

    lax.fori_loop(0, 3, catch_up, 0)
    send(0)

    def step(i, carry):
        s = 4 + 2 * i
        finish(s - 1, ring.at[3])
        for f in range(4):
            count(s, f, ring.at[0])
        sib_copy(s - 1).start()
        send(s - 3)
        finish(s, ring.at[0])
        for f in range(4):
            count(s + 1, f, ring.at[3])
        sib_copy(s).start()
        send(s - 2)
        return carry

    lax.fori_loop(0, 6, step, 0)
    finish(15, ring.at[3])
    sib_copy(15).start()
    send(13)
    send(14)
    relay(15)
    slots[p] = outb[15]

    pacc[...] = slots[p, 0:128, :].astype(F32)

    def arrive(s, carry):
        src = behind(15 - s)
        pltpu.make_async_remote_copy(
            src_ref=outb.at[s], dst_ref=slots.at[src], send_sem=s2.at[s], recv_sem=r2.at[src],
            device_id=(g, ahead(15 - s) * 2 + c), device_id_type=MESH,
        ).wait_recv()
        pacc[...] += slots[src, 0:128, :].astype(F32)
        return carry

    lax.fori_loop(0, 15, arrive, 0)
    pre = pacc[...]
    weight = jnp.broadcast_to(w_out[...], (128, 128)).T
    gate = jax.nn.sigmoid(pre)
    logit = jnp.sum(pre * gate * weight, axis=0, keepdims=True)
    prob = jax.nn.sigmoid(logit)
    delta = gate * (1.0 + pre * (1.0 - gate)) * weight * (prob - labels[...])
    delta_low = delta.astype(BF)

    nothing = jnp.zeros((128, 128), BF)
    twice = jnp.concatenate(
        [
            jnp.concatenate([delta_low, nothing], axis=1),
            jnp.concatenate([nothing, delta_low], axis=1),
        ],
        axis=0,
    )

    def norms(q, carry):
        acc, ssq = carry
        weights = w_v[pl.ds(q * 32, 32)]
        side = jnp.concatenate(
            [weights[:16].reshape(2048, 128), weights[16:].reshape(2048, 128)], axis=1
        )
        grad = split_dot(side, twice, ((1,), (0,)))
        square = jnp.sum((grad * grad).reshape(16, 128, 256), axis=1)
        for i in range(4):
            tail = slots[q * 4 + i, 128:144, :].astype(F32)
            half = square[:, :128] if i < 2 else square[:, 128:]
            acc = acc + half[(i % 2) * 8 : (i % 2) * 8 + 8] * tail[0:8]
            ssq = ssq + tail[8:16]
        return acc, ssq

    acc, ssq = lax.fori_loop(
        0, 4, norms, (jnp.zeros((8, 128), F32), jnp.zeros((8, 128), F32))
    )
    norm_sq = jnp.sum(acc, axis=0, keepdims=True) + jnp.sum(
        ssq, axis=0, keepdims=True
    ) * jnp.sum(delta * delta, axis=0, keepdims=True)
    factor = CLIP / jnp.maximum(jnp.sqrt(norm_sq), CLIP)
    clip[t] = (factor * delta).T.astype(BF)

    def high_one(f):
        row = lax.shift_right_logical(touched_v[pl.ds(f, 1), :], 7)
        return jnp.where(high_of == row, 1.0, 0.0).astype(BF)

    def three(values):
        first = values.astype(BF)
        rest = values - first.astype(F32)
        second = rest.astype(BF)
        return first, second, (rest - second.astype(F32)).astype(BF)

    def chip(down, over):
        return lax.rem(y + 4 - down, 4) * 4 + lax.rem(x + 4 - over, 4)

    def beside(i):
        if i < 3:
            return y * 4 + lax.rem(x + 1 + i, 4)
        return lax.rem(y + i - 2, 4) * 4 + x

    def clip_copy(i, src):
        return pltpu.make_async_remote_copy(
            src_ref=clip.at[src * 2 + c], dst_ref=clip.at[src * 2 + c], send_sem=s3.at[i],
            recv_sem=r3.at[src], device_id=(g, beside(i) * 2 + c), device_id_type=MESH,
        )

    def half_copy(n, src):
        upper = n % 6 < 3
        rows = pl.ds(0, 64) if upper else pl.ds(64, 64)
        return pltpu.make_async_remote_copy(
            src_ref=clip.at[src * 2 + c, rows], dst_ref=clip.at[src * 2 + c, rows],
            send_sem=s8.at[n], recv_sem=(r8 if upper else r9).at[src],
            device_id=(g, beside(n % 3 + (3 if upper else 0)) * 2 + c), device_id_type=MESH,
        )

    def pass_on(src):
        return pltpu.make_async_remote_copy(
            src_ref=clip.at[src * 2 + c], dst_ref=clip.at[src * 2 + c], send_sem=s4.at[src],
            recv_sem=r4.at[src], device_id=(g, sib), device_id_type=MESH,
        )

    def passed(src):
        return pltpu.make_async_remote_copy(
            src_ref=clip.at[src * 2 + c], dst_ref=clip.at[src * 2 + 1 - c], send_sem=s4.at[src],
            recv_sem=r4.at[src], device_id=(g, sib), device_id_type=MESH,
        )

    for i in (0, 3, 2, 5, 1, 4):
        clip_copy(i, p).start()
    pass_on(p).start()
    for i in (0, 2, 1):
        src = chip(0, i + 1)
        clip_copy(i, src).wait_recv()
        for j in (0, 2, 1):
            half_copy(i * 6 + j, src).start()
        pass_on(src).start()
        src = chip(i + 1, 0)
        clip_copy(i, src).wait_recv()
        for j in (3, 5, 4):
            half_copy(i * 6 + j, src).start()
        pass_on(src).start()

    lanes = lax.broadcasted_iota(jnp.int32, (512, 128), 1)
    for f in range(4):
        is_high = high_one(f)
        values = jnp.concatenate(
            [accum[f : f + 1, q * 128 : (q + 1) * 128] for q in range(16)], axis=0
        )
        first, second, third = three(values)
        spread_out = split_dot(
            jnp.concatenate([is_high, is_high, is_high], axis=0),
            jnp.concatenate([first, second, third], axis=0),
            ((0,), (0,)),
        )
        found = jnp.where(lanes == low_col[f], spread_out, 0.0)
        accb[f] = jnp.broadcast_to(jnp.sum(found, axis=1, keepdims=True), (512, 128))

    def diagonals(down):
        for over in (1, 3, 2):
            src = chip(down, over)
            half_copy(0, src).wait_recv()
            half_copy(3, src).wait_recv()
            pass_on(src).start()

    def product(f, src, chips):
        b0 = pl.multiple_of(src * 256, 256)
        block = clip[pl.ds(src * 2, 2 * chips)].reshape(256 * chips, 128)
        return split_dot(counts[f, :, pl.ds(b0, 256 * chips)], block, ((1,), (0,)))

    for over in range(4):
        passed(chip(0, over)).wait_recv()

    def own_row(f, carry):
        s_acc[f] = product(f, y * 4, 4)
        return carry

    lax.fori_loop(0, 4, own_row, 0)
    diagonals(1)
    for down in (1, 3, 2):
        passed(chip(down, 0)).wait_recv()
    diagonals(3)

    def own_column(f, carry):
        s_acc[f] += (
            product(f, chip(1, 0), 1) + product(f, chip(3, 0), 1) + product(f, chip(2, 0), 1)
        )
        return carry

    lax.fori_loop(0, 4, own_column, 0)
    diagonals(2)
    for down in (1, 3, 2):
        for over in (1, 3, 2):
            passed(chip(down, over)).wait_recv()

    def other_blocks(i, carry):
        f = lax.rem(g + 1 + i, 4)
        part = s_acc[f]
        for down in (1, 3, 2):
            for over in (1, 3, 2):
                part = part + product(f, chip(down, over), 1)
        part = part * scale
        s_acc[f] = part

        @pl.when(i < 3)
        def _():
            zsend[i] = part.astype(BF)
            pltpu.make_async_remote_copy(
                src_ref=zsend.at[i], dst_ref=zrecv.at[g], send_sem=s5.at[i],
                recv_sem=r5.at[g], device_id=(f, t), device_id_type=MESH,
            ).start()

        return carry

    lax.fori_loop(0, 4, other_blocks, 0)
    summed = s_acc[g]
    for i in range(3):
        src = lax.rem(g + 3 - i, 4)
        pltpu.make_async_remote_copy(
            src_ref=zsend.at[i], dst_ref=zrecv.at[src], send_sem=s5.at[i], recv_sem=r5.at[src],
            device_id=(lax.rem(g + 1 + i, 4), t), device_id_type=MESH,
        ).wait_recv()
        summed = summed + zrecv[src].astype(F32)
    low = summed.astype(BF)
    rg[g] = split_dot(low, w_v[t * 4 + g], ((1,), (1,))).astype(BF)

    def row_copy(i):
        return pltpu.make_async_remote_copy(
            src_ref=rg.at[g], dst_ref=rg.at[g], send_sem=s6.at[i], recv_sem=r6.at[g],
            device_id=(lax.rem(g + 1 + i, 4), t), device_id_type=MESH,
        )

    def dense_copy(i):
        to = lax.rem(g + 1 + i, 4)
        return pltpu.make_async_remote_copy(
            src_ref=dsend.at[to], dst_ref=dense_v.at[g], send_sem=s7.at[i], recv_sem=r7.at[g],
            device_id=(to, t), device_id_type=MESH,
        )

    for i in range(3):
        row_copy(i).start()
    dsend[...] = split_dot(trows[g].T.astype(BF), low, ((1,), (0,))).reshape(4, 32, 128)
    for i in range(3):
        dense_copy(i).start()
    dense_v[g] = dsend[g]

    def rows_save(f):
        return pltpu.make_async_copy(rows_v.at[f], rows_out.at[f], out_sem.at[f])

    def update(f):
        listed = rg[f].astype(F32) + noise[f]
        mean = jnp.sum(listed * listed, axis=1, keepdims=True) * (1.0 / 128.0)
        new_acc = accb[f] + mean
        rows_v[f] = trows[f] - LEARN * listed / jnp.sqrt(new_acc)
        is_high = high_one(f)
        first, second, third = three(jnp.where(lanes == low_col[f], mean, 0.0))
        macc_v[f] = (
            split_dot(is_high, first, ((1,), (0,)))
            + split_dot(is_high, second, ((1,), (0,)))
            + split_dot(is_high, third, ((1,), (0,)))
        )
        rows_save(f).start()

    update(g)
    for i in range(3):
        src = lax.rem(g + 3 - i, 4)
        pltpu.make_async_remote_copy(
            src_ref=rg.at[g], dst_ref=rg.at[src], send_sem=s6.at[i], recv_sem=r6.at[src],
            device_id=(lax.rem(g + 1 + i, 4), t), device_id_type=MESH,
        ).wait_recv()
        update(src)
    for i in range(3):
        src = lax.rem(g + 3 - i, 4)
        pltpu.make_async_remote_copy(
            src_ref=dsend.at[0], dst_ref=dense_v.at[src], send_sem=s7.at[i],
            recv_sem=r7.at[src], device_id=(lax.rem(g + 1 + i, 4), t), device_id_type=MESH,
        ).wait_recv()

    saves = [
        pltpu.make_async_copy(macc_v, macc_out, out_sem.at[4]),
        pltpu.make_async_copy(dense_v, dense_out, out_sem.at[5]),
    ]
    for save in saves:
        save.start()

    def drain(s, carry):
        sib_copy(s).wait_send()
        pass_on(s).wait_send()
        return carry

    def drain_far(s, carry):
        out_copy(s).wait_send()
        return carry

    lax.fori_loop(0, 16, drain, 0)
    lax.fori_loop(0, 15, drain_far, 0)
    for i in range(6):
        clip_copy(i, p).wait_send()
    for n in range(18):
        half_copy(n, p).wait_send()
    for i in range(3):
        pltpu.make_async_remote_copy(
            src_ref=zsend.at[i], dst_ref=zrecv.at[g], send_sem=s5.at[i], recv_sem=r5.at[g],
            device_id=(lax.rem(g + 1 + i, 4), t), device_id_type=MESH,
        ).wait_send()
        row_copy(i).wait_send()
        dense_copy(i).wait_send()
    for f in range(4):
        rows_save(f).wait()
    for save in saves:
        save.wait()


def write_rows(
    touched_h, accum_h, macc_h, dense_h, noise_h, table_h, rows_h,
    table_out, accum_out, dense_out,
    touched_s, accum, macc, dense, noise, block, rows, sem, in_sem, rows_sem, out_sem,
):
    def load(f):
        return pltpu.make_async_copy(table_h.at[f], block.at[f], in_sem.at[f])

    def load_rows(f):
        return pltpu.make_async_copy(rows_h.at[f], rows.at[f], rows_sem.at[f])

    def save(f):
        return pltpu.make_async_copy(block.at[f], table_out.at[f], out_sem.at[f])

    load(0).start()
    load_rows(0).start()
    small = [
        pltpu.make_async_copy(source, target, sem.at[i])
        for i, (source, target) in enumerate(
            (
                (touched_h, touched_s), (accum_h, accum), (macc_h, macc),
                (dense_h, dense), (noise_h, noise),
            )
        )
    ]
    for copy in small:
        copy.start()
    for f in range(1, 4):
        load(f).start()
        load_rows(f).start()
    for copy in small:
        copy.wait()
    dense[...] += noise[...]
    save_dense = pltpu.make_async_copy(dense, dense_out, sem.at[5])
    save_dense.start()
    for f in range(4):
        for q in range(16):
            lanes = slice(q * 128, (q + 1) * 128)
            accum[f : f + 1, lanes] += macc[f, q : q + 1, :]
    save_accum = pltpu.make_async_copy(accum, accum_out, sem.at[6])
    save_accum.start()
    for f in range(4):
        load(f).wait()
        load_rows(f).wait()

        def put(n, carry):
            k = pl.multiple_of(n * 64, 64)
            for i in range(64):
                block[f, pl.ds(touched_s[f, k + i], 1), :] = rows[f, pl.ds(k + i, 1), :]
            return carry

        lax.fori_loop(0, 8, put, 0)
        save(f).start()
    save_dense.wait()
    save_accum.wait()
    for f in range(4):
        save(f).wait()


def body(table, accum, w_hidden, w_out, ids, labels, touched, row_noise, dense_noise):
    vmem = pl.BlockSpec(memory_space=pltpu.VMEM)
    smem = pl.BlockSpec(memory_space=pltpu.SMEM)
    hbm = pl.BlockSpec(memory_space=pl.ANY)
    far = pl.BlockSpec(memory_space=pltpu.HBM)
    dma = pltpu.SemaphoreType.DMA
    rows, macc, dense = pl.pallas_call(
        core,
        out_shape=(
            jax.ShapeDtypeStruct((4, 512, 128), F32),
            jax.ShapeDtypeStruct((4, 16, 128), F32),
            jax.ShapeDtypeStruct((4, 32, 128), F32),
        ),
        in_specs=[smem, vmem, vmem, vmem, vmem, vmem, vmem, hbm, hbm],
        out_specs=(far, far, far),
        scratch_shapes=[
            pltpu.VMEM((4, 512, 128), F32),
            pltpu.VMEM((4, 16, 128), F32),
            pltpu.VMEM((4, 32, 128), F32),
            pltpu.VMEM((4, 2048, 128), F32),
            pltpu.VMEM((128, 128, 128), BF),
            pltpu.VMEM((4, 512, 128), F32),
            pltpu.VMEM((4, 128, 512), BF),
            pltpu.VMEM((4, 16, 128), jnp.int32),
            pltpu.VMEM((4, 512, 128), jnp.int32),
            pltpu.VMEM((128, 512), BF),
            pltpu.VMEM((4, 512, 4096), BF),
            pltpu.VMEM((4, 4, 512, 256), BF),
            pltpu.VMEM((512, 256), BF),
            pltpu.VMEM((16, 8, 256), F32),
            pltpu.VMEM((16, 144, 128), F32),
            pltpu.VMEM((16, 144, 128), BF),
            pltpu.VMEM((16, 144, 128), BF),
            pltpu.VMEM((16, 144, 128), BF),
            pltpu.VMEM((16, 144, 128), BF),
            pltpu.VMEM((128, 128), F32),
            pltpu.VMEM((32, 128, 128), BF),
            pltpu.VMEM((4, 512, 128), F32),
            pltpu.VMEM((4, 512, 128), F32),
            pltpu.VMEM((3, 512, 128), BF),
            pltpu.VMEM((4, 512, 128), BF),
            pltpu.VMEM((4, 512, 128), BF),
            pltpu.VMEM((4, 32, 128), F32),
            dma((5,)),
            dma((16,)), dma((16,)), dma((16,)), dma((16,)),
            dma((6,)), dma((16,)), dma((16,)), dma((16,)),
            dma((3,)), dma((4,)), dma((3,)), dma((4,)), dma((3,)), dma((4,)),
            dma((18,)), dma((16,)), dma((16,)), dma((6,)),
        ],
        compiler_params=pltpu.CompilerParams(
            collective_id=0, has_side_effects=True, vmem_limit_bytes=56 * 1024 * 1024
        ),
        cost_estimate=pl.CostEstimate(
            flops=6 * 10**9, bytes_accessed=12 * 2**20, transcendentals=10**5
        ),
        name="step",
    )(
        touched, accum, ids, touched, w_out.reshape(1, 128), labels.reshape(1, 128),
        row_noise, table, w_hidden,
    )
    return pl.pallas_call(
        write_rows,
        out_shape=(
            jax.ShapeDtypeStruct((4, 2048, 128), F32),
            jax.ShapeDtypeStruct((4, 2048), F32),
            jax.ShapeDtypeStruct((4, 32, 128), F32),
        ),
        in_specs=[hbm] * 7,
        out_specs=(hbm, hbm, hbm),
        scratch_shapes=[
            pltpu.SMEM((4, 512), jnp.int32),
            pltpu.VMEM((4, 2048), F32),
            pltpu.VMEM((4, 16, 128), F32),
            pltpu.VMEM((4, 32, 128), F32),
            pltpu.VMEM((4, 32, 128), F32),
            pltpu.VMEM((4, 2048, 128), F32),
            pltpu.VMEM((4, 512, 128), F32),
            dma((7,)), dma((4,)), dma((4,)), dma((4,)),
        ],
        compiler_params=pltpu.CompilerParams(vmem_limit_bytes=60 * 1024 * 1024),
        name="write_rows",
    )(touched, accum, macc, dense, dense_noise, table, rows)


def solution(mesh):
    in_specs = (
        P("table", None, None),
        P("table", None),
        P(),
        P(),
        P("table", None, "group"),
        P(("group", "table")),
        P("table", None),
        P("table", None, None),
        P("table", "group", None),
    )
    out_specs = (P("table", None, None), P("table", None), P("table", "group", None))
    return jax.shard_map(body, mesh=mesh, in_specs=in_specs, out_specs=out_specs, check_vma=False)
```

```python
import functools

import jax
import jax.numpy as jnp
from jax import lax
from jax.experimental import pallas as pl
from jax.experimental.pallas import tpu as pltpu
from jax.sharding import PartitionSpec as P

CLIP = 1.0
LEARN = 0.05
MESH = pl.DeviceIdType.MESH
BF = jnp.bfloat16
F32 = jnp.float32


def scale_of(i):
    return 16.0**i if i < 7 else 1.0


def split_dot(a, b, dims):
    return lax.dot_general(a, b, (dims, ((), ())), preferred_element_type=F32)


def core(
    touched_h, accum_h, ids_h, w_out_h, labels_h, noise_h, table_h, w_h,
    rows_out, macc_out, dense_out,
    touched_s, touched_v, accum, ids, w_out, labels, noise, rows_v, macc_v, dense_v,
    table_v, w_v, trows, ttr, smap, low_col, counts, ring, bags, both_ids, send_ids,
    outb, slots, pacc, clip, accb, s_acc, half_send, half_recv, zsend, zrecv, rg, dsend,
    load_sem, s1, r1, s2, r2, s3, r3, s4, r4, s5, r5, s6, r6, s7, r7, out_sem,
):
    g = lax.axis_index("group")
    t = lax.axis_index("table")
    c = lax.rem(t, 2)
    p = t // 2
    y = p // 4
    x = lax.rem(p, 4)
    sib = t + 1 - 2 * c

    def ahead(off):
        return lax.rem(y + off // 4, 4) * 4 + lax.rem(x + lax.rem(off, 4), 4)

    def behind(off):
        return lax.rem(y + 4 - off // 4, 4) * 4 + lax.rem(x + 4 - lax.rem(off, 4), 4)

    loads = [
        pltpu.make_async_copy(source, target, load_sem.at[i])
        for i, (source, target) in enumerate(
            (
                (touched_h, touched_v), (touched_h, touched_s), (ids_h, ids), (table_h, table_v),
                (w_h, w_v), (w_out_h, w_out), (labels_h, labels), (noise_h, noise),
                (accum_h, accum),
            )
        )
    ]
    for load in loads[:4]:
        load.start()

    barrier = pltpu.get_barrier_semaphore()

    def greet(off, carry):
        pl.semaphore_signal(
            barrier, inc=1, device_id=(g, ahead(off) * 2 + c), device_id_type=MESH
        )
        return carry

    lax.fori_loop(1, 16, greet, 0)
    pl.semaphore_signal(barrier, inc=1, device_id=(g, sib), device_id_type=MESH)
    for i in range(1, 4):
        pl.semaphore_signal(
            barrier, inc=1, device_id=(lax.rem(g + i, 4), t), device_id_type=MESH
        )

    loads[0].wait()
    high_of = lax.broadcasted_iota(jnp.int32, (16, 512), 0)
    low_of = lax.broadcasted_iota(jnp.int32, (128, 512), 0)
    lane = lax.broadcasted_iota(jnp.int32, (1, 512), 1)
    for f in range(4):
        row = touched_v[f : f + 1, :]
        row_low = row & 127
        is_high = high_of == lax.shift_right_logical(row, 7)
        is_low = jnp.where(low_of == row_low, 1.0, 0.0).astype(BF)
        number = jnp.concatenate(
            [
                jnp.where(is_high, lax.shift_right_logical(lane, 4), 0),
                jnp.where(is_high, lane & 15, 0),
            ],
            axis=0,
        )
        pair = split_dot(number.astype(F32).astype(BF), is_low, ((1,), (1,)))
        smap[c * 4 + f] = (pair[:16] * 16.0 + pair[16:]).astype(jnp.int32)
        for q in range(4):
            wide = jnp.broadcast_to(row_low[:, q * 128 : (q + 1) * 128], (128, 128))
            low_col[f, q * 128 : (q + 1) * 128, :] = wide.T

    loads[2].wait()
    for f in range(4):
        for q in range(16):
            to = slice(q * 128, q * 128 + 128)
            ours = pl.ds(pl.multiple_of(q * 256 + c * 128, 128), 128)
            theirs = pl.ds(pl.multiple_of(q * 256 + 128 - c * 128, 128), 128)
            both_ids[c * 4 + f, :, to] = ids[f, :, ours]
            send_ids[f, :, to] = ids[f, :, theirs]

    own_part = pl.ds(c * 4, 4)

    def trade(i):
        source, target = (
            (send_ids, both_ids.at[own_part]),
            (smap.at[own_part], smap.at[own_part]),
            (ttr.at[own_part, pl.ds(0, 128)], ttr.at[own_part, pl.ds(0, 128)]),
        )[i]
        return pltpu.make_async_remote_copy(
            src_ref=source, dst_ref=target, send_sem=s1.at[i], recv_sem=r1.at[i],
            device_id=(g, sib), device_id_type=MESH,
        )

    def traded(i):
        other = pl.ds(4 - c * 4, 4)
        source, target = (
            (send_ids, both_ids.at[other]),
            (smap.at[other], smap.at[other]),
            (ttr.at[other, pl.ds(0, 128)], ttr.at[other, pl.ds(0, 128)]),
        )[i]
        return pltpu.make_async_remote_copy(
            src_ref=source, dst_ref=target, send_sem=s1.at[i], recv_sem=r1.at[i],
            device_id=(g, sib), device_id_type=MESH,
        )

    def pair_ahead(s):
        off = 7 - s
        return lax.rem(y + off // 2, 4) * 4 + lax.rem(x // 2 + lax.rem(off, 2), 2) * 2

    def pair_behind(s):
        off = 7 - s
        return lax.rem(y + 4 - off // 2, 4) * 4 + lax.rem(x // 2 + lax.rem(off, 2), 2) * 2

    sublane = lax.broadcasted_iota(jnp.int32, (8, 128), 0)
    scale = jnp.concatenate([jnp.full((64, 128), 1.0 / scale_of(i), F32) for i in range(8)], axis=0)

    def count(s, f):
        b0 = pl.multiple_of(pair_ahead(s) * 128, 256)
        bag = both_ids[f, :, pl.ds(b0, 256)]
        others = jnp.zeros((8, 256), F32)
        for d in range(1, 5):
            others = others + jnp.where(bag == pltpu.roll(bag, d, 0), 1.0 if d == 4 else 2.0, 0.0)
        slots_of = []
        for half in range(2):
            part = bag[:, half * 128 : half * 128 + 128]
            high = lax.shift_right_logical(part, 7)
            low = part & 127
            slot = jnp.zeros((8, 128), jnp.int32)
            for q in range(16):
                row = jnp.broadcast_to(smap[f, q : q + 1, :], (8, 128))
                slot = jnp.where(high == q, jnp.take_along_axis(row, low, axis=1), slot)
            slots_of.append(slot)
        halves = []
        for slot in slots_of:
            word = slot & 63
            digit = lax.shift_left(
                jnp.ones((8, 128), jnp.int32), lax.shift_right_logical(slot, 6) * 4
            )
            packed = [jnp.zeros((8, 128), jnp.int32) for _ in range(8)]
            for h in range(8):
                place = jnp.broadcast_to(word[h : h + 1], (8, 128)) - sublane
                value = jnp.broadcast_to(digit[h : h + 1], (8, 128))
                for v in range(8):
                    packed[v] = packed[v] + jnp.where(place == 8 * v, value, 0)
            packed = jnp.concatenate(packed, axis=0)
            tiles = []
            for i in range(7):
                tiles.append((packed & (15 << (4 * i))).astype(F32).astype(BF))
            tiles.append(lax.shift_right_logical(packed, 28).astype(F32).astype(BF))
            halves.append(jnp.concatenate(tiles, axis=0))
        block = jnp.concatenate(halves, axis=1)
        bags[s, pl.ds(f, 1), :] = 8.0 + jnp.sum(others, axis=0, keepdims=True)
        ring[f] = block
        counts[f, :, pl.ds(b0, 256)] = block

    def early(n, carry):
        count(0, c * 4 + n)
        return carry

    def early_other(n, carry):
        count(0, 4 - c * 4 + n)
        return carry

    lax.fori_loop(0, 4, early, 0)
    pl.semaphore_wait(barrier, 19)
    trade(0).start()
    trade(1).start()
    loads[1].wait()
    loads[3].wait()
    for load in loads[4:]:
        load.start()

    def pick(n, carry):
        f = n // 16
        k = lax.rem(n, 16) * 32
        for i in range(32):
            r = touched_s[f, k + i]
            trows[f, pl.ds(k + i, 1), :] = table_v[f, pl.ds(r, 1), :]
        return carry

    lax.fori_loop(0, 64, pick, 0)
    for f in range(4):
        ttr[c * 4 + f, 0:128, :] = (trows[f] * scale).T.astype(BF)
    trade(2).start()
    traded(0).wait_recv()
    traded(1).wait_recv()
    lax.fori_loop(0, 4, early_other, 0)
    loads[4].wait()
    traded(2).wait_recv()
    for f in range(8):
        side = w_v[p * 8 + f].astype(F32).T.astype(BF)
        ttr[f, 128:256, :] = split_dot(side, ttr[f, 0:128, :], ((1,), (0,))).astype(BF)

    rows8 = lax.broadcasted_iota(jnp.int32, (8, 256), 0)

    def out_copy(s, half):
        return pltpu.make_async_remote_copy(
            src_ref=outb.at[s * 2 + half], dst_ref=slots.at[p], send_sem=s2.at[s * 2 + half],
            recv_sem=r2.at[p], device_id=(g, (pair_ahead(s) + half) * 2 + c),
            device_id_type=MESH,
        )

    def finish(s, after):
        sumsq = jnp.zeros((1, 256), F32)
        part = jnp.zeros((128, 256), F32)
        for f in range(8):
            both = split_dot(ttr[f], ring[f], ((1,), (0,)))
            pooled = both[:128].astype(BF).astype(F32)
            sumsq = sumsq + jnp.sum(pooled * pooled, axis=0, keepdims=True)
            part = part + both[128:]
            if after is not None:
                count(after, f)
        high = sumsq.astype(BF).astype(F32)
        squares = jnp.where(rows8 == 0, high, 0.0)
        squares = jnp.where(rows8 == 1, sumsq - high, squares)
        extra = jnp.concatenate([bags[s], squares], axis=0)
        for half in range(2):
            lanes_of = slice(half * 128, half * 128 + 128)
            outb[s * 2 + half, 0:128, :] = part[:, lanes_of].astype(BF)
            outb[s * 2 + half, 128:144, :] = extra[:, lanes_of].astype(BF)

    def step(s, carry):
        finish(s, s + 1)
        out_copy(s, 0).start()
        out_copy(s, 1).start()
        return carry

    lax.fori_loop(0, 7, step, 0)
    finish(7, None)
    odd = lax.rem(x, 2)
    out_copy(7, 1 - odd).start()
    slots[p] = outb[14 + odd]
    for f in range(8):
        s_acc[f] = jnp.zeros((512, 128), F32)

    pacc[...] = slots[p, 0:128, :].astype(F32)

    def from_chip(src):
        pltpu.make_async_remote_copy(
            src_ref=outb.at[0], dst_ref=slots.at[src], send_sem=s2.at[0], recv_sem=r2.at[src],
            device_id=(g, sib), device_id_type=MESH,
        ).wait_recv()
        pacc[...] += slots[src, 0:128, :].astype(F32)

    def arrive(s, carry):
        from_chip(pair_behind(s))
        from_chip(pair_behind(s) + 1)
        return carry

    lax.fori_loop(0, 7, arrive, 0)
    from_chip(p + 1 - 2 * odd)
    loads[5].wait()
    loads[6].wait()
    pre = pacc[...]
    weight = jnp.broadcast_to(w_out[...], (128, 128)).T
    gate = jax.nn.sigmoid(pre)
    logit = jnp.sum(pre * gate * weight, axis=0, keepdims=True)
    prob = jax.nn.sigmoid(logit)
    delta = gate * (1.0 + pre * (1.0 - gate)) * weight * (prob - labels[...])
    delta_low = delta.astype(BF)

    nothing = jnp.zeros((128, 128), BF)
    twice = jnp.concatenate(
        [
            jnp.concatenate([delta_low, nothing], axis=1),
            jnp.concatenate([nothing, delta_low], axis=1),
        ],
        axis=0,
    )

    def norms(q, carry):
        acc, ssq = carry
        weights = w_v[pl.ds(q * 32, 32)]
        side = jnp.concatenate(
            [weights[:16].reshape(2048, 128), weights[16:].reshape(2048, 128)], axis=1
        )
        grad = split_dot(side, twice, ((1,), (0,)))
        square = jnp.sum((grad * grad).reshape(16, 128, 256), axis=1)
        for i in range(4):
            tail = slots[q * 4 + i, 128:144, :].astype(F32)
            half = square[:, :128] if i < 2 else square[:, 128:]
            acc = acc + half[(i % 2) * 8 : (i % 2) * 8 + 8] * tail[0:8]
            ssq = ssq + tail[8:16]
        return acc, ssq

    acc, ssq = lax.fori_loop(
        0, 4, norms, (jnp.zeros((8, 128), F32), jnp.zeros((8, 128), F32))
    )
    norm_sq = jnp.sum(acc, axis=0, keepdims=True) + jnp.sum(
        ssq, axis=0, keepdims=True
    ) * jnp.sum(delta * delta, axis=0, keepdims=True)
    factor = CLIP / jnp.maximum(jnp.sqrt(norm_sq), CLIP)
    clip[p] = (factor * delta).T.astype(BF)

    def high_one(f):
        row = lax.shift_right_logical(touched_v[pl.ds(f, 1), :], 7)
        return jnp.where(high_of == row, 1.0, 0.0).astype(BF)

    def three(values):
        first = values.astype(BF)
        rest = values - first.astype(F32)
        second = rest.astype(BF)
        return first, second, (rest - second.astype(F32)).astype(BF)

    def nth(table, n):
        packed = sum(v << (4 * i) for i, v in enumerate(table))
        packed = packed - (1 << 32) if packed >= 1 << 31 else packed
        return lax.shift_right_logical(jnp.int32(packed), 4 * n) & 15

    def offsets(n):
        return nth((0, 3, 12, 15, 13, 8, 9, 11), n), nth((1, 4, 5, 7, 2, 6, 14, 10), n)

    def clip_copy(off, src):
        return pltpu.make_async_remote_copy(
            src_ref=clip.at[src], dst_ref=clip.at[src], send_sem=s3.at[off],
            recv_sem=r3.at[src], device_id=(g, ahead(off) * 2 + c), device_id_type=MESH,
        )

    def spread(n, carry):
        for off in offsets(n):
            clip_copy(off, p).start()
        return carry

    clip_copy(1, p).start()
    lax.fori_loop(1, 8, spread, 0)

    lanes = lax.broadcasted_iota(jnp.int32, (512, 128), 1)
    loads[8].wait()
    for f in range(4):
        is_high = high_one(f)
        values = jnp.concatenate(
            [accum[f : f + 1, q * 128 : (q + 1) * 128] for q in range(16)], axis=0
        )
        first, second, third = three(values)
        spread_out = split_dot(
            jnp.concatenate([is_high, is_high, is_high], axis=0),
            jnp.concatenate([first, second, third], axis=0),
            ((0,), (0,)),
        )
        found = jnp.where(lanes == low_col[f], spread_out, 0.0)
        accb[f] = jnp.broadcast_to(jnp.sum(found, axis=1, keepdims=True), (512, 128))

    def product(f, n):
        chips = [behind(off) for off in offsets(n)]
        side = [counts[f, :, pl.ds(pl.multiple_of(q * 128, 128), 128)] for q in chips]
        rows = [clip[q] for q in chips]
        return split_dot(
            jnp.concatenate(side, axis=1), jnp.concatenate(rows, axis=0), ((1,), (0,))
        )

    def arrived(off):
        clip_copy(off, behind(off)).wait_recv()

    def drain(s, carry):
        out_copy(s, 0).wait_send()
        out_copy(s, 1).wait_send()
        return carry

    lax.fori_loop(0, 7, drain, 0)
    out_copy(7, 1 - odd).wait_send()
    for i in range(3):
        trade(i).wait_send()

    def gather(n, carry):
        for f in range(8):
            s_acc[f] += product(f, n - 1)
        for off in offsets(n):
            arrived(off)
        return carry

    arrived(1)
    lax.fori_loop(1, 8, gather, 0)

    def half_copy(i):
        return pltpu.make_async_remote_copy(
            src_ref=half_send.at[i], dst_ref=half_recv.at[i], send_sem=s4.at[i],
            recv_sem=r4.at[i], device_id=(g, sib), device_id_type=MESH,
        )

    def other_features(i, carry):
        f = 4 - c * 4 + lax.rem(g + 1 + i, 4)
        half_send[i] = ((s_acc[f] + product(f, 7)) * scale).astype(BF)
        half_copy(i).start()
        return carry

    lax.fori_loop(0, 4, other_features, 0)

    def own_features(i, carry):
        to = lax.rem(g + 1 + i, 4)
        f = c * 4 + to
        part = (s_acc[f] + product(f, 7)) * scale
        half_copy(i).wait_recv()
        part = part + half_recv[i].astype(F32)
        s_acc[f] = part

        @pl.when(i < 3)
        def _():
            zsend[i] = part.astype(BF)
            pltpu.make_async_remote_copy(
                src_ref=zsend.at[i], dst_ref=zrecv.at[g], send_sem=s5.at[i],
                recv_sem=r5.at[g], device_id=(to, t), device_id_type=MESH,
            ).start()

        return carry

    lax.fori_loop(0, 4, own_features, 0)

    def drain_far(off, carry):
        clip_copy(off, p).wait_send()
        return carry

    lax.fori_loop(1, 16, drain_far, 0)
    for i in range(4):
        half_copy(i).wait_send()
    summed = s_acc[c * 4 + g]
    for i in range(3):
        src = lax.rem(g + 3 - i, 4)
        pltpu.make_async_remote_copy(
            src_ref=zsend.at[i], dst_ref=zrecv.at[src], send_sem=s5.at[i], recv_sem=r5.at[src],
            device_id=(lax.rem(g + 1 + i, 4), t), device_id_type=MESH,
        ).wait_recv()
        summed = summed + zrecv[src].astype(F32)
    low = summed.astype(BF)
    rg[g] = split_dot(low, w_v[t * 4 + g], ((1,), (1,))).astype(BF)

    def row_copy(i):
        return pltpu.make_async_remote_copy(
            src_ref=rg.at[g], dst_ref=rg.at[g], send_sem=s6.at[i], recv_sem=r6.at[g],
            device_id=(lax.rem(g + 1 + i, 4), t), device_id_type=MESH,
        )

    def dense_copy(i):
        to = lax.rem(g + 1 + i, 4)
        return pltpu.make_async_remote_copy(
            src_ref=dsend.at[to], dst_ref=dense_v.at[g], send_sem=s7.at[i], recv_sem=r7.at[g],
            device_id=(to, t), device_id_type=MESH,
        )

    for i in range(3):
        row_copy(i).start()
    dsend[...] = split_dot(trows[g].T.astype(BF), low, ((1,), (0,))).reshape(4, 32, 128)
    for i in range(3):
        dense_copy(i).start()
    dense_v[g] = dsend[g]

    def rows_save(f):
        return pltpu.make_async_copy(rows_v.at[f], rows_out.at[f], out_sem.at[f])

    def update(f):
        listed = rg[f].astype(F32) + noise[f]
        mean = jnp.sum(listed * listed, axis=1, keepdims=True) * (1.0 / 128.0)
        new_acc = accb[f] + mean
        rows_v[f] = trows[f] - LEARN * listed / jnp.sqrt(new_acc)
        is_high = high_one(f)
        first, second, third = three(jnp.where(lanes == low_col[f], mean, 0.0))
        macc_v[f] = (
            split_dot(is_high, first, ((1,), (0,)))
            + split_dot(is_high, second, ((1,), (0,)))
            + split_dot(is_high, third, ((1,), (0,)))
        )
        rows_save(f).start()

    loads[7].wait()
    update(g)
    for i in range(3):
        src = lax.rem(g + 3 - i, 4)
        pltpu.make_async_remote_copy(
            src_ref=rg.at[g], dst_ref=rg.at[src], send_sem=s6.at[i], recv_sem=r6.at[src],
            device_id=(lax.rem(g + 1 + i, 4), t), device_id_type=MESH,
        ).wait_recv()
        update(src)
    for i in range(3):
        src = lax.rem(g + 3 - i, 4)
        pltpu.make_async_remote_copy(
            src_ref=dsend.at[0], dst_ref=dense_v.at[src], send_sem=s7.at[i],
            recv_sem=r7.at[src], device_id=(lax.rem(g + 1 + i, 4), t), device_id_type=MESH,
        ).wait_recv()

    saves = [
        pltpu.make_async_copy(macc_v, macc_out, out_sem.at[4]),
        pltpu.make_async_copy(dense_v, dense_out, out_sem.at[5]),
    ]
    for save in saves:
        save.start()

    for i in range(3):
        pltpu.make_async_remote_copy(
            src_ref=zsend.at[i], dst_ref=zrecv.at[g], send_sem=s5.at[i], recv_sem=r5.at[g],
            device_id=(lax.rem(g + 1 + i, 4), t), device_id_type=MESH,
        ).wait_send()
        row_copy(i).wait_send()
        dense_copy(i).wait_send()
    for f in range(4):
        rows_save(f).wait()
    for save in saves:
        save.wait()


def write_rows(
    touched_h, accum_h, macc_h, dense_h, noise_h, table_h, rows_h,
    table_out, accum_out, dense_out,
    touched_s, accum, macc, dense, noise, block, rows, sem, in_sem, rows_sem, out_sem,
):
    def load(f):
        return pltpu.make_async_copy(table_h.at[f], block.at[f], in_sem.at[f])

    def load_rows(f):
        return pltpu.make_async_copy(rows_h.at[f], rows.at[f], rows_sem.at[f])

    def save(f):
        return pltpu.make_async_copy(block.at[f], table_out.at[f], out_sem.at[f])

    load(0).start()
    load_rows(0).start()
    small = [
        pltpu.make_async_copy(source, target, sem.at[i])
        for i, (source, target) in enumerate(
            (
                (touched_h, touched_s), (accum_h, accum), (macc_h, macc),
                (dense_h, dense), (noise_h, noise),
            )
        )
    ]
    for copy in small:
        copy.start()
    for f in range(1, 4):
        load(f).start()
        load_rows(f).start()
    for copy in small:
        copy.wait()
    dense[...] += noise[...]
    save_dense = pltpu.make_async_copy(dense, dense_out, sem.at[5])
    save_dense.start()
    for f in range(4):
        for q in range(16):
            lanes = slice(q * 128, (q + 1) * 128)
            accum[f : f + 1, lanes] += macc[f, q : q + 1, :]
    save_accum = pltpu.make_async_copy(accum, accum_out, sem.at[6])
    save_accum.start()
    for f in range(4):
        load(f).wait()
        load_rows(f).wait()

        def put(n, carry):
            k = pl.multiple_of(n * 64, 64)
            for i in range(64):
                block[f, pl.ds(touched_s[f, k + i], 1), :] = rows[f, pl.ds(k + i, 1), :]
            return carry

        lax.fori_loop(0, 8, put, 0)
        save(f).start()
    save_dense.wait()
    save_accum.wait()
    for f in range(4):
        save(f).wait()


def body(table, accum, w_hidden, w_out, ids, labels, touched, row_noise, dense_noise):
    hbm = pl.BlockSpec(memory_space=pl.ANY)
    dma = pltpu.SemaphoreType.DMA
    rows, macc, dense = pl.pallas_call(
        core,
        out_shape=(
            jax.ShapeDtypeStruct((4, 512, 128), F32),
            jax.ShapeDtypeStruct((4, 16, 128), F32),
            jax.ShapeDtypeStruct((4, 32, 128), F32),
        ),
        in_specs=[hbm] * 8,
        out_specs=(hbm, hbm, hbm),
        scratch_shapes=[
            pltpu.SMEM((4, 512), jnp.int32),
            pltpu.VMEM((4, 512), jnp.int32),
            pltpu.VMEM((4, 2048), F32),
            pltpu.VMEM((4, 8, 4096), jnp.int32),
            pltpu.VMEM((1, 128), F32),
            pltpu.VMEM((1, 128), F32),
            pltpu.VMEM((4, 512, 128), F32),
            pltpu.VMEM((4, 512, 128), F32),
            pltpu.VMEM((4, 16, 128), F32),
            pltpu.VMEM((4, 32, 128), F32),
            pltpu.VMEM((4, 2048, 128), F32),
            pltpu.VMEM((128, 128, 128), BF),
            pltpu.VMEM((4, 512, 128), F32),
            pltpu.VMEM((8, 256, 512), BF),
            pltpu.VMEM((8, 16, 128), jnp.int32),
            pltpu.VMEM((4, 512, 128), jnp.int32),
            pltpu.VMEM((8, 512, 2048), BF),
            pltpu.VMEM((8, 512, 256), BF),
            pltpu.VMEM((8, 8, 256), F32),
            pltpu.VMEM((8, 8, 2048), jnp.int32),
            pltpu.VMEM((4, 8, 2048), jnp.int32),
            pltpu.VMEM((16, 144, 128), BF),
            pltpu.VMEM((16, 144, 128), BF),
            pltpu.VMEM((128, 128), F32),
            pltpu.VMEM((16, 128, 128), BF),
            pltpu.VMEM((4, 512, 128), F32),
            pltpu.VMEM((8, 512, 128), F32),
            pltpu.VMEM((4, 512, 128), BF),
            pltpu.VMEM((4, 512, 128), BF),
            pltpu.VMEM((3, 512, 128), BF),
            pltpu.VMEM((4, 512, 128), BF),
            pltpu.VMEM((4, 512, 128), BF),
            pltpu.VMEM((4, 32, 128), F32),
            dma((9,)),
            dma((3,)), dma((3,)), dma((16,)), dma((16,)), dma((16,)), dma((16,)),
            dma((4,)), dma((4,)),
            dma((3,)), dma((4,)), dma((3,)), dma((4,)), dma((3,)), dma((4,)),
            dma((6,)),
        ],
        compiler_params=pltpu.CompilerParams(
            collective_id=0, has_side_effects=True, vmem_limit_bytes=56 * 1024 * 1024
        ),
        cost_estimate=pl.CostEstimate(
            flops=6 * 10**9, bytes_accessed=12 * 2**20, transcendentals=10**5
        ),
        name="step",
    )(
        touched, accum, ids, w_out.reshape(1, 128), labels.reshape(1, 128),
        row_noise, table, w_hidden,
    )
    return pl.pallas_call(
        write_rows,
        out_shape=(
            jax.ShapeDtypeStruct((4, 2048, 128), F32),
            jax.ShapeDtypeStruct((4, 2048), F32),
            jax.ShapeDtypeStruct((4, 32, 128), F32),
        ),
        in_specs=[hbm] * 7,
        out_specs=(hbm, hbm, hbm),
        scratch_shapes=[
            pltpu.SMEM((4, 512), jnp.int32),
            pltpu.VMEM((4, 2048), F32),
            pltpu.VMEM((4, 16, 128), F32),
            pltpu.VMEM((4, 32, 128), F32),
            pltpu.VMEM((4, 32, 128), F32),
            pltpu.VMEM((4, 2048, 128), F32),
            pltpu.VMEM((4, 512, 128), F32),
            dma((7,)), dma((4,)), dma((4,)), dma((4,)),
        ],
        compiler_params=pltpu.CompilerParams(vmem_limit_bytes=60 * 1024 * 1024),
        name="write_rows",
    )(touched, accum, macc, dense, dense_noise, table, rows)


def solution(mesh):
    in_specs = (
        P("table", None, None),
        P("table", None),
        P(),
        P(),
        P("table", None, "group"),
        P(("group", "table")),
        P("table", None),
        P("table", None, None),
        P("table", "group", None),
    )
    out_specs = (P("table", None, None), P("table", None), P("table", "group", None))
    return jax.shard_map(body, mesh=mesh, in_specs=in_specs, out_specs=out_specs, check_vma=False)
```

```python
import functools

import jax
import jax.numpy as jnp
from jax import lax
from jax.experimental import pallas as pl
from jax.experimental.pallas import tpu as pltpu
from jax.sharding import PartitionSpec as P

CLIP = 1.0
LEARN = 0.05
MESH = pl.DeviceIdType.MESH
BF = jnp.bfloat16
F32 = jnp.float32


def scale_of(i):
    return 16.0**i if i < 7 else 1.0


def split_dot(a, b, dims):
    return lax.dot_general(a, b, (dims, ((), ())), preferred_element_type=F32)


def core(
    touched_h, accum_h, ids_h, w_out_h, labels_h, noise_h, table_h, w_h,
    rows_out, macc_out, dense_out,
    touched_s, touched_v, accum, ids, w_out, labels, noise, rows_v, macc_v, dense_v,
    table_v, w_v, trows, ttr, smap, low_col, counts, ring, bags, both_ids, send_ids,
    outb, slots, pacc, clip, accb, s_acc, half_send, half_recv, zsend, zrecv, rg, dsend,
    load_sem, s1, r1, s2, r2, s3, r3, s4, r4, s5, r5, s6, r6, s7, r7, out_sem,
):
    g = lax.axis_index("group")
    t = lax.axis_index("table")
    c = lax.rem(t, 2)
    p = t // 2
    y = p // 4
    x = lax.rem(p, 4)
    sib = t + 1 - 2 * c

    def ahead(off):
        return lax.rem(y + off // 4, 4) * 4 + lax.rem(x + lax.rem(off, 4), 4)

    def behind(off):
        return lax.rem(y + 4 - off // 4, 4) * 4 + lax.rem(x + 4 - lax.rem(off, 4), 4)

    loads = [
        pltpu.make_async_copy(source, target, load_sem.at[i])
        for i, (source, target) in enumerate(
            (
                (touched_h, touched_v), (touched_h, touched_s), (ids_h, ids), (table_h, table_v),
                (w_h, w_v), (w_out_h, w_out), (labels_h, labels), (noise_h, noise),
                (accum_h, accum),
            )
        )
    ]
    for load in loads[:4]:
        load.start()

    barrier = pltpu.get_barrier_semaphore()

    def greet(off, carry):
        pl.semaphore_signal(
            barrier, inc=1, device_id=(g, ahead(off) * 2 + c), device_id_type=MESH
        )
        return carry

    lax.fori_loop(1, 16, greet, 0)
    pl.semaphore_signal(barrier, inc=1, device_id=(g, sib), device_id_type=MESH)
    for i in range(1, 4):
        pl.semaphore_signal(
            barrier, inc=1, device_id=(lax.rem(g + i, 4), t), device_id_type=MESH
        )

    loads[0].wait()
    high_of = lax.broadcasted_iota(jnp.int32, (16, 512), 0)
    low_of = lax.broadcasted_iota(jnp.int32, (128, 512), 0)
    lane = lax.broadcasted_iota(jnp.int32, (1, 512), 1)
    for f in range(4):
        row = touched_v[f : f + 1, :]
        row_low = row & 127
        is_high = high_of == lax.shift_right_logical(row, 7)
        is_low = jnp.where(low_of == row_low, 1.0, 0.0).astype(BF)
        number = jnp.concatenate(
            [
                jnp.where(is_high, lax.shift_right_logical(lane, 4), 0),
                jnp.where(is_high, lane & 15, 0),
            ],
            axis=0,
        )
        pair = split_dot(number.astype(F32).astype(BF), is_low, ((1,), (1,)))
        smap[c * 4 + f] = (pair[:16] * 16.0 + pair[16:]).astype(jnp.int32)
        for q in range(4):
            wide = jnp.broadcast_to(row_low[:, q * 128 : (q + 1) * 128], (128, 128))
            low_col[f, q * 128 : (q + 1) * 128, :] = wide.T

    loads[2].wait()
    for f in range(4):
        for q in range(16):
            to = slice(q * 128, q * 128 + 128)
            ours = pl.ds(pl.multiple_of(q * 256 + c * 128, 128), 128)
            theirs = pl.ds(pl.multiple_of(q * 256 + 128 - c * 128, 128), 128)
            both_ids[c * 4 + f, :, to] = ids[f, :, ours]
            send_ids[f, :, to] = ids[f, :, theirs]

    own_part = pl.ds(c * 4, 4)

    def trade(i):
        source, target = (
            (send_ids, both_ids.at[own_part]),
            (smap.at[own_part], smap.at[own_part]),
            (ttr.at[own_part, pl.ds(0, 128)], ttr.at[own_part, pl.ds(0, 128)]),
        )[i]
        return pltpu.make_async_remote_copy(
            src_ref=source, dst_ref=target, send_sem=s1.at[i], recv_sem=r1.at[i],
            device_id=(g, sib), device_id_type=MESH,
        )

    def traded(i):
        other = pl.ds(4 - c * 4, 4)
        source, target = (
            (send_ids, both_ids.at[other]),
            (smap.at[other], smap.at[other]),
            (ttr.at[other, pl.ds(0, 128)], ttr.at[other, pl.ds(0, 128)]),
        )[i]
        return pltpu.make_async_remote_copy(
            src_ref=source, dst_ref=target, send_sem=s1.at[i], recv_sem=r1.at[i],
            device_id=(g, sib), device_id_type=MESH,
        )

    def pair_ahead(s):
        off = 7 - s
        return lax.rem(y + off // 2, 4) * 4 + lax.rem(x // 2 + lax.rem(off, 2), 2) * 2

    def pair_behind(s):
        off = 7 - s
        return lax.rem(y + 4 - off // 2, 4) * 4 + lax.rem(x // 2 + lax.rem(off, 2), 2) * 2

    sublane = lax.broadcasted_iota(jnp.int32, (8, 128), 0)
    scale = jnp.concatenate([jnp.full((64, 128), 1.0 / scale_of(i), F32) for i in range(8)], axis=0)

    def count(s, f):
        b0 = pl.multiple_of(pair_ahead(s) * 128, 256)
        bag = both_ids[f, :, pl.ds(b0, 256)]
        others = jnp.zeros((8, 256), F32)
        for d in range(1, 5):
            others = others + jnp.where(bag == pltpu.roll(bag, d, 0), 1.0 if d == 4 else 2.0, 0.0)
        slots_of = []
        for half in range(2):
            part = bag[:, half * 128 : half * 128 + 128]
            high = lax.shift_right_logical(part, 7)
            low = part & 127
            slot = jnp.zeros((8, 128), jnp.int32)
            for q in range(16):
                row = jnp.broadcast_to(smap[f, q : q + 1, :], (8, 128))
                slot = jnp.where(high == q, jnp.take_along_axis(row, low, axis=1), slot)
            slots_of.append(slot)
        halves = []
        for slot in slots_of:
            word = slot & 63
            digit = lax.shift_left(
                jnp.ones((8, 128), jnp.int32), lax.shift_right_logical(slot, 6) * 4
            )
            packed = [jnp.zeros((8, 128), jnp.int32) for _ in range(8)]
            for h in range(8):
                place = jnp.broadcast_to(word[h : h + 1], (8, 128)) - sublane
                value = jnp.broadcast_to(digit[h : h + 1], (8, 128))
                for v in range(8):
                    packed[v] = packed[v] + jnp.where(place == 8 * v, value, 0)
            packed = jnp.concatenate(packed, axis=0)
            tiles = []
            for i in range(7):
                tiles.append((packed & (15 << (4 * i))).astype(F32).astype(BF))
            tiles.append(lax.shift_right_logical(packed, 28).astype(F32).astype(BF))
            halves.append(jnp.concatenate(tiles, axis=0))
        block = jnp.concatenate(halves, axis=1)
        bags[s, pl.ds(f, 1), :] = 8.0 + jnp.sum(others, axis=0, keepdims=True)
        ring[f] = block
        counts[f, :, pl.ds(b0, 256)] = block

    def early(n, carry):
        count(0, c * 4 + n)
        return carry

    def early_other(n, carry):
        count(0, 4 - c * 4 + n)
        return carry

    lax.fori_loop(0, 4, early, 0)
    pl.semaphore_wait(barrier, 19)
    trade(0).start()
    trade(1).start()
    loads[1].wait()
    loads[3].wait()
    for load in loads[4:]:
        load.start()

    def pick(n, carry):
        f = n // 16
        k = lax.rem(n, 16) * 32
        for i in range(32):
            r = touched_s[f, k + i]
            trows[f, pl.ds(k + i, 1), :] = table_v[f, pl.ds(r, 1), :]
        return carry

    lax.fori_loop(0, 64, pick, 0)
    for f in range(4):
        ttr[c * 4 + f, 0:128, :] = (trows[f] * scale).T.astype(BF)
    trade(2).start()
    traded(0).wait_recv()
    traded(1).wait_recv()
    lax.fori_loop(0, 4, early_other, 0)
    loads[4].wait()
    traded(2).wait_recv()
    for f in range(8):
        side = w_v[p * 8 + f].astype(F32).T.astype(BF)
        ttr[f, 128:256, :] = split_dot(side, ttr[f, 0:128, :], ((1,), (0,))).astype(BF)

    rows8 = lax.broadcasted_iota(jnp.int32, (8, 256), 0)

    def out_copy(s, half):
        return pltpu.make_async_remote_copy(
            src_ref=outb.at[s * 2 + half], dst_ref=slots.at[p], send_sem=s2.at[s * 2 + half],
            recv_sem=r2.at[p], device_id=(g, (pair_ahead(s) + half) * 2 + c),
            device_id_type=MESH,
        )

    def finish(s, after):
        sumsq = jnp.zeros((1, 256), F32)
        part = jnp.zeros((128, 256), F32)
        for f in range(8):
            both = split_dot(ttr[f], ring[f], ((1,), (0,)))
            pooled = both[:128].astype(BF).astype(F32)
            sumsq = sumsq + jnp.sum(pooled * pooled, axis=0, keepdims=True)
            part = part + both[128:]
            if after is not None:
                count(after, f)
        high = sumsq.astype(BF).astype(F32)
        squares = jnp.where(rows8 == 0, high, 0.0)
        squares = jnp.where(rows8 == 1, sumsq - high, squares)
        extra = jnp.concatenate([bags[s], squares], axis=0)
        for half in range(2):
            lanes_of = slice(half * 128, half * 128 + 128)
            outb[s * 2 + half, 0:128, :] = part[:, lanes_of].astype(BF)
            outb[s * 2 + half, 128:144, :] = extra[:, lanes_of].astype(BF)

    def step(s, carry):
        finish(s, s + 1)
        out_copy(s, 0).start()
        out_copy(s, 1).start()
        return carry

    lax.fori_loop(0, 7, step, 0)
    finish(7, None)
    odd = lax.rem(x, 2)
    out_copy(7, 1 - odd).start()
    slots[p] = outb[14 + odd]
    for f in range(8):
        s_acc[f] = jnp.zeros((512, 128), F32)

    pacc[...] = slots[p, 0:128, :].astype(F32)

    def from_chip(src):
        pltpu.make_async_remote_copy(
            src_ref=outb.at[0], dst_ref=slots.at[src], send_sem=s2.at[0], recv_sem=r2.at[src],
            device_id=(g, sib), device_id_type=MESH,
        ).wait_recv()
        pacc[...] += slots[src, 0:128, :].astype(F32)

    def arrive(s, carry):
        from_chip(pair_behind(s))
        from_chip(pair_behind(s) + 1)
        return carry

    lax.fori_loop(0, 7, arrive, 0)
    from_chip(p + 1 - 2 * odd)
    loads[5].wait()
    loads[6].wait()
    pre = pacc[...]
    weight = jnp.broadcast_to(w_out[...], (128, 128)).T
    gate = jax.nn.sigmoid(pre)
    logit = jnp.sum(pre * gate * weight, axis=0, keepdims=True)
    prob = jax.nn.sigmoid(logit)
    delta = gate * (1.0 + pre * (1.0 - gate)) * weight * (prob - labels[...])
    delta_low = delta.astype(BF)

    nothing = jnp.zeros((128, 128), BF)
    twice = jnp.concatenate(
        [
            jnp.concatenate([delta_low, nothing], axis=1),
            jnp.concatenate([nothing, delta_low], axis=1),
        ],
        axis=0,
    )

    def norms(q, carry):
        acc, ssq = carry
        weights = w_v[pl.ds(q * 32, 32)]
        side = jnp.concatenate(
            [weights[:16].reshape(2048, 128), weights[16:].reshape(2048, 128)], axis=1
        )
        grad = split_dot(side, twice, ((1,), (0,)))
        square = jnp.sum((grad * grad).reshape(16, 128, 256), axis=1)
        for i in range(4):
            tail = slots[q * 4 + i, 128:144, :].astype(F32)
            half = square[:, :128] if i < 2 else square[:, 128:]
            acc = acc + half[(i % 2) * 8 : (i % 2) * 8 + 8] * tail[0:8]
            ssq = ssq + tail[8:16]
        return acc, ssq

    acc, ssq = lax.fori_loop(
        0, 4, norms, (jnp.zeros((8, 128), F32), jnp.zeros((8, 128), F32))
    )
    norm_sq = jnp.sum(acc, axis=0, keepdims=True) + jnp.sum(
        ssq, axis=0, keepdims=True
    ) * jnp.sum(delta * delta, axis=0, keepdims=True)
    factor = CLIP / jnp.maximum(jnp.sqrt(norm_sq), CLIP)
    clip[p] = (factor * delta).T.astype(BF)

    def high_one(f):
        row = lax.shift_right_logical(touched_v[pl.ds(f, 1), :], 7)
        return jnp.where(high_of == row, 1.0, 0.0).astype(BF)

    def three(values):
        first = values.astype(BF)
        rest = values - first.astype(F32)
        second = rest.astype(BF)
        return first, second, (rest - second.astype(F32)).astype(BF)

    def nth(table, n):
        packed = sum(v << (4 * i) for i, v in enumerate(table))
        packed = packed - (1 << 32) if packed >= 1 << 31 else packed
        return lax.shift_right_logical(jnp.int32(packed), 4 * n) & 15

    def offsets(n):
        return nth((0, 3, 12, 15, 13, 8, 9, 11), n), nth((1, 4, 5, 7, 2, 6, 14, 10), n)

    def clip_copy(off, src):
        return pltpu.make_async_remote_copy(
            src_ref=clip.at[src], dst_ref=clip.at[src], send_sem=s3.at[off],
            recv_sem=r3.at[src], device_id=(g, ahead(off) * 2 + c), device_id_type=MESH,
        )

    def spread(n, carry):
        for off in offsets(n):
            clip_copy(off, p).start()
        return carry

    clip_copy(1, p).start()
    lax.fori_loop(1, 8, spread, 0)

    lanes = lax.broadcasted_iota(jnp.int32, (512, 128), 1)
    loads[8].wait()
    for f in range(4):
        is_high = high_one(f)
        values = jnp.concatenate(
            [accum[f : f + 1, q * 128 : (q + 1) * 128] for q in range(16)], axis=0
        )
        first, second, third = three(values)
        spread_out = split_dot(
            jnp.concatenate([is_high, is_high, is_high], axis=0),
            jnp.concatenate([first, second, third], axis=0),
            ((0,), (0,)),
        )
        found = jnp.where(lanes == low_col[f], spread_out, 0.0)
        accb[f] = jnp.broadcast_to(jnp.sum(found, axis=1, keepdims=True), (512, 128))

    def product(f, n, first=0, rows=512):
        chips = [behind(off) for off in offsets(n)]
        side = [
            counts[f, first : first + rows, pl.ds(pl.multiple_of(q * 128, 128), 128)] for q in chips
        ]
        blocks = [clip[q] for q in chips]
        return split_dot(
            jnp.concatenate(side, axis=1), jnp.concatenate(blocks, axis=0), ((1,), (0,))
        )

    def arrived(off):
        clip_copy(off, behind(off)).wait_recv()

    def drain(s, carry):
        out_copy(s, 0).wait_send()
        out_copy(s, 1).wait_send()
        return carry

    lax.fori_loop(0, 7, drain, 0)
    out_copy(7, 1 - odd).wait_send()
    for i in range(3):
        trade(i).wait_send()

    def gather(n, carry):
        for f in range(8):
            s_acc[f] += product(f, n - 1)
        for off in offsets(n):
            arrived(off)
        return carry

    arrived(1)
    lax.fori_loop(1, 8, gather, 0)

    def piece(part):
        return pl.ds(part * 256, 256)

    def half_copy(part, i):
        return pltpu.make_async_remote_copy(
            src_ref=half_send.at[i, piece(part)], dst_ref=half_recv.at[i, piece(part)],
            send_sem=s4.at[part * 4 + i], recv_sem=r4.at[part * 4 + i],
            device_id=(g, sib), device_id_type=MESH,
        )

    def sum_copy(part, i, src):
        return pltpu.make_async_remote_copy(
            src_ref=zsend.at[i, piece(part)], dst_ref=zrecv.at[src, piece(part)],
            send_sem=s5.at[part * 3 + i], recv_sem=r5.at[part * 4 + src],
            device_id=(lax.rem(g + 1 + i, 4), t), device_id_type=MESH,
        )

    def row_copy(part, i, src):
        return pltpu.make_async_remote_copy(
            src_ref=rg.at[src, piece(part)], dst_ref=rg.at[src, piece(part)],
            send_sem=s6.at[part * 3 + i], recv_sem=r6.at[part * 4 + src],
            device_id=(lax.rem(g + 1 + i, 4), t), device_id_type=MESH,
        )

    def dense_copy(i, src):
        to = lax.rem(g + 1 + i, 4)
        return pltpu.make_async_remote_copy(
            src_ref=dsend.at[to], dst_ref=dense_v.at[src], send_sem=s7.at[i],
            recv_sem=r7.at[src], device_id=(to, t), device_id_type=MESH,
        )

    def source(i):
        return lax.rem(g + 3 - i, 4)

    def rows_sum(f, part):
        rows = slice(part * 256, part * 256 + 256)
        return (s_acc[f, rows] + product(f, 7, part * 256, 256)) * scale[rows]

    for part in range(2):

        def other_features(i, carry):
            f = 4 - c * 4 + lax.rem(g + 1 + i, 4)
            half_send[i, piece(part)] = rows_sum(f, part).astype(BF)
            half_copy(part, i).start()
            return carry

        lax.fori_loop(0, 4, other_features, 0)

    for part in range(2):

        def own_features(i, carry):
            f = c * 4 + lax.rem(g + 1 + i, 4)
            total = rows_sum(f, part)
            half_copy(part, i).wait_recv()
            total = total + half_recv[i, piece(part)].astype(F32)
            s_acc[f, piece(part)] = total

            @pl.when(i < 3)
            def _():
                zsend[i, piece(part)] = total.astype(BF)
                sum_copy(part, i, g).start()

            return carry

        lax.fori_loop(0, 4, own_features, 0)

    def drain_far(off, carry):
        clip_copy(off, p).wait_send()
        return carry

    lax.fori_loop(1, 16, drain_far, 0)
    for part in range(2):
        for i in range(4):
            half_copy(part, i).wait_send()

    side = trows[g].T.astype(BF)
    dense_sum = jnp.zeros((128, 128), F32)
    for part in range(2):
        summed = s_acc[c * 4 + g, piece(part)]
        for i in range(3):
            sum_copy(part, i, source(i)).wait_recv()
            summed = summed + zrecv[source(i), piece(part)].astype(F32)
        low = summed.astype(BF)
        rg[g, piece(part)] = split_dot(low, w_v[t * 4 + g], ((1,), (1,))).astype(BF)
        for i in range(3):
            row_copy(part, i, g).start()
        dense_sum = dense_sum + split_dot(
            side[:, part * 256 : part * 256 + 256], low, ((1,), (0,))
        )
    dsend[...] = dense_sum.reshape(4, 32, 128)
    for i in range(3):
        dense_copy(i, g).start()
    dense_v[g] = dsend[g]

    def rows_save(f, part):
        return pltpu.make_async_copy(
            rows_v.at[f, piece(part)], rows_out.at[f, piece(part)], out_sem.at[part * 4 + f]
        )

    def update(f, part):
        rows = slice(part * 256, part * 256 + 256)
        listed = rg[f, rows].astype(F32) + noise[f, rows]
        mean = jnp.sum(listed * listed, axis=1, keepdims=True) * (1.0 / 128.0)
        new_acc = accb[f, rows] + mean
        rows_v[f, rows] = trows[f, rows] - LEARN * listed / jnp.sqrt(new_acc)
        rows_save(f, part).start()
        is_high = high_one(f)[:, rows]
        added = jnp.zeros((16, 128), F32)
        for one in three(jnp.where(lanes[rows] == low_col[f, rows], mean, 0.0)):
            added = added + split_dot(is_high, one, ((1,), (0,)))
        macc_v[f] = added if part == 0 else macc_v[f] + added

    loads[7].wait()
    for part in range(2):
        update(g, part)
        for i in range(3):
            row_copy(part, i, source(i)).wait_recv()
            update(source(i), part)
    for i in range(3):
        dense_copy(i, source(i)).wait_recv()
    saves = [
        pltpu.make_async_copy(macc_v, macc_out, out_sem.at[8]),
        pltpu.make_async_copy(dense_v, dense_out, out_sem.at[9]),
    ]
    for save in saves:
        save.start()
    for part in range(2):
        for i in range(3):
            sum_copy(part, i, g).wait_send()
            row_copy(part, i, g).wait_send()
    for i in range(3):
        dense_copy(i, g).wait_send()
    for part in range(2):
        for f in range(4):
            rows_save(f, part).wait()
    for save in saves:
        save.wait()


def write_rows(
    touched_h, accum_h, macc_h, dense_h, noise_h, table_h, rows_h,
    table_out, accum_out, dense_out,
    touched_s, accum, macc, dense, noise, block, rows, sem, in_sem, rows_sem, out_sem,
):
    def load(f):
        return pltpu.make_async_copy(table_h.at[f], block.at[f], in_sem.at[f])

    def load_rows(f):
        return pltpu.make_async_copy(rows_h.at[f], rows.at[f], rows_sem.at[f])

    def save(f):
        return pltpu.make_async_copy(block.at[f], table_out.at[f], out_sem.at[f])

    load(0).start()
    load_rows(0).start()
    small = [
        pltpu.make_async_copy(source, target, sem.at[i])
        for i, (source, target) in enumerate(
            (
                (touched_h, touched_s), (accum_h, accum), (macc_h, macc),
                (dense_h, dense), (noise_h, noise),
            )
        )
    ]
    for copy in small:
        copy.start()
    for f in range(1, 4):
        load(f).start()
        load_rows(f).start()
    for copy in small:
        copy.wait()
    dense[...] += noise[...]
    save_dense = pltpu.make_async_copy(dense, dense_out, sem.at[5])
    save_dense.start()
    for f in range(4):
        for q in range(16):
            lanes = slice(q * 128, (q + 1) * 128)
            accum[f : f + 1, lanes] += macc[f, q : q + 1, :]
    save_accum = pltpu.make_async_copy(accum, accum_out, sem.at[6])
    save_accum.start()
    for f in range(4):
        load(f).wait()
        load_rows(f).wait()

        def put(n, carry):
            k = pl.multiple_of(n * 64, 64)
            for i in range(64):
                block[f, pl.ds(touched_s[f, k + i], 1), :] = rows[f, pl.ds(k + i, 1), :]
            return carry

        lax.fori_loop(0, 8, put, 0)
        save(f).start()
    save_dense.wait()
    save_accum.wait()
    for f in range(4):
        save(f).wait()


def body(table, accum, w_hidden, w_out, ids, labels, touched, row_noise, dense_noise):
    hbm = pl.BlockSpec(memory_space=pl.ANY)
    dma = pltpu.SemaphoreType.DMA
    rows, macc, dense = pl.pallas_call(
        core,
        out_shape=(
            jax.ShapeDtypeStruct((4, 512, 128), F32),
            jax.ShapeDtypeStruct((4, 16, 128), F32),
            jax.ShapeDtypeStruct((4, 32, 128), F32),
        ),
        in_specs=[hbm] * 8,
        out_specs=(hbm, hbm, hbm),
        scratch_shapes=[
            pltpu.SMEM((4, 512), jnp.int32),
            pltpu.VMEM((4, 512), jnp.int32),
            pltpu.VMEM((4, 2048), F32),
            pltpu.VMEM((4, 8, 4096), jnp.int32),
            pltpu.VMEM((1, 128), F32),
            pltpu.VMEM((1, 128), F32),
            pltpu.VMEM((4, 512, 128), F32),
            pltpu.VMEM((4, 512, 128), F32),
            pltpu.VMEM((4, 16, 128), F32),
            pltpu.VMEM((4, 32, 128), F32),
            pltpu.VMEM((4, 2048, 128), F32),
            pltpu.VMEM((128, 128, 128), BF),
            pltpu.VMEM((4, 512, 128), F32),
            pltpu.VMEM((8, 256, 512), BF),
            pltpu.VMEM((8, 16, 128), jnp.int32),
            pltpu.VMEM((4, 512, 128), jnp.int32),
            pltpu.VMEM((8, 512, 2048), BF),
            pltpu.VMEM((8, 512, 256), BF),
            pltpu.VMEM((8, 8, 256), F32),
            pltpu.VMEM((8, 8, 2048), jnp.int32),
            pltpu.VMEM((4, 8, 2048), jnp.int32),
            pltpu.VMEM((16, 144, 128), BF),
            pltpu.VMEM((16, 144, 128), BF),
            pltpu.VMEM((128, 128), F32),
            pltpu.VMEM((16, 128, 128), BF),
            pltpu.VMEM((4, 512, 128), F32),
            pltpu.VMEM((8, 512, 128), F32),
            pltpu.VMEM((4, 512, 128), BF),
            pltpu.VMEM((4, 512, 128), BF),
            pltpu.VMEM((3, 512, 128), BF),
            pltpu.VMEM((4, 512, 128), BF),
            pltpu.VMEM((4, 512, 128), BF),
            pltpu.VMEM((4, 32, 128), F32),
            dma((9,)),
            dma((3,)), dma((3,)), dma((16,)), dma((16,)), dma((16,)), dma((16,)),
            dma((8,)), dma((8,)),
            dma((6,)), dma((8,)), dma((6,)), dma((8,)), dma((3,)), dma((4,)),
            dma((10,)),
        ],
        compiler_params=pltpu.CompilerParams(
            collective_id=0, has_side_effects=True, vmem_limit_bytes=56 * 1024 * 1024
        ),
        cost_estimate=pl.CostEstimate(
            flops=6 * 10**9, bytes_accessed=12 * 2**20, transcendentals=10**5
        ),
        name="step",
    )(
        touched, accum, ids, w_out.reshape(1, 128), labels.reshape(1, 128),
        row_noise, table, w_hidden,
    )
    return pl.pallas_call(
        write_rows,
        out_shape=(
            jax.ShapeDtypeStruct((4, 2048, 128), F32),
            jax.ShapeDtypeStruct((4, 2048), F32),
            jax.ShapeDtypeStruct((4, 32, 128), F32),
        ),
        in_specs=[hbm] * 7,
        out_specs=(hbm, hbm, hbm),
        scratch_shapes=[
            pltpu.SMEM((4, 512), jnp.int32),
            pltpu.VMEM((4, 2048), F32),
            pltpu.VMEM((4, 16, 128), F32),
            pltpu.VMEM((4, 32, 128), F32),
            pltpu.VMEM((4, 32, 128), F32),
            pltpu.VMEM((4, 2048, 128), F32),
            pltpu.VMEM((4, 512, 128), F32),
            dma((7,)), dma((4,)), dma((4,)), dma((4,)),
        ],
        compiler_params=pltpu.CompilerParams(vmem_limit_bytes=60 * 1024 * 1024),
        name="write_rows",
    )(touched, accum, macc, dense, dense_noise, table, rows)


def solution(mesh):
    in_specs = (
        P("table", None, None),
        P("table", None),
        P(),
        P(),
        P("table", None, "group"),
        P(("group", "table")),
        P("table", None),
        P("table", None, None),
        P("table", "group", None),
    )
    out_specs = (P("table", None, None), P("table", None), P("table", "group", None))
    return jax.shard_map(body, mesh=mesh, in_specs=in_specs, out_specs=out_specs, check_vma=False)
```

```python
import functools

import jax
import jax.numpy as jnp
from jax import lax
from jax.experimental import pallas as pl
from jax.experimental.pallas import tpu as pltpu
from jax.sharding import PartitionSpec as P

CLIP = 1.0
LEARN = 0.05
MESH = pl.DeviceIdType.MESH
BF = jnp.bfloat16
F32 = jnp.float32


def scale_of(i):
    return 16.0**i if i < 7 else 1.0


def split_dot(a, b, dims):
    return lax.dot_general(a, b, (dims, ((), ())), preferred_element_type=F32)


def core(
    touched_h, accum_h, ids_h, w_out_h, labels_h, noise_h, table_h, w_h,
    rows_out, macc_out, dense_out,
    touched_s, touched_v, accum, ids, w_out, labels, noise, rows_v, macc_v, dense_v,
    table_v, w_v, trows, ttr, smap, low_col, counts, ring, bags, both_ids, send_ids,
    outb, slots, pacc, clip, accb, s_acc, half_send, half_recv, zsend, zrecv, rg, dsend,
    load_sem, s1, r1, s2, r2, s3, r3, s4, r4, s5, r5, s6, r6, s7, r7, out_sem,
):
    g = lax.axis_index("group")
    t = lax.axis_index("table")
    c = lax.rem(t, 2)
    p = t // 2
    y = p // 4
    x = lax.rem(p, 4)
    sib = t + 1 - 2 * c

    def ahead(off):
        return lax.rem(y + off // 4, 4) * 4 + lax.rem(x + lax.rem(off, 4), 4)

    def behind(off):
        return lax.rem(y + 4 - off // 4, 4) * 4 + lax.rem(x + 4 - lax.rem(off, 4), 4)

    loads = [
        pltpu.make_async_copy(source, target, load_sem.at[i])
        for i, (source, target) in enumerate(
            (
                (touched_h, touched_v), (touched_h.at[0], touched_s.at[pl.ds(0, 512)]),
                (ids_h, ids), (table_h, table_v),
                (w_h, w_v), (w_out_h, w_out), (labels_h, labels), (noise_h, noise),
                (accum_h, accum),
                (touched_h.at[1], touched_s.at[pl.ds(512, 512)]),
                (touched_h.at[2], touched_s.at[pl.ds(1024, 512)]),
                (touched_h.at[3], touched_s.at[pl.ds(1536, 512)]),
            )
        )
    ]
    for load in loads[:4] + loads[9:]:
        load.start()

    barrier = pltpu.get_barrier_semaphore()

    def greet(off, carry):
        pl.semaphore_signal(
            barrier, inc=1, device_id=(g, ahead(off) * 2 + c), device_id_type=MESH
        )
        return carry

    lax.fori_loop(1, 16, greet, 0)
    pl.semaphore_signal(barrier, inc=1, device_id=(g, sib), device_id_type=MESH)
    for i in range(1, 4):
        pl.semaphore_signal(
            barrier, inc=1, device_id=(lax.rem(g + i, 4), t), device_id_type=MESH
        )

    loads[0].wait()
    high_of = lax.broadcasted_iota(jnp.int32, (16, 512), 0)
    low_of = lax.broadcasted_iota(jnp.int32, (128, 512), 0)
    lane = lax.broadcasted_iota(jnp.int32, (1, 512), 1)
    for f in range(4):
        row = touched_v[f : f + 1, :]
        row_low = row & 127
        is_high = high_of == lax.shift_right_logical(row, 7)
        is_low = jnp.where(low_of == row_low, 1.0, 0.0).astype(BF)
        number = jnp.concatenate(
            [
                jnp.where(is_high, lax.shift_right_logical(lane, 4), 0),
                jnp.where(is_high, lane & 15, 0),
            ],
            axis=0,
        )
        pair = split_dot(number.astype(F32).astype(BF), is_low, ((1,), (1,)))
        place = (pair[:16] * 16.0 + pair[16:]).astype(jnp.int32)
        for j in range(6):
            word = place[3 * j : 3 * j + 1]
            for i in range(1, min(3, 16 - 3 * j)):
                word = word | lax.shift_left(place[3 * j + i : 3 * j + i + 1], 9 * i)
            smap[c * 4 + f, j : j + 1, :] = word
        smap[c * 4 + f, 6:8, :] = jnp.zeros((2, 128), jnp.int32)
        for q in range(4):
            wide = jnp.broadcast_to(row_low[:, q * 128 : (q + 1) * 128], (128, 128))
            low_col[f, q * 128 : (q + 1) * 128, :] = wide.T

    loads[2].wait()
    for f in range(4):
        for q in range(16):
            to = slice(q * 128, q * 128 + 128)
            ours = pl.ds(pl.multiple_of(q * 256 + c * 128, 128), 128)
            theirs = pl.ds(pl.multiple_of(q * 256 + 128 - c * 128, 128), 128)
            both_ids[c * 4 + f, :, to] = ids[f, :, ours]
            send_ids[f, :, to] = ids[f, :, theirs]

    own_part = pl.ds(c * 4, 4)

    def trade(i):
        source, target = (
            (send_ids, both_ids.at[own_part]),
            (smap.at[own_part], smap.at[own_part]),
            (ttr.at[own_part, pl.ds(0, 128)], ttr.at[own_part, pl.ds(0, 128)]),
        )[i]
        return pltpu.make_async_remote_copy(
            src_ref=source, dst_ref=target, send_sem=s1.at[i], recv_sem=r1.at[i],
            device_id=(g, sib), device_id_type=MESH,
        )

    def traded(i):
        other = pl.ds(4 - c * 4, 4)
        source, target = (
            (send_ids, both_ids.at[other]),
            (smap.at[other], smap.at[other]),
            (ttr.at[other, pl.ds(0, 128)], ttr.at[other, pl.ds(0, 128)]),
        )[i]
        return pltpu.make_async_remote_copy(
            src_ref=source, dst_ref=target, send_sem=s1.at[i], recv_sem=r1.at[i],
            device_id=(g, sib), device_id_type=MESH,
        )

    def pair_ahead(s):
        off = 7 - s
        return lax.rem(y + off // 2, 4) * 4 + lax.rem(x // 2 + lax.rem(off, 2), 2) * 2

    def pair_behind(s):
        off = 7 - s
        return lax.rem(y + 4 - off // 2, 4) * 4 + lax.rem(x // 2 + lax.rem(off, 2), 2) * 2

    sublane = lax.broadcasted_iota(jnp.int32, (8, 128), 0)
    scale = jnp.concatenate([jnp.full((64, 128), 1.0 / scale_of(i), F32) for i in range(8)], axis=0)

    def count(s, f):
        b0 = pl.multiple_of(pair_ahead(s) * 128, 256)
        bag = both_ids[f, :, pl.ds(b0, 256)]
        others = jnp.zeros((8, 256), F32)
        for d in range(1, 5):
            others = others + jnp.where(bag == pltpu.roll(bag, d, 0), 1.0 if d == 4 else 2.0, 0.0)
        slots_of = []
        for half in range(2):
            part = bag[:, half * 128 : half * 128 + 128]
            high = lax.shift_right_logical(part, 7)
            low = part & 127
            third = lax.shift_right_logical(high * 11, 5)
            found = jnp.zeros((8, 128), jnp.int32)
            for q in range(6):
                row = jnp.broadcast_to(smap[f, q : q + 1, :], (8, 128))
                found = jnp.where(third == q, jnp.take_along_axis(row, low, axis=1), found)
            slots_of.append(lax.shift_right_logical(found, (high - third * 3) * 9) & 511)
        halves = []
        for slot in slots_of:
            word = slot & 63
            digit = lax.shift_left(
                jnp.ones((8, 128), jnp.int32), lax.shift_right_logical(slot, 6) * 4
            )
            packed = [jnp.zeros((8, 128), jnp.int32) for _ in range(8)]
            for h in range(8):
                place = jnp.broadcast_to(word[h : h + 1], (8, 128)) - sublane
                value = jnp.broadcast_to(digit[h : h + 1], (8, 128))
                for v in range(8):
                    packed[v] = packed[v] + jnp.where(place == 8 * v, value, 0)
            packed = jnp.concatenate(packed, axis=0)
            tiles = []
            for i in range(7):
                tiles.append((packed & (15 << (4 * i))).astype(F32).astype(BF))
            tiles.append(lax.shift_right_logical(packed, 28).astype(F32).astype(BF))
            halves.append(jnp.concatenate(tiles, axis=0))
        block = jnp.concatenate(halves, axis=1)
        bags[s, pl.ds(f, 1), :] = 8.0 + jnp.sum(others, axis=0, keepdims=True)
        ring[f] = block
        counts[f, :, pl.ds(b0, 256)] = block

    def early(n, carry):
        count(0, c * 4 + n)
        return carry

    def early_other(n, carry):
        count(0, 4 - c * 4 + n)
        return carry

    lax.fori_loop(0, 4, early, 0)
    pl.semaphore_wait(barrier, 19)
    trade(0).start()
    trade(1).start()
    loads[1].wait()
    loads[3].wait()
    for load in loads[9:]:
        load.wait()
    for load in loads[4:9]:
        load.start()

    for f in range(4):

        def pick(n, carry):
            k = pl.multiple_of(n * 32, 32)
            for i in range(32):
                r = touched_s[f * 512 + k + i]
                trows[f, pl.ds(k + i, 1), :] = table_v[f, pl.ds(r, 1), :]
            return carry

        lax.fori_loop(0, 16, pick, 0)
    for f in range(4):
        ttr[c * 4 + f, 0:128, :] = (trows[f] * scale).T.astype(BF)
    trade(2).start()
    loads[4].wait()

    def project(f):
        side = w_v[p * 8 + f].astype(F32).T.astype(BF)
        ttr[f, 128:256, :] = split_dot(side, ttr[f, 0:128, :], ((1,), (0,))).astype(BF)

    traded(0).wait_recv()
    traded(1).wait_recv()
    lax.fori_loop(0, 4, early_other, 0)
    traded(2).wait_recv()
    for f in range(4):
        project(f)
        project(4 + f)

    rows8 = lax.broadcasted_iota(jnp.int32, (8, 256), 0)

    def out_copy(s, half):
        return pltpu.make_async_remote_copy(
            src_ref=outb.at[s * 2 + half], dst_ref=slots.at[p], send_sem=s2.at[s * 2 + half],
            recv_sem=r2.at[p], device_id=(g, (pair_ahead(s) + half) * 2 + c),
            device_id_type=MESH,
        )

    def finish(s, after):
        sumsq = jnp.zeros((1, 256), F32)
        part = jnp.zeros((128, 256), F32)
        for f in range(8):
            both = split_dot(ttr[f], ring[f], ((1,), (0,)))
            pooled = both[:128].astype(BF).astype(F32)
            sumsq = sumsq + jnp.sum(pooled * pooled, axis=0, keepdims=True)
            part = part + both[128:]
            if after is not None:
                count(after, f)
        high = sumsq.astype(BF).astype(F32)
        squares = jnp.where(rows8 == 0, high, 0.0)
        squares = jnp.where(rows8 == 1, sumsq - high, squares)
        extra = jnp.concatenate([bags[s], squares], axis=0)
        for half in range(2):
            lanes_of = slice(half * 128, half * 128 + 128)
            outb[s * 2 + half, 0:128, :] = part[:, lanes_of].astype(BF)
            outb[s * 2 + half, 128:144, :] = extra[:, lanes_of].astype(BF)

    def step(s, carry):
        finish(s, s + 1)
        out_copy(s, 0).start()
        out_copy(s, 1).start()
        return carry

    lax.fori_loop(0, 7, step, 0)
    finish(7, None)
    odd = lax.rem(x, 2)
    out_copy(7, 1 - odd).start()
    slots[p] = outb[14 + odd]
    for f in range(8):
        s_acc[f] = jnp.zeros((512, 128), F32)

    pacc[...] = slots[p, 0:128, :].astype(F32)

    def from_chip(src):
        pltpu.make_async_remote_copy(
            src_ref=outb.at[0], dst_ref=slots.at[src], send_sem=s2.at[0], recv_sem=r2.at[src],
            device_id=(g, sib), device_id_type=MESH,
        ).wait_recv()
        pacc[...] += slots[src, 0:128, :].astype(F32)

    def arrive(s, carry):
        from_chip(pair_behind(s))
        from_chip(pair_behind(s) + 1)
        return carry

    lax.fori_loop(0, 7, arrive, 0)
    from_chip(p + 1 - 2 * odd)
    loads[5].wait()
    loads[6].wait()
    pre = pacc[...]
    weight = jnp.broadcast_to(w_out[...], (128, 128)).T
    gate = jax.nn.sigmoid(pre)
    logit = jnp.sum(pre * gate * weight, axis=0, keepdims=True)
    prob = jax.nn.sigmoid(logit)
    delta = gate * (1.0 + pre * (1.0 - gate)) * weight * (prob - labels[...])
    delta_low = delta.astype(BF)

    nothing = jnp.zeros((128, 128), BF)
    twice = jnp.concatenate(
        [
            jnp.concatenate([delta_low, nothing], axis=1),
            jnp.concatenate([nothing, delta_low], axis=1),
        ],
        axis=0,
    )

    def norms(q, carry):
        acc, ssq = carry
        weights = w_v[pl.ds(q * 32, 32)]
        side = jnp.concatenate(
            [weights[:16].reshape(2048, 128), weights[16:].reshape(2048, 128)], axis=1
        )
        grad = split_dot(side, twice, ((1,), (0,)))
        square = jnp.sum((grad * grad).reshape(16, 128, 256), axis=1)
        for i in range(4):
            tail = slots[q * 4 + i, 128:144, :].astype(F32)
            half = square[:, :128] if i < 2 else square[:, 128:]
            acc = acc + half[(i % 2) * 8 : (i % 2) * 8 + 8] * tail[0:8]
            ssq = ssq + tail[8:16]
        return acc, ssq

    acc, ssq = lax.fori_loop(
        0, 4, norms, (jnp.zeros((8, 128), F32), jnp.zeros((8, 128), F32))
    )
    norm_sq = jnp.sum(acc, axis=0, keepdims=True) + jnp.sum(
        ssq, axis=0, keepdims=True
    ) * jnp.sum(delta * delta, axis=0, keepdims=True)
    factor = CLIP / jnp.maximum(jnp.sqrt(norm_sq), CLIP)
    clip[p] = (factor * delta).T.astype(BF)

    def high_one(f):
        row = lax.shift_right_logical(touched_v[pl.ds(f, 1), :], 7)
        return jnp.where(high_of == row, 1.0, 0.0).astype(BF)

    def three(values):
        first = values.astype(BF)
        rest = values - first.astype(F32)
        second = rest.astype(BF)
        return first, second, (rest - second.astype(F32)).astype(BF)

    def nth(table, n):
        packed = sum(v << (4 * i) for i, v in enumerate(table))
        packed = packed - (1 << 32) if packed >= 1 << 31 else packed
        return lax.shift_right_logical(jnp.int32(packed), 4 * n) & 15

    def offsets(n):
        return nth((0, 3, 12, 15, 13, 8, 9, 11), n), nth((1, 4, 5, 7, 2, 6, 14, 10), n)

    def clip_copy(off, src):
        return pltpu.make_async_remote_copy(
            src_ref=clip.at[src], dst_ref=clip.at[src], send_sem=s3.at[off],
            recv_sem=r3.at[src], device_id=(g, ahead(off) * 2 + c), device_id_type=MESH,
        )

    def spread(n, carry):
        for off in offsets(n):
            clip_copy(off, p).start()
        return carry

    clip_copy(1, p).start()
    lax.fori_loop(1, 8, spread, 0)

    lanes = lax.broadcasted_iota(jnp.int32, (512, 128), 1)
    loads[8].wait()
    for f in range(4):
        is_high = high_one(f)
        values = jnp.concatenate(
            [accum[f : f + 1, q * 128 : (q + 1) * 128] for q in range(16)], axis=0
        )
        first, second, third = three(values)
        spread_out = split_dot(
            jnp.concatenate([is_high, is_high, is_high], axis=0),
            jnp.concatenate([first, second, third], axis=0),
            ((0,), (0,)),
        )
        found = jnp.where(lanes == low_col[f], spread_out, 0.0)
        accb[f] = jnp.broadcast_to(jnp.sum(found, axis=1, keepdims=True), (512, 128))

    def product(f, n, first=0, rows=512):
        chips = [behind(off) for off in offsets(n)]
        side = [
            counts[f, first : first + rows, pl.ds(pl.multiple_of(q * 128, 128), 128)] for q in chips
        ]
        blocks = [clip[q] for q in chips]
        return split_dot(
            jnp.concatenate(side, axis=1), jnp.concatenate(blocks, axis=0), ((1,), (0,))
        )

    def arrived(off):
        clip_copy(off, behind(off)).wait_recv()

    def drain(s, carry):
        out_copy(s, 0).wait_send()
        out_copy(s, 1).wait_send()
        return carry

    lax.fori_loop(0, 7, drain, 0)
    out_copy(7, 1 - odd).wait_send()
    for i in range(3):
        trade(i).wait_send()

    def gather(n, carry):
        for f in range(8):
            s_acc[f] += product(f, n - 1)
        for off in offsets(n):
            arrived(off)
        return carry

    arrived(1)
    lax.fori_loop(1, 8, gather, 0)

    def piece(part):
        return pl.ds(part * 256, 256)

    def half_copy(part, i):
        return pltpu.make_async_remote_copy(
            src_ref=half_send.at[i, piece(part)], dst_ref=half_recv.at[i, piece(part)],
            send_sem=s4.at[part * 4 + i], recv_sem=r4.at[part * 4 + i],
            device_id=(g, sib), device_id_type=MESH,
        )

    def sum_copy(part, i, src):
        return pltpu.make_async_remote_copy(
            src_ref=zsend.at[i, piece(part)], dst_ref=zrecv.at[src, piece(part)],
            send_sem=s5.at[part * 3 + i], recv_sem=r5.at[part * 4 + src],
            device_id=(lax.rem(g + 1 + i, 4), t), device_id_type=MESH,
        )

    def row_copy(part, i, src):
        return pltpu.make_async_remote_copy(
            src_ref=rg.at[src, piece(part)], dst_ref=rg.at[src, piece(part)],
            send_sem=s6.at[part * 3 + i], recv_sem=r6.at[part * 4 + src],
            device_id=(lax.rem(g + 1 + i, 4), t), device_id_type=MESH,
        )

    def dense_copy(i, src):
        to = lax.rem(g + 1 + i, 4)
        return pltpu.make_async_remote_copy(
            src_ref=dsend.at[to], dst_ref=dense_v.at[src], send_sem=s7.at[i],
            recv_sem=r7.at[src], device_id=(to, t), device_id_type=MESH,
        )

    def source(i):
        return lax.rem(g + 3 - i, 4)

    def rows_sum(f, part):
        rows = slice(part * 256, part * 256 + 256)
        return (s_acc[f, rows] + product(f, 7, part * 256, 256)) * scale[rows]

    for part in range(2):

        def other_features(i, carry):
            f = 4 - c * 4 + lax.rem(g + 1 + i, 4)
            half_send[i, piece(part)] = rows_sum(f, part).astype(BF)
            half_copy(part, i).start()
            return carry

        lax.fori_loop(0, 4, other_features, 0)

    for part in range(2):

        def own_features(i, carry):
            f = c * 4 + lax.rem(g + 1 + i, 4)
            total = rows_sum(f, part)
            half_copy(part, i).wait_recv()
            total = total + half_recv[i, piece(part)].astype(F32)
            s_acc[f, piece(part)] = total

            @pl.when(i < 3)
            def _():
                zsend[i, piece(part)] = total.astype(BF)
                sum_copy(part, i, g).start()

            return carry

        lax.fori_loop(0, 4, own_features, 0)

    def drain_far(off, carry):
        clip_copy(off, p).wait_send()
        return carry

    lax.fori_loop(1, 16, drain_far, 0)
    for part in range(2):
        for i in range(4):
            half_copy(part, i).wait_send()

    side = trows[g].T.astype(BF)
    dense_sum = jnp.zeros((128, 128), F32)
    for part in range(2):
        summed = s_acc[c * 4 + g, piece(part)]
        for i in range(3):
            sum_copy(part, i, source(i)).wait_recv()
            summed = summed + zrecv[source(i), piece(part)].astype(F32)
        low = summed.astype(BF)
        rg[g, piece(part)] = split_dot(low, w_v[t * 4 + g], ((1,), (1,))).astype(BF)
        for i in range(3):
            row_copy(part, i, g).start()
        dense_sum = dense_sum + split_dot(
            side[:, part * 256 : part * 256 + 256], low, ((1,), (0,))
        )
    dsend[...] = dense_sum.reshape(4, 32, 128)
    for i in range(3):
        dense_copy(i, g).start()
    dense_v[g] = dsend[g]

    def rows_save(f, part):
        return pltpu.make_async_copy(
            rows_v.at[f, piece(part)], rows_out.at[f, piece(part)], out_sem.at[part * 4 + f]
        )

    def update(f, part):
        rows = slice(part * 256, part * 256 + 256)
        listed = rg[f, rows].astype(F32) + noise[f, rows]
        mean = jnp.sum(listed * listed, axis=1, keepdims=True) * (1.0 / 128.0)
        new_acc = accb[f, rows] + mean
        rows_v[f, rows] = trows[f, rows] - LEARN * listed / jnp.sqrt(new_acc)
        rows_save(f, part).start()
        is_high = high_one(f)[:, rows]
        added = jnp.zeros((16, 128), F32)
        for one in three(jnp.where(lanes[rows] == low_col[f, rows], mean, 0.0)):
            added = added + split_dot(is_high, one, ((1,), (0,)))
        macc_v[f] = added if part == 0 else macc_v[f] + added

    loads[7].wait()
    for part in range(2):
        update(g, part)
        for i in range(3):
            row_copy(part, i, source(i)).wait_recv()
            update(source(i), part)
    for i in range(3):
        dense_copy(i, source(i)).wait_recv()
    saves = [
        pltpu.make_async_copy(macc_v, macc_out, out_sem.at[8]),
        pltpu.make_async_copy(dense_v, dense_out, out_sem.at[9]),
    ]
    for save in saves:
        save.start()
    for part in range(2):
        for i in range(3):
            sum_copy(part, i, g).wait_send()
            row_copy(part, i, g).wait_send()
    for i in range(3):
        dense_copy(i, g).wait_send()
    for part in range(2):
        for f in range(4):
            rows_save(f, part).wait()
    for save in saves:
        save.wait()


def write_rows(
    touched_h, accum_h, macc_h, dense_h, noise_h, table_h, rows_h,
    table_out, accum_out, dense_out,
    touched_s, accum, macc, dense, noise, block, rows, sem, in_sem, rows_sem, out_sem,
):
    def load(f):
        return pltpu.make_async_copy(table_h.at[f], block.at[f], in_sem.at[f])

    def load_rows(f):
        return pltpu.make_async_copy(rows_h.at[f], rows.at[f], rows_sem.at[f])

    def save(f):
        return pltpu.make_async_copy(block.at[f], table_out.at[f], out_sem.at[f])

    load(0).start()
    load_rows(0).start()
    small = [
        pltpu.make_async_copy(source, target, sem.at[i])
        for i, (source, target) in enumerate(
            (
                (touched_h.at[0], touched_s.at[pl.ds(0, 512)]),
                (touched_h.at[1], touched_s.at[pl.ds(512, 512)]),
                (touched_h.at[2], touched_s.at[pl.ds(1024, 512)]),
                (touched_h.at[3], touched_s.at[pl.ds(1536, 512)]),
                (accum_h, accum), (macc_h, macc),
                (dense_h, dense), (noise_h, noise),
            )
        )
    ]
    for copy in small:
        copy.start()
    for f in range(1, 4):
        load(f).start()
        load_rows(f).start()
    for copy in small[:4]:
        copy.wait()
    for f in range(4):
        load(f).wait()
        load_rows(f).wait()

        def put(n, carry):
            k = pl.multiple_of(n * 64, 64)
            for i in range(64):
                block[f, pl.ds(touched_s[f * 512 + k + i], 1), :] = rows[f, pl.ds(k + i, 1), :]
            return carry

        lax.fori_loop(0, 8, put, 0)
        save(f).start()
    for copy in small[4:]:
        copy.wait()
    dense[...] += noise[...]
    save_dense = pltpu.make_async_copy(dense, dense_out, sem.at[8])
    save_dense.start()
    for f in range(4):
        for q in range(16):
            lanes = slice(q * 128, (q + 1) * 128)
            accum[f : f + 1, lanes] += macc[f, q : q + 1, :]
    save_accum = pltpu.make_async_copy(accum, accum_out, sem.at[9])
    save_accum.start()
    save_dense.wait()
    save_accum.wait()
    for f in range(4):
        save(f).wait()


def body(table, accum, w_hidden, w_out, ids, labels, touched, row_noise, dense_noise):
    hbm = pl.BlockSpec(memory_space=pl.ANY)
    dma = pltpu.SemaphoreType.DMA
    rows, macc, dense = pl.pallas_call(
        core,
        out_shape=(
            jax.ShapeDtypeStruct((4, 512, 128), F32),
            jax.ShapeDtypeStruct((4, 16, 128), F32),
            jax.ShapeDtypeStruct((4, 32, 128), F32),
        ),
        in_specs=[hbm] * 8,
        out_specs=(hbm, hbm, hbm),
        scratch_shapes=[
            pltpu.SMEM((2048,), jnp.int32),
            pltpu.VMEM((4, 512), jnp.int32),
            pltpu.VMEM((4, 2048), F32),
            pltpu.VMEM((4, 8, 4096), jnp.int32),
            pltpu.VMEM((1, 128), F32),
            pltpu.VMEM((1, 128), F32),
            pltpu.VMEM((4, 512, 128), F32),
            pltpu.VMEM((4, 512, 128), F32),
            pltpu.VMEM((4, 16, 128), F32),
            pltpu.VMEM((4, 32, 128), F32),
            pltpu.VMEM((4, 2048, 128), F32),
            pltpu.VMEM((128, 128, 128), BF),
            pltpu.VMEM((4, 512, 128), F32),
            pltpu.VMEM((8, 256, 512), BF),
            pltpu.VMEM((8, 8, 128), jnp.int32),
            pltpu.VMEM((4, 512, 128), jnp.int32),
            pltpu.VMEM((8, 512, 2048), BF),
            pltpu.VMEM((8, 512, 256), BF),
            pltpu.VMEM((8, 8, 256), F32),
            pltpu.VMEM((8, 8, 2048), jnp.int32),
            pltpu.VMEM((4, 8, 2048), jnp.int32),
            pltpu.VMEM((16, 144, 128), BF),
            pltpu.VMEM((16, 144, 128), BF),
            pltpu.VMEM((128, 128), F32),
            pltpu.VMEM((16, 128, 128), BF),
            pltpu.VMEM((4, 512, 128), F32),
            pltpu.VMEM((8, 512, 128), F32),
            pltpu.VMEM((4, 512, 128), BF),
            pltpu.VMEM((4, 512, 128), BF),
            pltpu.VMEM((3, 512, 128), BF),
            pltpu.VMEM((4, 512, 128), BF),
            pltpu.VMEM((4, 512, 128), BF),
            pltpu.VMEM((4, 32, 128), F32),
            dma((12,)),
            dma((3,)), dma((3,)), dma((16,)), dma((16,)), dma((16,)), dma((16,)),
            dma((8,)), dma((8,)),
            dma((6,)), dma((8,)), dma((6,)), dma((8,)), dma((3,)), dma((4,)),
            dma((10,)),
        ],
        compiler_params=pltpu.CompilerParams(
            collective_id=0, has_side_effects=True, vmem_limit_bytes=56 * 1024 * 1024
        ),
        cost_estimate=pl.CostEstimate(
            flops=6 * 10**9, bytes_accessed=12 * 2**20, transcendentals=10**5
        ),
        name="step",
    )(
        touched, accum, ids, w_out.reshape(1, 128), labels.reshape(1, 128),
        row_noise, table, w_hidden,
    )
    return pl.pallas_call(
        write_rows,
        out_shape=(
            jax.ShapeDtypeStruct((4, 2048, 128), F32),
            jax.ShapeDtypeStruct((4, 2048), F32),
            jax.ShapeDtypeStruct((4, 32, 128), F32),
        ),
        in_specs=[hbm] * 7,
        out_specs=(hbm, hbm, hbm),
        scratch_shapes=[
            pltpu.SMEM((2048,), jnp.int32),
            pltpu.VMEM((4, 2048), F32),
            pltpu.VMEM((4, 16, 128), F32),
            pltpu.VMEM((4, 32, 128), F32),
            pltpu.VMEM((4, 32, 128), F32),
            pltpu.VMEM((4, 2048, 128), F32),
            pltpu.VMEM((4, 512, 128), F32),
            dma((10,)), dma((4,)), dma((4,)), dma((4,)),
        ],
        compiler_params=pltpu.CompilerParams(vmem_limit_bytes=60 * 1024 * 1024),
        name="write_rows",
    )(touched, accum, macc, dense, dense_noise, table, rows)


def solution(mesh):
    in_specs = (
        P("table", None, None),
        P("table", None),
        P(),
        P(),
        P("table", None, "group"),
        P(("group", "table")),
        P("table", None),
        P("table", None, None),
        P("table", "group", None),
    )
    out_specs = (P("table", None, None), P("table", None), P("table", "group", None))
    return jax.shard_map(body, mesh=mesh, in_specs=in_specs, out_specs=out_specs, check_vma=False)
```

```python
import functools

import jax
import jax.numpy as jnp
from jax import lax
from jax.experimental import pallas as pl
from jax.experimental.pallas import tpu as pltpu
from jax.sharding import PartitionSpec as P

CLIP = 1.0
LEARN = 0.05
MESH = pl.DeviceIdType.MESH
BF = jnp.bfloat16
F32 = jnp.float32


def scale_of(i):
    return 16.0**i if i < 7 else 1.0


def split_dot(a, b, dims):
    return lax.dot_general(a, b, (dims, ((), ())), preferred_element_type=F32)


def core(
    touched_h, accum_h, ids_h, w_out_h, labels_h, noise_h, table_h, w_h,
    rows_out, macc_out, dense_out,
    touched_s, touched_v, accum, ids, w_out, labels, noise, rows_v, macc_v, dense_v,
    table_v, w_v, trows, ttr, smap, low_col, counts, ring, bags, both_ids, send_ids,
    outb, slots, pacc, clip, accb, s_acc, half_send, half_recv, zsend, zrecv, rg, dsend,
    load_sem, s1, r1, s2, r2, s3, r3, s4, r4, s5, r5, s6, r6, s7, r7, out_sem,
):
    g = lax.axis_index("group")
    t = lax.axis_index("table")
    c = lax.rem(t, 2)
    p = t // 2
    y = p // 4
    x = lax.rem(p, 4)
    sib = t + 1 - 2 * c

    def ahead(off):
        return lax.rem(y + off // 4, 4) * 4 + lax.rem(x + lax.rem(off, 4), 4)

    def behind(off):
        return lax.rem(y + 4 - off // 4, 4) * 4 + lax.rem(x + 4 - lax.rem(off, 4), 4)

    loads = [
        pltpu.make_async_copy(source, target, load_sem.at[i])
        for i, (source, target) in enumerate(
            (
                (touched_h, touched_v), (touched_h.at[0], touched_s.at[pl.ds(0, 512)]),
                (ids_h, ids), (table_h, table_v),
                (w_h, w_v), (w_out_h, w_out), (labels_h, labels), (noise_h, noise),
                (accum_h, accum),
                (touched_h.at[1], touched_s.at[pl.ds(512, 512)]),
                (touched_h.at[2], touched_s.at[pl.ds(1024, 512)]),
                (touched_h.at[3], touched_s.at[pl.ds(1536, 512)]),
            )
        )
    ]
    for load in loads[:4] + loads[9:]:
        load.start()

    barrier = pltpu.get_barrier_semaphore()

    def greet(off, carry):
        pl.semaphore_signal(
            barrier, inc=1, device_id=(g, ahead(off) * 2 + c), device_id_type=MESH
        )
        return carry

    lax.fori_loop(1, 16, greet, 0)
    pl.semaphore_signal(barrier, inc=1, device_id=(g, sib), device_id_type=MESH)
    for i in range(1, 4):
        pl.semaphore_signal(
            barrier, inc=1, device_id=(lax.rem(g + i, 4), t), device_id_type=MESH
        )

    loads[0].wait()
    high_of = lax.broadcasted_iota(jnp.int32, (16, 512), 0)
    low_of = lax.broadcasted_iota(jnp.int32, (128, 512), 0)
    lane = lax.broadcasted_iota(jnp.int32, (1, 512), 1)
    for f in range(4):
        row = touched_v[f : f + 1, :]
        row_low = row & 127
        is_high = high_of == lax.shift_right_logical(row, 7)
        is_low = jnp.where(low_of == row_low, 1.0, 0.0).astype(BF)
        number = jnp.concatenate(
            [
                jnp.where(is_high, lax.shift_right_logical(lane, 4), 0),
                jnp.where(is_high, lane & 15, 0),
            ],
            axis=0,
        )
        pair = split_dot(number.astype(F32).astype(BF), is_low, ((1,), (1,)))
        place = (pair[:16] * 16.0 + pair[16:]).astype(jnp.int32)
        for j in range(6):
            word = place[3 * j : 3 * j + 1]
            for i in range(1, min(3, 16 - 3 * j)):
                word = word | lax.shift_left(place[3 * j + i : 3 * j + i + 1], 9 * i)
            smap[c * 4 + f, j : j + 1, :] = word
        smap[c * 4 + f, 6:8, :] = jnp.zeros((2, 128), jnp.int32)
        for q in range(4):
            wide = jnp.broadcast_to(row_low[:, q * 128 : (q + 1) * 128], (128, 128))
            low_col[f, q * 128 : (q + 1) * 128, :] = wide.T

    loads[2].wait()
    for f in range(4):
        for q in range(16):
            to = slice(q * 128, q * 128 + 128)
            ours = pl.ds(pl.multiple_of(q * 256 + c * 128, 128), 128)
            theirs = pl.ds(pl.multiple_of(q * 256 + 128 - c * 128, 128), 128)
            both_ids[c * 4 + f, :, to] = ids[f, :, ours]
            send_ids[f, :, to] = ids[f, :, theirs]

    own_part = pl.ds(c * 4, 4)

    def trade(i):
        source, target = (
            (send_ids, both_ids.at[own_part]),
            (smap.at[own_part], smap.at[own_part]),
            (ttr.at[own_part, pl.ds(0, 128)], ttr.at[own_part, pl.ds(0, 128)]),
        )[i]
        return pltpu.make_async_remote_copy(
            src_ref=source, dst_ref=target, send_sem=s1.at[i], recv_sem=r1.at[i],
            device_id=(g, sib), device_id_type=MESH,
        )

    def traded(i):
        other = pl.ds(4 - c * 4, 4)
        source, target = (
            (send_ids, both_ids.at[other]),
            (smap.at[other], smap.at[other]),
            (ttr.at[other, pl.ds(0, 128)], ttr.at[other, pl.ds(0, 128)]),
        )[i]
        return pltpu.make_async_remote_copy(
            src_ref=source, dst_ref=target, send_sem=s1.at[i], recv_sem=r1.at[i],
            device_id=(g, sib), device_id_type=MESH,
        )

    def pair_ahead(s):
        off = 7 - s
        return lax.rem(y + off // 2, 4) * 4 + lax.rem(x // 2 + lax.rem(off, 2), 2) * 2

    def pair_behind(s):
        off = 7 - s
        return lax.rem(y + 4 - off // 2, 4) * 4 + lax.rem(x // 2 + lax.rem(off, 2), 2) * 2

    sublane = lax.broadcasted_iota(jnp.int32, (8, 128), 0)
    scale = jnp.concatenate([jnp.full((64, 128), 1.0 / scale_of(i), F32) for i in range(8)], axis=0)

    def count(s, f):
        b0 = pl.multiple_of(pair_ahead(s) * 128, 256)
        bag = both_ids[f, :, pl.ds(b0, 256)]
        others = jnp.zeros((8, 256), F32)
        for d in range(1, 5):
            others = others + jnp.where(bag == pltpu.roll(bag, d, 0), 1.0 if d == 4 else 2.0, 0.0)
        slots_of = []
        for half in range(2):
            part = bag[:, half * 128 : half * 128 + 128]
            high = lax.shift_right_logical(part, 7)
            low = part & 127
            third = lax.shift_right_logical(high * 11, 5)
            found = jnp.zeros((8, 128), jnp.int32)
            for q in range(6):
                row = jnp.broadcast_to(smap[f, q : q + 1, :], (8, 128))
                found = jnp.where(third == q, jnp.take_along_axis(row, low, axis=1), found)
            slots_of.append(lax.shift_right_logical(found, (high - third * 3) * 9) & 511)
        halves = []
        for slot in slots_of:
            word = slot & 63
            digit = lax.shift_left(
                jnp.ones((8, 128), jnp.int32), lax.shift_right_logical(slot, 6) * 4
            )
            packed = [jnp.zeros((8, 128), jnp.int32) for _ in range(8)]
            for h in range(8):
                place = jnp.broadcast_to(word[h : h + 1], (8, 128)) - sublane
                value = jnp.broadcast_to(digit[h : h + 1], (8, 128))
                for v in range(8):
                    packed[v] = packed[v] + jnp.where(place == 8 * v, value, 0)
            packed = jnp.concatenate(packed, axis=0)
            tiles = []
            for i in range(7):
                tiles.append((packed & (15 << (4 * i))).astype(F32).astype(BF))
            tiles.append(lax.shift_right_logical(packed, 28).astype(F32).astype(BF))
            halves.append(jnp.concatenate(tiles, axis=0))
        block = jnp.concatenate(halves, axis=1)
        bags[s, pl.ds(f, 1), :] = 8.0 + jnp.sum(others, axis=0, keepdims=True)
        ring[f] = block
        counts[f, :, pl.ds(b0, 256)] = block

    for n in range(4):
        count(0, c * 4 + n)
    pl.semaphore_wait(barrier, 19)
    trade(0).start()
    trade(1).start()
    loads[1].wait()
    loads[3].wait()
    for load in loads[9:]:
        load.wait()
    for load in loads[4:9]:
        load.start()

    for f in range(4):

        def pick(n, carry):
            k = pl.multiple_of(n * 128, 128)
            for i in range(128):
                r = touched_s[f * 512 + k + i]
                trows[f, pl.ds(k + i, 1), :] = table_v[f, pl.ds(r, 1), :]
            return carry

        lax.fori_loop(0, 4, pick, 0)
    for f in range(4):
        ttr[c * 4 + f, 0:128, :] = (trows[f] * scale).T.astype(BF)
    trade(2).start()
    loads[4].wait()

    def project(f):
        side = w_v[p * 8 + f].astype(F32).T.astype(BF)
        ttr[f, 128:256, :] = split_dot(side, ttr[f, 0:128, :], ((1,), (0,))).astype(BF)

    traded(0).wait_recv()
    traded(1).wait_recv()
    for n in range(4):
        count(0, 4 - c * 4 + n)
    traded(2).wait_recv()
    for f in range(4):
        project(f)
        project(4 + f)

    rows8 = lax.broadcasted_iota(jnp.int32, (8, 256), 0)

    def out_copy(s, half):
        return pltpu.make_async_remote_copy(
            src_ref=outb.at[s * 2 + half], dst_ref=slots.at[p], send_sem=s2.at[s * 2 + half],
            recv_sem=r2.at[p], device_id=(g, (pair_ahead(s) + half) * 2 + c),
            device_id_type=MESH,
        )

    def finish(s, after):
        sumsq = jnp.zeros((1, 256), F32)
        part = jnp.zeros((128, 256), F32)
        for f in range(8):
            both = split_dot(ttr[f], ring[f], ((1,), (0,)))
            pooled = both[:128].astype(BF).astype(F32)
            sumsq = sumsq + jnp.sum(pooled * pooled, axis=0, keepdims=True)
            part = part + both[128:]
            if after is not None:
                count(after, f)
        high = sumsq.astype(BF).astype(F32)
        squares = jnp.where(rows8 == 0, high, 0.0)
        squares = jnp.where(rows8 == 1, sumsq - high, squares)
        extra = jnp.concatenate([bags[s], squares], axis=0)
        for half in range(2):
            lanes_of = slice(half * 128, half * 128 + 128)
            outb[s * 2 + half, 0:128, :] = part[:, lanes_of].astype(BF)
            outb[s * 2 + half, 128:144, :] = extra[:, lanes_of].astype(BF)

    def step(s, carry):
        finish(s, s + 1)
        out_copy(s, 0).start()
        out_copy(s, 1).start()
        return carry

    lax.fori_loop(0, 7, step, 0)
    finish(7, None)
    odd = lax.rem(x, 2)
    out_copy(7, 1 - odd).start()
    slots[p] = outb[14 + odd]
    for f in range(8):
        s_acc[f] = jnp.zeros((512, 128), F32)

    pacc[...] = slots[p, 0:128, :].astype(F32)

    def from_chip(src):
        pltpu.make_async_remote_copy(
            src_ref=outb.at[0], dst_ref=slots.at[src], send_sem=s2.at[0], recv_sem=r2.at[src],
            device_id=(g, sib), device_id_type=MESH,
        ).wait_recv()
        pacc[...] += slots[src, 0:128, :].astype(F32)

    def arrive(s, carry):
        from_chip(pair_behind(s))
        from_chip(pair_behind(s) + 1)
        return carry

    lax.fori_loop(0, 7, arrive, 0)
    from_chip(p + 1 - 2 * odd)
    loads[5].wait()
    loads[6].wait()
    pre = pacc[...]
    weight = jnp.broadcast_to(w_out[...], (128, 128)).T
    gate = jax.nn.sigmoid(pre)
    logit = jnp.sum(pre * gate * weight, axis=0, keepdims=True)
    prob = jax.nn.sigmoid(logit)
    delta = gate * (1.0 + pre * (1.0 - gate)) * weight * (prob - labels[...])
    delta_low = delta.astype(BF)

    nothing = jnp.zeros((128, 128), BF)
    twice = jnp.concatenate(
        [
            jnp.concatenate([delta_low, nothing], axis=1),
            jnp.concatenate([nothing, delta_low], axis=1),
        ],
        axis=0,
    )

    def norms(q, carry):
        acc, ssq = carry
        weights = w_v[pl.ds(q * 32, 32)]
        side = jnp.concatenate(
            [weights[:16].reshape(2048, 128), weights[16:].reshape(2048, 128)], axis=1
        )
        grad = split_dot(side, twice, ((1,), (0,)))
        square = jnp.sum((grad * grad).reshape(16, 128, 256), axis=1)
        for i in range(4):
            tail = slots[q * 4 + i, 128:144, :].astype(F32)
            half = square[:, :128] if i < 2 else square[:, 128:]
            acc = acc + half[(i % 2) * 8 : (i % 2) * 8 + 8] * tail[0:8]
            ssq = ssq + tail[8:16]
        return acc, ssq

    acc, ssq = lax.fori_loop(
        0, 4, norms, (jnp.zeros((8, 128), F32), jnp.zeros((8, 128), F32))
    )
    norm_sq = jnp.sum(acc, axis=0, keepdims=True) + jnp.sum(
        ssq, axis=0, keepdims=True
    ) * jnp.sum(delta * delta, axis=0, keepdims=True)
    factor = CLIP / jnp.maximum(jnp.sqrt(norm_sq), CLIP)
    clip[p] = (factor * delta).T.astype(BF)

    def high_one(f):
        row = lax.shift_right_logical(touched_v[pl.ds(f, 1), :], 7)
        return jnp.where(high_of == row, 1.0, 0.0).astype(BF)

    def three(values):
        first = values.astype(BF)
        rest = values - first.astype(F32)
        second = rest.astype(BF)
        return first, second, (rest - second.astype(F32)).astype(BF)

    def nth(table, n):
        packed = sum(v << (4 * i) for i, v in enumerate(table))
        packed = packed - (1 << 32) if packed >= 1 << 31 else packed
        return lax.shift_right_logical(jnp.int32(packed), 4 * n) & 15

    def offsets(n):
        return nth((0, 3, 12, 8, 15, 13, 14, 11), n), nth((1, 4, 2, 5, 7, 6, 9, 10), n)

    def clip_copy(off, src):
        return pltpu.make_async_remote_copy(
            src_ref=clip.at[src], dst_ref=clip.at[src], send_sem=s3.at[off],
            recv_sem=r3.at[src], device_id=(g, ahead(off) * 2 + c), device_id_type=MESH,
        )

    def spread(n, carry):
        for off in offsets(n):
            clip_copy(off, p).start()
        return carry

    clip_copy(1, p).start()
    lax.fori_loop(1, 8, spread, 0)

    lanes = lax.broadcasted_iota(jnp.int32, (512, 128), 1)
    loads[8].wait()
    for f in range(4):
        is_high = high_one(f)
        values = jnp.concatenate(
            [accum[f : f + 1, q * 128 : (q + 1) * 128] for q in range(16)], axis=0
        )
        first, second, third = three(values)
        spread_out = split_dot(
            jnp.concatenate([is_high, is_high, is_high], axis=0),
            jnp.concatenate([first, second, third], axis=0),
            ((0,), (0,)),
        )
        found = jnp.where(lanes == low_col[f], spread_out, 0.0)
        accb[f] = jnp.broadcast_to(jnp.sum(found, axis=1, keepdims=True), (512, 128))

    def product(f, n, first=0, rows=512):
        chips = [behind(off) for off in offsets(n)]
        side = [
            counts[f, first : first + rows, pl.ds(pl.multiple_of(q * 128, 128), 128)] for q in chips
        ]
        blocks = [clip[q] for q in chips]
        return split_dot(
            jnp.concatenate(side, axis=1), jnp.concatenate(blocks, axis=0), ((1,), (0,))
        )

    def arrived(off):
        clip_copy(off, behind(off)).wait_recv()

    def drain(s, carry):
        out_copy(s, 0).wait_send()
        out_copy(s, 1).wait_send()
        return carry

    lax.fori_loop(0, 7, drain, 0)
    out_copy(7, 1 - odd).wait_send()
    for i in range(3):
        trade(i).wait_send()

    def gather(n, carry):
        for f in range(8):
            s_acc[f] += product(f, n - 1)
        for off in offsets(n):
            arrived(off)
        return carry

    arrived(1)
    lax.fori_loop(1, 8, gather, 0)

    def turn(i):
        return (2, 1, 3, 0)[i]

    def piece(part):
        return pl.ds(part * 256, 256)

    def half_copy(part, i):
        return pltpu.make_async_remote_copy(
            src_ref=half_send.at[i, piece(part)], dst_ref=half_recv.at[i, piece(part)],
            send_sem=s4.at[part * 4 + i], recv_sem=r4.at[part * 4 + i],
            device_id=(g, sib), device_id_type=MESH,
        )

    def sum_copy(part, i, src):
        return pltpu.make_async_remote_copy(
            src_ref=zsend.at[i, piece(part)], dst_ref=zrecv.at[src, piece(part)],
            send_sem=s5.at[part * 3 + i], recv_sem=r5.at[part * 4 + src],
            device_id=(lax.rem(g + turn(i), 4), t), device_id_type=MESH,
        )

    def row_copy(part, i, src):
        return pltpu.make_async_remote_copy(
            src_ref=rg.at[src, piece(part)], dst_ref=rg.at[src, piece(part)],
            send_sem=s6.at[part * 3 + i], recv_sem=r6.at[part * 4 + src],
            device_id=(lax.rem(g + turn(i), 4), t), device_id_type=MESH,
        )

    def dense_copy(i, src):
        to = lax.rem(g + turn(i), 4)
        return pltpu.make_async_remote_copy(
            src_ref=dsend.at[to], dst_ref=dense_v.at[src], send_sem=s7.at[i],
            recv_sem=r7.at[src], device_id=(to, t), device_id_type=MESH,
        )

    def source(i):
        return lax.rem(g + 4 - turn(i), 4)

    def rows_sum(f, part):
        rows = slice(part * 256, part * 256 + 256)
        return (s_acc[f, rows] + product(f, 7, part * 256, 256)) * scale[rows]

    for part in range(2):

        for i in range(4):
            f = 4 - c * 4 + lax.rem(g + turn(i), 4)
            half_send[i, piece(part)] = rows_sum(f, part).astype(BF)
        for i in range(4):
            half_copy(part, i).start()

    for part in range(2):
        for i in range(4):
            f = c * 4 + lax.rem(g + turn(i), 4)
            s_acc[f, piece(part)] = rows_sum(f, part)
        for i in range(4):
            f = c * 4 + lax.rem(g + turn(i), 4)
            half_copy(part, i).wait_recv()
            total = s_acc[f, piece(part)] + half_recv[i, piece(part)].astype(F32)
            if i < 3:
                zsend[i, piece(part)] = total.astype(BF)
                sum_copy(part, i, g).start()
            else:
                s_acc[f, piece(part)] = total

    def drain_far(off, carry):
        clip_copy(off, p).wait_send()
        return carry

    lax.fori_loop(1, 16, drain_far, 0)
    for part in range(2):
        for i in range(4):
            half_copy(part, i).wait_send()

    side = trows[g].T.astype(BF)
    dense_sum = jnp.zeros((128, 128), F32)
    for part in range(2):
        summed = s_acc[c * 4 + g, piece(part)]
        for i in range(3):
            sum_copy(part, i, source(i)).wait_recv()
            summed = summed + zrecv[source(i), piece(part)].astype(F32)
        low = summed.astype(BF)
        rg[g, piece(part)] = split_dot(low, w_v[t * 4 + g], ((1,), (1,))).astype(BF)
        for i in range(3):
            row_copy(part, i, g).start()
        dense_sum = dense_sum + split_dot(
            side[:, part * 256 : part * 256 + 256], low, ((1,), (0,))
        )
    dsend[...] = dense_sum.reshape(4, 32, 128)
    for i in range(3):
        dense_copy(i, g).start()
    dense_v[g] = dsend[g]

    def rows_save(f, part):
        return pltpu.make_async_copy(
            rows_v.at[f, piece(part)], rows_out.at[f, piece(part)], out_sem.at[part * 4 + f]
        )

    def update(f, part):
        rows = slice(part * 256, part * 256 + 256)
        listed = rg[f, rows].astype(F32) + noise[f, rows]
        mean = jnp.sum(listed * listed, axis=1, keepdims=True) * (1.0 / 128.0)
        new_acc = accb[f, rows] + mean
        rows_v[f, rows] = trows[f, rows] - LEARN * listed / jnp.sqrt(new_acc)
        rows_save(f, part).start()
        is_high = high_one(f)[:, rows]
        added = jnp.zeros((16, 128), F32)
        for one in three(jnp.where(lanes[rows] == low_col[f, rows], mean, 0.0)):
            added = added + split_dot(is_high, one, ((1,), (0,)))
        macc_v[f] = added if part == 0 else macc_v[f] + added

    loads[7].wait()
    for part in range(2):
        update(g, part)
        for i in range(3):
            row_copy(part, i, source(i)).wait_recv()
            update(source(i), part)
    for i in range(3):
        dense_copy(i, source(i)).wait_recv()
    saves = [
        pltpu.make_async_copy(macc_v, macc_out, out_sem.at[8]),
        pltpu.make_async_copy(dense_v, dense_out, out_sem.at[9]),
    ]
    for save in saves:
        save.start()
    for part in range(2):
        for i in range(3):
            sum_copy(part, i, g).wait_send()
            row_copy(part, i, g).wait_send()
    for i in range(3):
        dense_copy(i, g).wait_send()
    for part in range(2):
        for f in range(4):
            rows_save(f, part).wait()
    for save in saves:
        save.wait()


def write_rows(
    touched_h, accum_h, macc_h, dense_h, noise_h, table_h, rows_h,
    table_out, accum_out, dense_out,
    touched_s, accum, macc, dense, noise, block, rows, sem, in_sem, rows_sem, out_sem,
):
    def load(f):
        return pltpu.make_async_copy(table_h.at[f], block.at[f], in_sem.at[f])

    def load_rows(f):
        return pltpu.make_async_copy(rows_h.at[f], rows.at[f], rows_sem.at[f])

    def save(f):
        return pltpu.make_async_copy(block.at[f], table_out.at[f], out_sem.at[f])

    load(0).start()
    load_rows(0).start()
    small = [
        pltpu.make_async_copy(source, target, sem.at[i])
        for i, (source, target) in enumerate(
            (
                (touched_h.at[0], touched_s.at[pl.ds(0, 512)]),
                (touched_h.at[1], touched_s.at[pl.ds(512, 512)]),
                (touched_h.at[2], touched_s.at[pl.ds(1024, 512)]),
                (touched_h.at[3], touched_s.at[pl.ds(1536, 512)]),
                (accum_h, accum), (macc_h, macc),
                (dense_h, dense), (noise_h, noise),
            )
        )
    ]
    for copy in small:
        copy.start()
    for f in range(1, 4):
        load(f).start()
        load_rows(f).start()
    for copy in small[:4]:
        copy.wait()
    for f in range(4):
        load(f).wait()
        load_rows(f).wait()

        def put(n, carry):
            k = pl.multiple_of(n * 128, 128)
            for i in range(128):
                block[f, pl.ds(touched_s[f * 512 + k + i], 1), :] = rows[f, pl.ds(k + i, 1), :]
            return carry

        lax.fori_loop(0, 4, put, 0)
        save(f).start()
    for copy in small[4:]:
        copy.wait()
    dense[...] += noise[...]
    save_dense = pltpu.make_async_copy(dense, dense_out, sem.at[8])
    save_dense.start()
    for f in range(4):
        for q in range(16):
            lanes = slice(q * 128, (q + 1) * 128)
            accum[f : f + 1, lanes] += macc[f, q : q + 1, :]
    save_accum = pltpu.make_async_copy(accum, accum_out, sem.at[9])
    save_accum.start()
    save_dense.wait()
    save_accum.wait()
    for f in range(4):
        save(f).wait()


def body(table, accum, w_hidden, w_out, ids, labels, touched, row_noise, dense_noise):
    hbm = pl.BlockSpec(memory_space=pl.ANY)
    dma = pltpu.SemaphoreType.DMA
    rows, macc, dense = pl.pallas_call(
        core,
        out_shape=(
            jax.ShapeDtypeStruct((4, 512, 128), F32),
            jax.ShapeDtypeStruct((4, 16, 128), F32),
            jax.ShapeDtypeStruct((4, 32, 128), F32),
        ),
        in_specs=[hbm] * 8,
        out_specs=(hbm, hbm, hbm),
        scratch_shapes=[
            pltpu.SMEM((2048,), jnp.int32),
            pltpu.VMEM((4, 512), jnp.int32),
            pltpu.VMEM((4, 2048), F32),
            pltpu.VMEM((4, 8, 4096), jnp.int32),
            pltpu.VMEM((1, 128), F32),
            pltpu.VMEM((1, 128), F32),
            pltpu.VMEM((4, 512, 128), F32),
            pltpu.VMEM((4, 512, 128), F32),
            pltpu.VMEM((4, 16, 128), F32),
            pltpu.VMEM((4, 32, 128), F32),
            pltpu.VMEM((4, 2048, 128), F32),
            pltpu.VMEM((128, 128, 128), BF),
            pltpu.VMEM((4, 512, 128), F32),
            pltpu.VMEM((8, 256, 512), BF),
            pltpu.VMEM((8, 8, 128), jnp.int32),
            pltpu.VMEM((4, 512, 128), jnp.int32),
            pltpu.VMEM((8, 512, 2048), BF),
            pltpu.VMEM((8, 512, 256), BF),
            pltpu.VMEM((8, 8, 256), F32),
            pltpu.VMEM((8, 8, 2048), jnp.int32),
            pltpu.VMEM((4, 8, 2048), jnp.int32),
            pltpu.VMEM((16, 144, 128), BF),
            pltpu.VMEM((16, 144, 128), BF),
            pltpu.VMEM((128, 128), F32),
            pltpu.VMEM((16, 128, 128), BF),
            pltpu.VMEM((4, 512, 128), F32),
            pltpu.VMEM((8, 512, 128), F32),
            pltpu.VMEM((4, 512, 128), BF),
            pltpu.VMEM((4, 512, 128), BF),
            pltpu.VMEM((3, 512, 128), BF),
            pltpu.VMEM((4, 512, 128), BF),
            pltpu.VMEM((4, 512, 128), BF),
            pltpu.VMEM((4, 32, 128), F32),
            dma((12,)),
            dma((3,)), dma((3,)), dma((16,)), dma((16,)), dma((16,)), dma((16,)),
            dma((8,)), dma((8,)),
            dma((6,)), dma((8,)), dma((6,)), dma((8,)), dma((3,)), dma((4,)),
            dma((10,)),
        ],
        compiler_params=pltpu.CompilerParams(
            collective_id=0, has_side_effects=True, vmem_limit_bytes=56 * 1024 * 1024
        ),
        cost_estimate=pl.CostEstimate(
            flops=6 * 10**9, bytes_accessed=12 * 2**20, transcendentals=10**5
        ),
        name="step",
    )(
        touched, accum, ids, w_out.reshape(1, 128), labels.reshape(1, 128),
        row_noise, table, w_hidden,
    )
    return pl.pallas_call(
        write_rows,
        out_shape=(
            jax.ShapeDtypeStruct((4, 2048, 128), F32),
            jax.ShapeDtypeStruct((4, 2048), F32),
            jax.ShapeDtypeStruct((4, 32, 128), F32),
        ),
        in_specs=[hbm] * 7,
        out_specs=(hbm, hbm, hbm),
        scratch_shapes=[
            pltpu.SMEM((2048,), jnp.int32),
            pltpu.VMEM((4, 2048), F32),
            pltpu.VMEM((4, 16, 128), F32),
            pltpu.VMEM((4, 32, 128), F32),
            pltpu.VMEM((4, 32, 128), F32),
            pltpu.VMEM((4, 2048, 128), F32),
            pltpu.VMEM((4, 512, 128), F32),
            dma((10,)), dma((4,)), dma((4,)), dma((4,)),
        ],
        compiler_params=pltpu.CompilerParams(vmem_limit_bytes=60 * 1024 * 1024),
        name="write_rows",
    )(touched, accum, macc, dense, dense_noise, table, rows)


def solution(mesh):
    in_specs = (
        P("table", None, None),
        P("table", None),
        P(),
        P(),
        P("table", None, "group"),
        P(("group", "table")),
        P("table", None),
        P("table", None, None),
        P("table", "group", None),
    )
    out_specs = (P("table", None, None), P("table", None), P("table", "group", None))
    return jax.shard_map(body, mesh=mesh, in_specs=in_specs, out_specs=out_specs, check_vma=False)
```

```python
import functools

import jax
import jax.numpy as jnp
from jax import lax
from jax.experimental import pallas as pl
from jax.experimental.pallas import tpu as pltpu
from jax.sharding import PartitionSpec as P

CLIP = 1.0
LEARN = 0.05
MESH = pl.DeviceIdType.MESH
BF = jnp.bfloat16
F32 = jnp.float32


def scale_of(i):
    return 16.0**i if i < 7 else 1.0


def split_dot(a, b, dims):
    return lax.dot_general(a, b, (dims, ((), ())), preferred_element_type=F32)


def core(
    touched_h, accum_h, ids_h, w_out_h, labels_h, noise_h, table_h, w_h,
    rows_out, macc_out, dense_out,
    touched_s, touched_v, accum, ids, w_out, labels, noise, rows_v, macc_v, dense_v,
    table_v, w_v, trows, ttr, smap, low_col, counts, ring, bags, both_ids, send_ids,
    outb, slots, pacc, clip, accb, s_acc, half_send, half_recv, zsend, zrecv, rg, dsend,
    load_sem, s1, r1, s2, r2, s3, r3, s4, r4, s5, r5, s6, r6, s7, r7, out_sem,
):
    g = lax.axis_index("group")
    t = lax.axis_index("table")
    c = lax.rem(t, 2)
    p = t // 2
    y = p // 4
    x = lax.rem(p, 4)
    sib = t + 1 - 2 * c

    def ahead(off):
        return lax.rem(y + off // 4, 4) * 4 + lax.rem(x + lax.rem(off, 4), 4)

    def behind(off):
        return lax.rem(y + 4 - off // 4, 4) * 4 + lax.rem(x + 4 - lax.rem(off, 4), 4)

    loads = [
        pltpu.make_async_copy(source, target, load_sem.at[i])
        for i, (source, target) in enumerate(
            (
                (touched_h, touched_v), (touched_h.at[0], touched_s.at[pl.ds(0, 512)]),
                (ids_h, ids), (table_h, table_v),
                (w_h, w_v), (w_out_h, w_out), (labels_h, labels), (noise_h, noise),
                (accum_h, accum),
                (touched_h.at[1], touched_s.at[pl.ds(512, 512)]),
                (touched_h.at[2], touched_s.at[pl.ds(1024, 512)]),
                (touched_h.at[3], touched_s.at[pl.ds(1536, 512)]),
            )
        )
    ]
    for load in loads[:4] + loads[9:]:
        load.start()

    barrier = pltpu.get_barrier_semaphore()

    def greet(off, carry):
        pl.semaphore_signal(
            barrier, inc=1, device_id=(g, ahead(off) * 2 + c), device_id_type=MESH
        )
        return carry

    lax.fori_loop(1, 16, greet, 0)
    pl.semaphore_signal(barrier, inc=1, device_id=(g, sib), device_id_type=MESH)
    for i in range(1, 4):
        pl.semaphore_signal(
            barrier, inc=1, device_id=(lax.rem(g + i, 4), t), device_id_type=MESH
        )

    loads[0].wait()
    high_of = lax.broadcasted_iota(jnp.int32, (16, 512), 0)
    low_of = lax.broadcasted_iota(jnp.int32, (128, 512), 0)
    lane = lax.broadcasted_iota(jnp.int32, (1, 512), 1)
    for f in range(4):
        row = touched_v[f : f + 1, :]
        row_low = row & 127
        is_high = high_of == lax.shift_right_logical(row, 7)
        is_low = jnp.where(low_of == row_low, 1.0, 0.0).astype(BF)
        number = jnp.concatenate(
            [
                jnp.where(is_high, lax.shift_right_logical(lane, 4), 0),
                jnp.where(is_high, lane & 15, 0),
            ],
            axis=0,
        )
        pair = split_dot(number.astype(F32).astype(BF), is_low, ((1,), (1,)))
        place = (pair[:16] * 16.0 + pair[16:]).astype(jnp.int32)
        for j in range(6):
            word = place[3 * j : 3 * j + 1]
            for i in range(1, min(3, 16 - 3 * j)):
                word = word | lax.shift_left(place[3 * j + i : 3 * j + i + 1], 9 * i)
            smap[c * 4 + f, j : j + 1, :] = word
        smap[c * 4 + f, 6:8, :] = jnp.zeros((2, 128), jnp.int32)
        for q in range(4):
            wide = jnp.broadcast_to(row_low[:, q * 128 : (q + 1) * 128], (128, 128))
            low_col[f, q * 128 : (q + 1) * 128, :] = wide.T

    loads[2].wait()
    for f in range(4):
        for q in range(16):
            to = slice(q * 128, q * 128 + 128)
            ours = pl.ds(pl.multiple_of(q * 256 + c * 128, 128), 128)
            theirs = pl.ds(pl.multiple_of(q * 256 + 128 - c * 128, 128), 128)
            both_ids[c * 4 + f, :, to] = ids[f, :, ours]
            send_ids[f, :, to] = ids[f, :, theirs]

    own_part = pl.ds(c * 4, 4)

    def trade(i):
        source, target = (
            (send_ids, both_ids.at[own_part]),
            (smap.at[own_part], smap.at[own_part]),
            (ttr.at[own_part, pl.ds(0, 128)], ttr.at[own_part, pl.ds(0, 128)]),
        )[i]
        return pltpu.make_async_remote_copy(
            src_ref=source, dst_ref=target, send_sem=s1.at[i], recv_sem=r1.at[i],
            device_id=(g, sib), device_id_type=MESH,
        )

    def traded(i):
        other = pl.ds(4 - c * 4, 4)
        source, target = (
            (send_ids, both_ids.at[other]),
            (smap.at[other], smap.at[other]),
            (ttr.at[other, pl.ds(0, 128)], ttr.at[other, pl.ds(0, 128)]),
        )[i]
        return pltpu.make_async_remote_copy(
            src_ref=source, dst_ref=target, send_sem=s1.at[i], recv_sem=r1.at[i],
            device_id=(g, sib), device_id_type=MESH,
        )

    def pair_ahead(s):
        off = 7 - s
        return lax.rem(y + off // 2, 4) * 4 + lax.rem(x // 2 + lax.rem(off, 2), 2) * 2

    def pair_behind(s):
        off = 7 - s
        return lax.rem(y + 4 - off // 2, 4) * 4 + lax.rem(x // 2 + lax.rem(off, 2), 2) * 2

    sublane = lax.broadcasted_iota(jnp.int32, (8, 128), 0)
    scale = jnp.concatenate([jnp.full((64, 128), 1.0 / scale_of(i), F32) for i in range(8)], axis=0)

    def count(s, f):
        b0 = pl.multiple_of(pair_ahead(s) * 128, 256)
        bag = both_ids[f, :, pl.ds(b0, 256)]
        others = jnp.zeros((8, 256), F32)
        for d in range(1, 5):
            others = others + jnp.where(bag == pltpu.roll(bag, d, 0), 1.0 if d == 4 else 2.0, 0.0)
        slots_of = []
        for half in range(2):
            part = bag[:, half * 128 : half * 128 + 128]
            high = lax.shift_right_logical(part, 7)
            low = part & 127
            third = lax.shift_right_logical(high * 11, 5)
            found = jnp.zeros((8, 128), jnp.int32)
            for q in range(6):
                row = jnp.broadcast_to(smap[f, q : q + 1, :], (8, 128))
                found = jnp.where(third == q, jnp.take_along_axis(row, low, axis=1), found)
            slots_of.append(lax.shift_right_logical(found, (high - third * 3) * 9) & 511)
        halves = []
        for slot in slots_of:
            word = slot & 63
            digit = lax.shift_left(
                jnp.ones((8, 128), jnp.int32), lax.shift_right_logical(slot, 6) * 4
            )
            packed = [jnp.zeros((8, 128), jnp.int32) for _ in range(8)]
            for h in range(8):
                place = jnp.broadcast_to(word[h : h + 1], (8, 128)) - sublane
                value = jnp.broadcast_to(digit[h : h + 1], (8, 128))
                for v in range(8):
                    packed[v] = packed[v] + jnp.where(place == 8 * v, value, 0)
            packed = jnp.concatenate(packed, axis=0)
            tiles = []
            for i in range(7):
                tiles.append((packed & (15 << (4 * i))).astype(F32).astype(BF))
            tiles.append(lax.shift_right_logical(packed, 28).astype(F32).astype(BF))
            halves.append(jnp.concatenate(tiles, axis=0))
        block = jnp.concatenate(halves, axis=1)
        bags[s, pl.ds(f, 1), :] = 8.0 + jnp.sum(others, axis=0, keepdims=True)
        ring[f] = block
        counts[f, :, pl.ds(b0, 256)] = block

    for n in range(4):
        count(0, c * 4 + n)
    pl.semaphore_wait(barrier, 19)
    trade(0).start()
    trade(1).start()
    loads[1].wait()
    loads[3].wait()
    for load in loads[9:]:
        load.wait()
    for load in loads[4:9]:
        load.start()

    for f in range(4):

        def pick(n, carry):
            k = pl.multiple_of(n * 128, 128)
            for i in range(128):
                r = touched_s[f * 512 + k + i]
                trows[f, pl.ds(k + i, 1), :] = table_v[f, pl.ds(r, 1), :]
            return carry

        lax.fori_loop(0, 4, pick, 0)
    for f in range(4):
        ttr[c * 4 + f, 0:128, :] = (trows[f] * scale).T.astype(BF)
    trade(2).start()
    loads[4].wait()

    def project(f):
        side = w_v[p * 8 + f].astype(F32).T.astype(BF)
        ttr[f, 128:256, :] = split_dot(side, ttr[f, 0:128, :], ((1,), (0,))).astype(BF)

    traded(0).wait_recv()
    traded(1).wait_recv()
    for n in range(4):
        count(0, 4 - c * 4 + n)
    traded(2).wait_recv()
    for f in range(4):
        project(f)
        project(4 + f)

    rows8 = lax.broadcasted_iota(jnp.int32, (8, 256), 0)

    def out_copy(s, half):
        return pltpu.make_async_remote_copy(
            src_ref=outb.at[s * 2 + half], dst_ref=slots.at[p], send_sem=s2.at[s * 2 + half],
            recv_sem=r2.at[p], device_id=(g, (pair_ahead(s) + half) * 2 + c),
            device_id_type=MESH,
        )

    def finish(s, after):
        sumsq = jnp.zeros((1, 256), F32)
        part = jnp.zeros((128, 256), F32)
        for f in range(8):
            both = split_dot(ttr[f], ring[f], ((1,), (0,)))
            pooled = both[:128].astype(BF).astype(F32)
            sumsq = sumsq + jnp.sum(pooled * pooled, axis=0, keepdims=True)
            part = part + both[128:]
            if after is not None:
                count(after, f)
        high = sumsq.astype(BF).astype(F32)
        squares = jnp.where(rows8 == 0, high, 0.0)
        squares = jnp.where(rows8 == 1, sumsq - high, squares)
        extra = jnp.concatenate([bags[s], squares], axis=0)
        for half in range(2):
            lanes_of = slice(half * 128, half * 128 + 128)
            outb[s * 2 + half, 0:128, :] = part[:, lanes_of].astype(BF)
            outb[s * 2 + half, 128:144, :] = extra[:, lanes_of].astype(BF)

    def step(s, carry):
        finish(s, s + 1)
        out_copy(s, 0).start()
        out_copy(s, 1).start()
        return carry

    lax.fori_loop(0, 7, step, 0)
    finish(7, None)
    odd = lax.rem(x, 2)
    out_copy(7, 1 - odd).start()
    slots[p] = outb[14 + odd]
    for f in range(8):
        s_acc[f] = jnp.zeros((512, 128), F32)

    def high_one(f):
        row = lax.shift_right_logical(touched_v[pl.ds(f, 1), :], 7)
        return jnp.where(high_of == row, 1.0, 0.0).astype(BF)

    def three(values):
        first = values.astype(BF)
        rest = values - first.astype(F32)
        second = rest.astype(BF)
        return first, second, (rest - second.astype(F32)).astype(BF)

    lanes = lax.broadcasted_iota(jnp.int32, (512, 128), 1)
    loads[8].wait()
    for f in range(4):
        is_high = high_one(f)
        values = jnp.concatenate(
            [accum[f : f + 1, q * 128 : (q + 1) * 128] for q in range(16)], axis=0
        )
        first, second, third = three(values)
        spread_out = split_dot(
            jnp.concatenate([is_high, is_high, is_high], axis=0),
            jnp.concatenate([first, second, third], axis=0),
            ((0,), (0,)),
        )
        found = jnp.where(lanes == low_col[f], spread_out, 0.0)
        accb[f] = jnp.broadcast_to(jnp.sum(found, axis=1, keepdims=True), (512, 128))

    pacc[...] = slots[p, 0:128, :].astype(F32)

    def from_chip(src):
        pltpu.make_async_remote_copy(
            src_ref=outb.at[0], dst_ref=slots.at[src], send_sem=s2.at[0], recv_sem=r2.at[src],
            device_id=(g, sib), device_id_type=MESH,
        ).wait_recv()
        pacc[...] += slots[src, 0:128, :].astype(F32)

    def arrive(s, carry):
        from_chip(pair_behind(s))
        from_chip(pair_behind(s) + 1)
        return carry

    lax.fori_loop(0, 7, arrive, 0)
    from_chip(p + 1 - 2 * odd)
    loads[5].wait()
    loads[6].wait()
    pre = pacc[...]
    weight = jnp.broadcast_to(w_out[...], (128, 128)).T
    gate = jax.nn.sigmoid(pre)
    logit = jnp.sum(pre * gate * weight, axis=0, keepdims=True)
    prob = jax.nn.sigmoid(logit)
    delta = gate * (1.0 + pre * (1.0 - gate)) * weight * (prob - labels[...])
    delta_low = delta.astype(BF)

    nothing = jnp.zeros((128, 128), BF)
    twice = jnp.concatenate(
        [
            jnp.concatenate([delta_low, nothing], axis=1),
            jnp.concatenate([nothing, delta_low], axis=1),
        ],
        axis=0,
    )

    def norms(q, carry):
        acc, ssq = carry
        weights = w_v[pl.ds(q * 32, 32)]
        side = jnp.concatenate(
            [weights[:16].reshape(2048, 128), weights[16:].reshape(2048, 128)], axis=1
        )
        grad = split_dot(side, twice, ((1,), (0,)))
        square = jnp.sum((grad * grad).reshape(16, 128, 256), axis=1)
        for i in range(4):
            tail = slots[q * 4 + i, 128:144, :].astype(F32)
            half = square[:, :128] if i < 2 else square[:, 128:]
            acc = acc + half[(i % 2) * 8 : (i % 2) * 8 + 8] * tail[0:8]
            ssq = ssq + tail[8:16]
        return acc, ssq

    acc, ssq = lax.fori_loop(
        0, 4, norms, (jnp.zeros((8, 128), F32), jnp.zeros((8, 128), F32))
    )
    norm_sq = jnp.sum(acc, axis=0, keepdims=True) + jnp.sum(
        ssq, axis=0, keepdims=True
    ) * jnp.sum(delta * delta, axis=0, keepdims=True)
    factor = CLIP / jnp.maximum(jnp.sqrt(norm_sq), CLIP)
    clip[p] = (factor * delta).T.astype(BF)

    def nth(table, n):
        packed = sum(v << (4 * i) for i, v in enumerate(table))
        packed = packed - (1 << 32) if packed >= 1 << 31 else packed
        return lax.shift_right_logical(jnp.int32(packed), 4 * n) & 15

    def offsets(n):
        return nth((0, 3, 12, 8, 15, 13, 14, 11), n), nth((1, 4, 2, 5, 7, 6, 9, 10), n)

    def clip_copy(off, src):
        return pltpu.make_async_remote_copy(
            src_ref=clip.at[src], dst_ref=clip.at[src], send_sem=s3.at[off],
            recv_sem=r3.at[src], device_id=(g, ahead(off) * 2 + c), device_id_type=MESH,
        )

    def spread(n, carry):
        for off in offsets(n):
            clip_copy(off, p).start()
        return carry

    clip_copy(1, p).start()
    lax.fori_loop(1, 8, spread, 0)

    def product(f, n, first=0, rows=512):
        chips = [behind(off) for off in offsets(n)]
        side = [
            counts[f, first : first + rows, pl.ds(pl.multiple_of(q * 128, 128), 128)] for q in chips
        ]
        blocks = [clip[q] for q in chips]
        return split_dot(
            jnp.concatenate(side, axis=1), jnp.concatenate(blocks, axis=0), ((1,), (0,))
        )

    def arrived(off):
        clip_copy(off, behind(off)).wait_recv()

    def gather(n, carry):
        for f in range(8):
            s_acc[f] += product(f, n - 1)
        for off in offsets(n):
            arrived(off)
        return carry

    arrived(1)
    lax.fori_loop(1, 8, gather, 0)

    def turn(i):
        return (2, 1, 3, 0)[i]

    def piece(part):
        return pl.ds(part * 256, 256)

    def half_copy(part, i):
        return pltpu.make_async_remote_copy(
            src_ref=half_send.at[i, piece(part)], dst_ref=half_recv.at[i, piece(part)],
            send_sem=s4.at[part * 4 + i], recv_sem=r4.at[part * 4 + i],
            device_id=(g, sib), device_id_type=MESH,
        )

    def sum_copy(part, i, src):
        return pltpu.make_async_remote_copy(
            src_ref=zsend.at[i, piece(part)], dst_ref=zrecv.at[src, piece(part)],
            send_sem=s5.at[part * 3 + i], recv_sem=r5.at[part * 4 + src],
            device_id=(lax.rem(g + turn(i), 4), t), device_id_type=MESH,
        )

    def row_copy(part, i, src):
        return pltpu.make_async_remote_copy(
            src_ref=rg.at[src, piece(part)], dst_ref=rg.at[src, piece(part)],
            send_sem=s6.at[part * 3 + i], recv_sem=r6.at[part * 4 + src],
            device_id=(lax.rem(g + turn(i), 4), t), device_id_type=MESH,
        )

    def dense_copy(i, src):
        to = lax.rem(g + turn(i), 4)
        return pltpu.make_async_remote_copy(
            src_ref=dsend.at[to], dst_ref=dense_v.at[src], send_sem=s7.at[i],
            recv_sem=r7.at[src], device_id=(to, t), device_id_type=MESH,
        )

    def source(i):
        return lax.rem(g + 4 - turn(i), 4)

    def rows_sum(f, part):
        rows = slice(part * 256, part * 256 + 256)
        return (s_acc[f, rows] + product(f, 7, part * 256, 256)) * scale[rows]

    for part in range(2):

        for i in range(4):
            f = 4 - c * 4 + lax.rem(g + turn(i), 4)
            half_send[i, piece(part)] = rows_sum(f, part).astype(BF)
        for i in range(4):
            half_copy(part, i).start()

    for part in range(2):
        for i in range(4):
            f = c * 4 + lax.rem(g + turn(i), 4)
            s_acc[f, piece(part)] = rows_sum(f, part)
        for i in range(4):
            f = c * 4 + lax.rem(g + turn(i), 4)
            half_copy(part, i).wait_recv()
            total = s_acc[f, piece(part)] + half_recv[i, piece(part)].astype(F32)
            if i < 3:
                zsend[i, piece(part)] = total.astype(BF)
                sum_copy(part, i, g).start()
            else:
                s_acc[f, piece(part)] = total

    def drain(s, carry):
        out_copy(s, 0).wait_send()
        out_copy(s, 1).wait_send()
        return carry

    lax.fori_loop(0, 7, drain, 0)
    out_copy(7, 1 - odd).wait_send()
    for i in range(3):
        trade(i).wait_send()

    def drain_far(off, carry):
        clip_copy(off, p).wait_send()
        return carry

    lax.fori_loop(1, 16, drain_far, 0)
    for part in range(2):
        for i in range(4):
            half_copy(part, i).wait_send()

    side = trows[g].T.astype(BF)
    dense_sum = jnp.zeros((128, 128), F32)
    for part in range(2):
        summed = s_acc[c * 4 + g, piece(part)]
        for i in range(3):
            sum_copy(part, i, source(i)).wait_recv()
            summed = summed + zrecv[source(i), piece(part)].astype(F32)
        low = summed.astype(BF)
        rg[g, piece(part)] = split_dot(low, w_v[t * 4 + g], ((1,), (1,))).astype(BF)
        for i in range(3):
            row_copy(part, i, g).start()
        dense_sum = dense_sum + split_dot(
            side[:, part * 256 : part * 256 + 256], low, ((1,), (0,))
        )
    dsend[...] = dense_sum.reshape(4, 32, 128)
    for i in range(3):
        dense_copy(i, g).start()
    dense_v[g] = dsend[g]

    def rows_save(f, part):
        return pltpu.make_async_copy(
            rows_v.at[f, piece(part)], rows_out.at[f, piece(part)], out_sem.at[part * 4 + f]
        )

    def update(f, part):
        rows = slice(part * 256, part * 256 + 256)
        listed = rg[f, rows].astype(F32) + noise[f, rows]
        mean = jnp.sum(listed * listed, axis=1, keepdims=True) * (1.0 / 128.0)
        new_acc = accb[f, rows] + mean
        rows_v[f, rows] = trows[f, rows] - LEARN * listed / jnp.sqrt(new_acc)
        rows_save(f, part).start()
        is_high = high_one(f)[:, rows]
        added = jnp.zeros((16, 128), F32)
        for one in three(jnp.where(lanes[rows] == low_col[f, rows], mean, 0.0)):
            added = added + split_dot(is_high, one, ((1,), (0,)))
        macc_v[f] = added if part == 0 else macc_v[f] + added

    loads[7].wait()
    for part in range(2):
        update(g, part)
        for i in range(3):
            row_copy(part, i, source(i)).wait_recv()
            update(source(i), part)
    for i in range(3):
        dense_copy(i, source(i)).wait_recv()
    saves = [
        pltpu.make_async_copy(macc_v, macc_out, out_sem.at[8]),
        pltpu.make_async_copy(dense_v, dense_out, out_sem.at[9]),
    ]
    for save in saves:
        save.start()
    for part in range(2):
        for i in range(3):
            sum_copy(part, i, g).wait_send()
            row_copy(part, i, g).wait_send()
    for i in range(3):
        dense_copy(i, g).wait_send()
    for part in range(2):
        for f in range(4):
            rows_save(f, part).wait()
    for save in saves:
        save.wait()


def write_rows(
    touched_h, accum_h, macc_h, dense_h, noise_h, table_h, rows_h,
    table_out, accum_out, dense_out,
    touched_s, accum, macc, dense, noise, block, rows, sem, in_sem, rows_sem, out_sem,
):
    def load(f):
        return pltpu.make_async_copy(table_h.at[f], block.at[f], in_sem.at[f])

    def load_rows(f):
        return pltpu.make_async_copy(rows_h.at[f], rows.at[f], rows_sem.at[f])

    def save(f):
        return pltpu.make_async_copy(block.at[f], table_out.at[f], out_sem.at[f])

    load(0).start()
    load_rows(0).start()
    small = [
        pltpu.make_async_copy(source, target, sem.at[i])
        for i, (source, target) in enumerate(
            (
                (touched_h.at[0], touched_s.at[pl.ds(0, 512)]),
                (touched_h.at[1], touched_s.at[pl.ds(512, 512)]),
                (touched_h.at[2], touched_s.at[pl.ds(1024, 512)]),
                (touched_h.at[3], touched_s.at[pl.ds(1536, 512)]),
                (accum_h, accum), (macc_h, macc),
                (dense_h, dense), (noise_h, noise),
            )
        )
    ]
    for copy in small:
        copy.start()
    for f in range(1, 4):
        load(f).start()
        load_rows(f).start()
    for copy in small[:4]:
        copy.wait()
    for f in range(4):
        load(f).wait()
        load_rows(f).wait()

        def put(n, carry):
            k = pl.multiple_of(n * 128, 128)
            for i in range(128):
                block[f, pl.ds(touched_s[f * 512 + k + i], 1), :] = rows[f, pl.ds(k + i, 1), :]
            return carry

        lax.fori_loop(0, 4, put, 0)
        save(f).start()
    for copy in small[4:]:
        copy.wait()
    dense[...] += noise[...]
    save_dense = pltpu.make_async_copy(dense, dense_out, sem.at[8])
    save_dense.start()
    for f in range(4):
        for q in range(16):
            lanes = slice(q * 128, (q + 1) * 128)
            accum[f : f + 1, lanes] += macc[f, q : q + 1, :]
    save_accum = pltpu.make_async_copy(accum, accum_out, sem.at[9])
    save_accum.start()
    save_dense.wait()
    save_accum.wait()
    for f in range(4):
        save(f).wait()


def body(table, accum, w_hidden, w_out, ids, labels, touched, row_noise, dense_noise):
    hbm = pl.BlockSpec(memory_space=pl.ANY)
    dma = pltpu.SemaphoreType.DMA
    rows, macc, dense = pl.pallas_call(
        core,
        out_shape=(
            jax.ShapeDtypeStruct((4, 512, 128), F32),
            jax.ShapeDtypeStruct((4, 16, 128), F32),
            jax.ShapeDtypeStruct((4, 32, 128), F32),
        ),
        in_specs=[hbm] * 8,
        out_specs=(hbm, hbm, hbm),
        scratch_shapes=[
            pltpu.SMEM((2048,), jnp.int32),
            pltpu.VMEM((4, 512), jnp.int32),
            pltpu.VMEM((4, 2048), F32),
            pltpu.VMEM((4, 8, 4096), jnp.int32),
            pltpu.VMEM((1, 128), F32),
            pltpu.VMEM((1, 128), F32),
            pltpu.VMEM((4, 512, 128), F32),
            pltpu.VMEM((4, 512, 128), F32),
            pltpu.VMEM((4, 16, 128), F32),
            pltpu.VMEM((4, 32, 128), F32),
            pltpu.VMEM((4, 2048, 128), F32),
            pltpu.VMEM((128, 128, 128), BF),
            pltpu.VMEM((4, 512, 128), F32),
            pltpu.VMEM((8, 256, 512), BF),
            pltpu.VMEM((8, 8, 128), jnp.int32),
            pltpu.VMEM((4, 512, 128), jnp.int32),
            pltpu.VMEM((8, 512, 2048), BF),
            pltpu.VMEM((8, 512, 256), BF),
            pltpu.VMEM((8, 8, 256), F32),
            pltpu.VMEM((8, 8, 2048), jnp.int32),
            pltpu.VMEM((4, 8, 2048), jnp.int32),
            pltpu.VMEM((16, 144, 128), BF),
            pltpu.VMEM((16, 144, 128), BF),
            pltpu.VMEM((128, 128), F32),
            pltpu.VMEM((16, 128, 128), BF),
            pltpu.VMEM((4, 512, 128), F32),
            pltpu.VMEM((8, 512, 128), F32),
            pltpu.VMEM((4, 512, 128), BF),
            pltpu.VMEM((4, 512, 128), BF),
            pltpu.VMEM((3, 512, 128), BF),
            pltpu.VMEM((4, 512, 128), BF),
            pltpu.VMEM((4, 512, 128), BF),
            pltpu.VMEM((4, 32, 128), F32),
            dma((12,)),
            dma((3,)), dma((3,)), dma((16,)), dma((16,)), dma((16,)), dma((16,)),
            dma((8,)), dma((8,)),
            dma((6,)), dma((8,)), dma((6,)), dma((8,)), dma((3,)), dma((4,)),
            dma((10,)),
        ],
        compiler_params=pltpu.CompilerParams(
            collective_id=0, has_side_effects=True, vmem_limit_bytes=56 * 1024 * 1024
        ),
        cost_estimate=pl.CostEstimate(
            flops=6 * 10**9, bytes_accessed=12 * 2**20, transcendentals=10**5
        ),
        name="step",
    )(
        touched, accum, ids, w_out.reshape(1, 128), labels.reshape(1, 128),
        row_noise, table, w_hidden,
    )
    return pl.pallas_call(
        write_rows,
        out_shape=(
            jax.ShapeDtypeStruct((4, 2048, 128), F32),
            jax.ShapeDtypeStruct((4, 2048), F32),
            jax.ShapeDtypeStruct((4, 32, 128), F32),
        ),
        in_specs=[hbm] * 7,
        out_specs=(hbm, hbm, hbm),
        scratch_shapes=[
            pltpu.SMEM((2048,), jnp.int32),
            pltpu.VMEM((4, 2048), F32),
            pltpu.VMEM((4, 16, 128), F32),
            pltpu.VMEM((4, 32, 128), F32),
            pltpu.VMEM((4, 32, 128), F32),
            pltpu.VMEM((4, 2048, 128), F32),
            pltpu.VMEM((4, 512, 128), F32),
            dma((10,)), dma((4,)), dma((4,)), dma((4,)),
        ],
        compiler_params=pltpu.CompilerParams(vmem_limit_bytes=60 * 1024 * 1024),
        name="write_rows",
    )(touched, accum, macc, dense, dense_noise, table, rows)


def solution(mesh):
    in_specs = (
        P("table", None, None),
        P("table", None),
        P(),
        P(),
        P("table", None, "group"),
        P(("group", "table")),
        P("table", None),
        P("table", None, None),
        P("table", "group", None),
    )
    out_specs = (P("table", None, None), P("table", None), P("table", "group", None))
    return jax.shard_map(body, mesh=mesh, in_specs=in_specs, out_specs=out_specs, check_vma=False)
```
